32 devices in a mesh: dp: 8 (over z, x), seq: 4 (over y, core).
Axes of the slice: x: 2, y: 2, z: 4, core: 2. Of those that a mesh axis runs over, the one named last changes fastest.
Arguments:
- tokens: bfloat16 [8, 1024, 768], P('dp', 'seq'), may hold values from -6 to 6
- prefix_len: int32 [8], P('dp'), may hold values from 102 to 512
- neighbours: bfloat16 [8, 32, 128, 768], P('dp', 'seq'), may hold values from -6 to 6
- neighbour_index: int32 [8, 16, 2], P('dp', 'seq'), may hold values from 0 to 31, as said below
- w_qkv: bfloat16 [768, 2304], P(('dp', 'seq')), may hold values from -0.21875 to 0.21875
- w_out: bfloat16 [768, 768], P(('dp', 'seq')), may hold values from -2.5 to 2.5
- w_cross_q: bfloat16 [768, 768], P(('dp', 'seq')), may hold values from -0.21875 to 0.21875
- w_cross_kv: bfloat16 [768, 1536], P(('dp', 'seq')), may hold values from -0.21875 to 0.21875
- w_cross_out: bfloat16 [768, 768], P(('dp', 'seq')), may hold values from -1.75 to 1.75
- w_up: bfloat16 [768, 3072], P(('dp', 'seq')), may hold values from -0.21875 to 0.21875
- w_down: bfloat16 [3072, 768], P(('dp', 'seq')), may hold values from -0.109375 to 0.109375
- gain_one: bfloat16 [768], P(('dp', 'seq')), may hold values from 0.5 to 1.5
- shift_one: bfloat16 [768], P(('dp', 'seq')), may hold values from -3 to 3
- gain_two: bfloat16 [768], P(('dp', 'seq')), may hold values from 0.5 to 1.5
- shift_two: bfloat16 [768], P(('dp', 'seq')), may hold values from -3 to 3
- gain_three: bfloat16 [768], P(('dp', 'seq')), may hold values from 0.5 to 1.5
- shift_three: bfloat16 [768], P(('dp', 'seq')), may hold values from -3 to 3
- cotangent: bfloat16 [8, 1024, 768], P('dp', 'seq'), may hold values from -6 to 6
Outputs:
- output: bfloat16 [8, 1024, 768], P('dp', 'seq')
- grad_tokens: float32 [8, 1024, 768], P('dp', 'seq')
- grad_neighbours: float32 [8, 32, 128, 768], P('dp', 'seq')
- grad_w_qkv: float32 [768, 2304], P(('dp', 'seq'))
- grad_w_out: float32 [768, 768], P(('dp', 'seq'))
- grad_w_cross_q: float32 [768, 768], P(('dp', 'seq'))
- grad_w_cross_kv: float32 [768, 1536], P(('dp', 'seq'))
- grad_w_cross_out: float32 [768, 768], P(('dp', 'seq'))
- grad_w_up: float32 [768, 3072], P(('dp', 'seq'))
- grad_w_down: float32 [3072, 768], P(('dp', 'seq'))
- grad_gain_one: float32 [768], P(('dp', 'seq'))
- grad_shift_one: float32 [768], P(('dp', 'seq'))
- grad_gain_two: float32 [768], P(('dp', 'seq'))
- grad_shift_two: float32 [768], P(('dp', 'seq'))
- grad_gain_three: float32 [768], P(('dp', 'seq'))
- grad_shift_three: float32 [768], P(('dp', 'seq'))
The draws below stay inside these ranges and needn't reach their ends.
Inputs may be any that keep to these rules, and one draw needn't show every extreme that they name: `neighbour_index`: for sequence s and quarter j (blocks j * 4 to (j + 1) * 4 - 1), the 8 indices name each slot from 2 * j * 4 to 2 * (j + 1) * 4 - 1 exactly once.
All inputs are finite; a program needn't handle non-finite values.
Results may differ from the reference program's by a relative error of at most 0.019.
Values may be sent and summed in bfloat16 or wider, within the bound.
A program may use at most 192 MiB of HBM per device.

```python
import jax
import jax.numpy as jnp
from jax import lax

D = 768
HEADS = 12
HEAD = 64
FF = 3072
SPAN = 64
NBR_LEN = 128
QUARTER = 256
LENGTH = 1024
SEQS = 8
SLOTS = 32
N_SEQ = 4


def draw_neighbour_index(key, part):
    block_size = 2 * (QUARTER // SPAN)
    key_list = jax.random.split(jax.random.fold_in(key, 17), SEQS * N_SEQ)
    orders = jax.vmap(lambda subkey: jax.random.permutation(subkey, block_size))(key_list)
    offsets = jnp.arange(SEQS * N_SEQ) % N_SEQ * block_size
    return (orders + offsets[:, None]).astype(jnp.int32).reshape(SEQS, LENGTH // SPAN, 2)


def with_ends(values, stream_key, least, top_value):
    place = [jax.random.randint(jax.random.fold_in(stream_key, axis), (), 0, length) for axis, length in enumerate(values.shape)]
    widest = values.shape.index(max(values.shape))
    beside = place[:widest] + [(place[widest] + 1) % values.shape[widest]] + place[widest + 1:]
    return values.at[tuple(place)].set(least).at[tuple(beside)].set(top_value)


def block_scale(key, shape, cuts, low, high):
    level = 1.0
    for position, shards_of in cuts:
        draws = jax.random.uniform(jax.random.fold_in(jax.random.fold_in(key, 6), position), (shards_of,), jnp.float32, low / len(cuts), high / len(cuts))
        level = level * jnp.repeat(jnp.exp(draws), shape[position] // shards_of).reshape((-1,) + (1,) * (len(shape) - 1 - position))
    return level


def noise(stream_key, dims, deviation, bound, pieces=(), held_as=jnp.bfloat16):
    gain = block_scale(stream_key, dims, pieces, -0.22, 0.18) if pieces else 1.0
    array = jax.random.normal(stream_key, dims, jnp.float32) * deviation * gain
    return jnp.minimum(jnp.maximum(array, -bound), bound).astype(held_as)


def setup_inputs(seed: int = 0) -> dict:
    streams_of = jax.random.split(jax.random.key(seed), 19)
    tokens = noise(streams_of[0], (SEQS, LENGTH, D), 1.0, 6.0, ((0, 8), (1, 4)))
    prefix_len = with_ends(jax.random.randint(streams_of[1], (SEQS,), LENGTH // 10, LENGTH // 2 + 1), jax.random.fold_in(streams_of[1], 1), LENGTH // 10, (LENGTH // 2 + 1) - 1).astype(jnp.int32)
    neighbours = noise(streams_of[2], (SEQS, SLOTS, NBR_LEN, D), 1.0, 6.0, ((0, 8), (1, 4)))
    neighbour_index = draw_neighbour_index(jax.random.fold_in(streams_of[18], 71), 0)
    w_qkv = noise(streams_of[4], (D, 3 * D), D ** -0.5, 0.21875, ((0, 32),))
    w_out = noise(streams_of[5], (D, D), (D // 128) ** -0.5, 2.5, ((0, 32),))
    w_cross_q = noise(streams_of[6], (D, D), D ** -0.5, 0.21875, ((0, 32),))
    w_cross_kv = noise(streams_of[7], (D, 2 * D), D ** -0.5, 0.21875, ((0, 32),))
    w_cross_out = noise(streams_of[8], (D, D), (D // 64) ** -0.5, 1.75, ((0, 32),))
    w_up = noise(streams_of[9], (D, FF), D ** -0.5, 0.21875, ((0, 32),))
    w_down = noise(streams_of[10], (FF, D), FF ** -0.5, 0.109375, ((0, 32),))
    gain_one = jnp.clip(1.0 + 0.1 * jax.random.normal(streams_of[11], (D,), jnp.float32), 0.5, 1.5).astype(jnp.bfloat16)
    shift_one = noise(streams_of[12], (D,), 0.3, 3.0, ((0, 32),))
    gain_two = jnp.clip(1.0 + 0.1 * jax.random.normal(streams_of[13], (D,), jnp.float32), 0.5, 1.5).astype(jnp.bfloat16)
    shift_two = noise(streams_of[14], (D,), 0.3, 3.0, ((0, 32),))
    gain_three = jnp.clip(1.0 + 0.1 * jax.random.normal(streams_of[15], (D,), jnp.float32), 0.5, 1.5).astype(jnp.bfloat16)
    shift_three = noise(streams_of[16], (D,), 0.3, 3.0, ((0, 32),))
    cotangent = noise(streams_of[17], (SEQS, LENGTH, D), 1.0, 6.0, ((0, 8), (1, 4)))
    return dict(tokens=tokens, prefix_len=prefix_len, neighbours=neighbours, neighbour_index=neighbour_index, w_qkv=w_qkv, w_out=w_out, w_cross_q=w_cross_q, w_cross_kv=w_cross_kv, w_cross_out=w_cross_out, w_up=w_up, w_down=w_down, gain_one=gain_one, shift_one=shift_one, gain_two=gain_two, shift_two=shift_two, gain_three=gain_three, shift_three=shift_three, cotangent=cotangent)


@jax.custom_vjp
def low(v):
    return lax.optimization_barrier(v.astype(jnp.bfloat16)).astype(jnp.float32)

@jax.custom_vjp
def low_back(v):
    return v

def low_keep(v):
    return (low(v), None)

def low_pass(kept, grad):
    return (grad,)

def back_keep(v):
    return (v, None)

def back_low(kept, grad):
    return (low(grad),)
low.defvjp(low_keep, low_pass)
low_back.defvjp(back_keep, back_low)
eps = 1e-05
masked = -1e+30

def matmul(left_side, right_side):
    return jnp.dot(left_side, right_side, precision=lax.Precision.HIGHEST, preferred_element_type=jnp.float32)

def layer_norm(array_in, gain_f, shift_f):
    avg_value = lax.optimization_barrier(jnp.mean(array_in, -1, keepdims=True))
    centred = array_in - avg_value
    return centred * lax.rsqrt(lax.optimization_barrier(jnp.mean(centred * centred, -1, keepdims=True)) + eps) * gain_f + shift_f

def rotate(array_in, cosine, sine_part):
    half_size = HEAD // 2
    first_half = array_in[..., :half_size]
    second = array_in[..., half_size:]
    cosine = cosine[:, None, :]
    sine_part = sine_part[:, None, :]
    return jnp.concatenate([first_half * cosine - second * sine_part, second * cosine + first_half * sine_part], -1)

def attend_sequence(packed):
    queries, key_rows, values, prefix = packed
    places = jnp.arange(LENGTH)
    visible = (places[None, :] <= places[:, None]) | (places[None, :] < prefix)
    scores = jnp.einsum('qhd,khd->hqk', queries, key_rows, precision=lax.Precision.HIGHEST) * HEAD ** (-0.5)
    scores = low_back(jnp.where(visible[None], scores, masked))
    weights = low(jax.nn.softmax(scores, -1))
    return jnp.einsum('hqk,khd->qhd', weights, values, precision=lax.Precision.HIGHEST)

def cross_sequence(packed):
    queries, key_rows, values = packed
    scores = low_back(jnp.einsum('cqhd,ckhd->chqk', queries, key_rows, precision=lax.Precision.HIGHEST) * HEAD ** (-0.5))
    weights = low(jax.nn.softmax(scores, -1))
    return jnp.einsum('chqk,ckhd->cqhd', weights, values, precision=lax.Precision.HIGHEST)

def forward(tokens_f, pool_f, params, prefix_len, neighbour_index):
    w_qkv, w_out, w_cross_q, w_cross_kv, w_cross_out, w_up, w_down, gain_one, shift_one, gain_two, shift_two, gain_three, shift_three = params
    normed_one = low(layer_norm(tokens_f, gain_one, shift_one))
    joined = low_back(matmul(normed_one, w_qkv))
    angles = jnp.arange(LENGTH).astype(jnp.float32)[:, None] * (10000.0 ** (-jnp.arange(HEAD // 2).astype(jnp.float32) / (HEAD // 2)))[None, :]
    cosine, sine_part = (jnp.cos(angles), jnp.sin(angles))
    query_raw = joined[..., :D].reshape(SEQS, LENGTH, HEADS, HEAD)
    key_raw = joined[..., D:2 * D].reshape(SEQS, LENGTH, HEADS, HEAD)
    value_raw = joined[..., 2 * D:].reshape(SEQS, LENGTH, HEADS, HEAD)
    query_rot = low(rotate(query_raw, cosine, sine_part))
    key_rot = low(rotate(key_raw, cosine, sine_part))
    value_self = low(value_raw)
    attended = lax.map(jax.checkpoint(attend_sequence), (query_rot, key_rot, value_self, prefix_len))
    attended = low_back(low(attended.reshape(SEQS, LENGTH, D)))
    first_sum = tokens_f + low_back(matmul(attended, w_out))
    normed_two = low(layer_norm(first_sum, gain_two, shift_two))
    cross_query = low_back(low(matmul(normed_two, w_cross_q)))
    pool_kv = low_back(low(matmul(pool_f, w_cross_kv)))
    picked = jnp.take_along_axis(pool_kv, neighbour_index.reshape(SEQS, SLOTS)[:, :, None, None], axis=1)
    picked = picked.reshape(SEQS, LENGTH // SPAN, 2 * NBR_LEN, 2 * D)
    cross_keys = picked[..., :D].reshape(SEQS, LENGTH // SPAN, 2 * NBR_LEN, HEADS, HEAD)
    cross_values = picked[..., D:].reshape(SEQS, LENGTH // SPAN, 2 * NBR_LEN, HEADS, HEAD)
    cross_queries = cross_query.reshape(SEQS, LENGTH // SPAN, SPAN, HEADS, HEAD)
    cross_mixed = lax.map(jax.checkpoint(cross_sequence), (cross_queries, cross_keys, cross_values))
    cross_mixed = low_back(low(cross_mixed.reshape(SEQS, LENGTH, D)))
    second_sum = first_sum + low_back(matmul(cross_mixed, w_cross_out))
    normed_three = low(layer_norm(second_sum, gain_three, shift_three))
    hidden_pre = low_back(matmul(normed_three, w_up))
    activated = low(jax.nn.gelu(hidden_pre, approximate=False))
    return second_sum + low_back(matmul(activated, w_down))

def reference(tokens, prefix_len, neighbours, neighbour_index, w_qkv, w_out, w_cross_q, w_cross_kv, w_cross_out, w_up, w_down, gain_one, shift_one, gain_two, shift_two, gain_three, shift_three, cotangent):
    params = tuple((item.astype(jnp.float32) for item in (w_qkv, w_out, w_cross_q, w_cross_kv, w_cross_out, w_up, w_down, gain_one, shift_one, gain_two, shift_two, gain_three, shift_three)))

    def wrapped(tokens_f, pool_f, *param_list):
        return forward(tokens_f, pool_f, param_list, prefix_len, neighbour_index)
    result, pullback = jax.vjp(wrapped, tokens.astype(jnp.float32), neighbours.astype(jnp.float32), *params)
    grads = pullback(cotangent.astype(jnp.float32))
    return (result.astype(jnp.bfloat16), grads[0], grads[1], grads[2], grads[3], grads[4], grads[5], grads[6], grads[7], grads[8], grads[9], grads[10], grads[11], grads[12], grads[13], grads[14])
```

```python
import functools
import math

import jax
import jax.numpy as jnp
import numpy as np
from jax import lax
from jax.experimental import pallas as pl
from jax.experimental.pallas import tpu as pltpu
from jax.sharding import PartitionSpec as P

HEAD = 64
eps = 1e-05
masked = -1e30
MESH = pl.DeviceIdType.MESH
bf16 = jnp.bfloat16
f32 = jnp.float32
NN = (((1,), (0,)), ((), ()))
NT = (((1,), (1,)), ((), ()))
TN = (((0,), (0,)), ((), ()))
LANES = 128


def dot(a, b, dims=NN):
    return lax.dot_general(a, b, dims, preferred_element_type=f32)


def norm_parts(v):
    centred = v - jnp.mean(v, -1, keepdims=True)
    inv = lax.rsqrt(jnp.mean(centred * centred, -1, keepdims=True) + eps)
    return centred * inv, inv


class Place:
    def __init__(self, nz):
        dp, s = lax.axis_index("dp"), lax.axis_index("seq")
        self.nz, self.dp, self.s = nz, dp, s
        self.z, self.x = lax.div(dp, 2), lax.rem(dp, 2)
        self.y, self.c = lax.div(s, 2), lax.rem(s, 2)
        x, y, z, c = self.x, self.y, self.z, self.c
        self.o = 1 - c
        self.own, self.at_x, self.at_y, self.at_d = (
            x * 2 + y,
            (1 - x) * 2 + y,
            x * 2 + 1 - y,
            (1 - x) * 2 + 1 - y,
        )
        self.to_z = [(lax.rem(z + j, nz) * 2 + x, s) for j in range(1, nz)]
        self.z_of = [lax.rem(z + j, nz) for j in range(1, nz)]
        self.z_from = [lax.rem(z - j + nz, nz) for j in range(1, nz)]
        self.to_x = (z * 2 + 1 - x, s)
        self.to_y = (dp, (1 - y) * 2 + c)
        self.to_c = (dp, y * 2 + 1 - c)
        self.s_y = (1 - y) * 2 + c
        self.s_c = y * 2 + 1 - c
        self.s_d = (1 - y) * 2 + 1 - c


def remote(src, dst, send, recv, device):
    return pltpu.make_async_remote_copy(
        src_ref=src, dst_ref=dst, send_sem=send, recv_sem=recv, device_id=device, device_id_type=MESH
    )


class Gather:
    def __init__(self, place, weights, chunks, send, recv):
        self.p, self.w, self.chunks, self.ss, self.rs = place, weights, chunks, send, recv
        self.sent = [[] for _ in chunks]

    def part(self, q, half, z, xy):
        k, start, width, _ = self.chunks[q]
        return self.w[k].at[half, z, xy, :, pl.ds(start, width)]

    def copy(self, q, j, ref, device):
        return remote(ref, ref, self.ss.at[q, j], self.rs.at[q, j], device)

    def send(self, q, j, ref, device):
        cp = self.copy(q, j, ref, device)
        cp.start()
        self.sent[q].append(cp)

    def wait(self, q, j, ref):
        self.copy(q, j, ref, self.p.to_c).wait_recv()

    def along_z(self, q):
        p = self.p
        for j, device in enumerate(p.to_z):
            self.send(q, j, self.part(q, p.c, p.z, p.own), device)

    def along_xy(self, q):
        p, allz = self.p, slice(None)
        for j, z in enumerate(p.z_from):
            self.wait(q, j, self.part(q, p.c, z, p.own))
        mine = self.part(q, p.c, allz, p.own)
        self.send(q, 3, mine, p.to_x)
        self.send(q, 4, mine, p.to_y)
        self.send(q, 7, mine, p.to_c)

    def across(self, q):
        p, allz, cut = self.p, slice(None), self.chunks[q][3]
        from_x, from_y = self.part(q, p.c, allz, p.at_x), self.part(q, p.c, allz, p.at_y)
        self.wait(q, 3, from_x)
        self.send(q, 5, self.part(q, p.c, pl.ds(0, cut), p.at_x), p.to_y)
        self.send(q, 8, from_x, p.to_c)
        self.wait(q, 4, from_y)
        self.send(q, 6, self.part(q, p.c, pl.ds(cut, p.nz - cut), p.at_y), p.to_x)
        self.send(q, 9, from_y, p.to_c)

    def last(self, q):
        p, cut = self.p, self.chunks[q][3]
        for j, z in ((5, pl.ds(0, cut)), (6, pl.ds(cut, p.nz - cut))):
            ref = self.part(q, p.c, z, p.at_d)
            self.wait(q, j, ref)
            self.send(q, j + 5, ref, p.to_c)

    def ready(self, q):
        p, allz, cut = self.p, slice(None), self.chunks[q][3]
        for j, z, xy in (
            (7, allz, p.own),
            (8, allz, p.at_x),
            (9, allz, p.at_y),
            (10, pl.ds(0, cut), p.at_d),
            (11, pl.ds(cut, p.nz - cut), p.at_d),
        ):
            self.wait(q, j, self.part(q, p.o, z, xy))

    def settle(self, q):
        for cp in self.sent[q]:
            cp.wait_send()
        self.sent[q] = []


def half_of(w, h, start=None, width=None):
    v = w[h] if start is None else w[h, :, :, :, pl.ds(start, width)]
    return v.reshape(-1, v.shape[-1])


def lane_masks():
    lane = lax.broadcasted_iota(jnp.int32, (1, LANES), 1)
    low = lane < HEAD
    return low, jnp.where(low, 1.0, 0.0).astype(bf16), jnp.where(low, 0.0, 1.0).astype(bf16)


def stacked(v, low, high):
    return jnp.concatenate([v * low, v * high], 0)


def swap_halves(v):
    lane = lax.broadcasted_iota(jnp.int32, v.shape, 1)
    first = lax.rem(lane, HEAD) < HEAD // 2
    return jnp.where(first, pltpu.roll(v, LANES - HEAD // 2, 1), pltpu.roll(v, HEAD // 2, 1))


def rotate(v, cosine, signed):
    return v * cosine + swap_halves(v) * signed


def forward(p, r, g, kv_sem):
    n = len(g.chunks)
    c, z = p.c, p.z
    w = r.w

    def step(t):
        if t < n:
            g.along_xy(t)
        if t + 3 < n:
            g.along_z(t + 3)
        if 0 <= t - 1 < n:
            g.across(t - 1)
        if 0 <= t - 2 < n:
            g.last(t - 2)

    first = remote(r.shards.at[p.o], r.beside, r.pair_sem.at[0], r.pair_sem.at[1], p.to_c)
    first.start()
    w[6][c, z, p.own] = r.w_down[...]
    first.wait_recv()
    start = 0
    for k in range(6):
        width = w[k].shape[-1]
        mine, other = r.shards[c, :, start : start + width], r.beside[:, start : start + width]
        top, low = jnp.where(c == 0, mine, other), jnp.where(c == 0, other, mine)
        w[k][c, z, p.own] = jnp.concatenate([top, low], 0).astype(bf16)
        start += width
        for q in range(3):
            if g.chunks[q][0] == k:
                g.along_z(q)
    step(0)
    tokens = r.tokens[...].astype(f32)
    unit, _ = norm_parts(tokens)
    step(1)
    step(2)
    g.ready(0)
    qkv_half = 3 * 384
    for h in range(2):
        r.vec[h] = jnp.transpose(half_of(w[0], h, qkv_half, LANES).astype(f32))[:8]

    def affine(v, i):
        return (v * r.vec[0, i : i + 1] + r.vec[1, i : i + 1]).astype(bf16)

    r.n1[...] = affine(unit, 0)
    cosine, signed = r.rope[p.s, :, :LANES], r.rope[p.s, :, LANES:]
    for i in (2, 3, 4, 5, 0, 1):
        joined = dot(r.n1[...], half_of(w[0], i // 3, (i % 3) * 384, 384))
        if i < 4:
            joined = jnp.concatenate(
                [rotate(joined[:, b : b + LANES], cosine, signed) for b in range(0, 384, LANES)], 1
            )
        part = joined.astype(bf16)
        if i < 2:
            r.q[:, i * 384 : (i + 1) * 384] = part
        else:
            r.kv[p.s, :, (i - 2) * 384 : (i - 1) * 384] = part
            if i == 5:
                kv_c = remote(r.kv.at[p.s], r.kv.at[p.s], kv_sem.at[0], kv_sem.at[1], p.to_c)
                kv_y = remote(r.kv.at[p.s], r.kv.at[p.s], kv_sem.at[2], kv_sem.at[3], p.to_y)
                kv_y.start()
                kv_c.start()
    step(3)

    g.ready(1)

    def pool_rows(i, carry):
        rows = r.neighbours[pl.ds(i * 2, 2)].reshape(-1, r.neighbours.shape[2])
        for h in range(2):
            width = w[1].shape[-1]
            r.pool[pl.ds(i * 2, 2), :, h * width : (h + 1) * width] = (
                dot(rows, half_of(w[1], h)).astype(bf16).reshape(2, -1, width)
            )
        return carry

    lax.fori_loop(0, r.neighbours.shape[0] // 2, pool_rows, 0)
    landed = r.kv.at[p.s_y]
    remote(landed, landed, kv_sem.at[2], kv_sem.at[3], p.to_y).wait_recv()
    kv_d = remote(landed, landed, kv_sem.at[4], kv_sem.at[5], p.to_c)
    kv_d.start()
    step(4)
    for ref, j in ((r.kv.at[p.s_c], 1), (r.kv.at[p.s_d], 5)):
        remote(ref, ref, kv_sem.at[j - 1], kv_sem.at[j], p.to_c).wait_recv()

    low_lane, low, high = lane_masks()
    quarter = tokens.shape[0]
    place = lax.rem(lax.broadcasted_iota(jnp.int32, (1, 2 * quarter), 1), quarter) + p.s * quarter
    limit = jnp.maximum(place, r.prefix[0] - 1)

    def self_pair(i, carry):
        cols = pl.ds(pl.multiple_of(i * LANES, LANES), LANES)
        vcols = pl.ds(pl.multiple_of(i * LANES + w[1].shape[-1], LANES), LANES)
        queries = stacked(r.q[:, cols], low, high) * bf16(HEAD**-0.5)
        keys = r.kv[:, :, cols].reshape(-1, LANES)
        values = r.kv[:, :, vcols].reshape(-1, LANES)
        scores = dot(keys, queries, NT)
        key_place = lax.broadcasted_iota(jnp.int32, scores.shape, 0)
        scores = jnp.where(key_place <= limit, scores, masked)
        top = jnp.max(scores, 0, keepdims=True)
        e = jnp.exp(scores - top)
        total = jnp.sum(e, 0, keepdims=True)
        weights = (e * (1.0 / total)).astype(bf16)
        r.lse[i] = top + jnp.log(total)
        mixed = dot(weights, values, TN)
        r.att[:, cols] = jnp.where(low_lane, mixed[:quarter], mixed[quarter:]).astype(bf16)
        return carry

    lax.fori_loop(0, 3, self_pair, 0)
    step(5)
    lax.fori_loop(3, 6, self_pair, 0)
    g.ready(2)

    def project(v, k):
        return jnp.concatenate([dot(v, half_of(w[k], h)) for h in range(2)], 1)

    first_sum = tokens + project(r.att[...], 2)
    r.first[...] = first_sum
    r.n2[...] = affine(norm_parts(first_sum)[0], 1)
    step(6)
    g.ready(3)
    r.cq[...] = project(r.n2[...], 3).astype(bf16)
    slots = r.neighbours.shape[0]
    span = quarter // (slots // 2)

    def cross_pair(i, carry):
        cols = pl.ds(pl.multiple_of(i * LANES, LANES), LANES)
        vcols = pl.ds(pl.multiple_of(i * LANES + w[1].shape[-1], LANES), LANES)
        for b in range(slots // 2):
            two = [lax.rem(r.index[2 * b + j], slots) for j in range(2)]
            rows = slice(b * span, (b + 1) * span)
            queries = stacked(r.cq[rows, cols], low, high) * bf16(HEAD**-0.5)
            keys = jnp.concatenate([r.pool[t, :, cols] for t in two], 0)
            values = jnp.concatenate([r.pool[t, :, vcols] for t in two], 0)
            scores = dot(keys, queries, NT)
            top = jnp.max(scores, 0, keepdims=True)
            e = jnp.exp(scores - top)
            total = jnp.sum(e, 0, keepdims=True)
            weights = (e * (1.0 / total)).astype(bf16)
            r.lse_cross[i, b : b + 1] = top + jnp.log(total)
            mixed = dot(weights, values, TN)
            r.cm[rows, cols] = jnp.where(low_lane, mixed[:span], mixed[span:]).astype(bf16)
        return carry

    lax.fori_loop(0, 6, cross_pair, 0)
    step(7)
    g.ready(4)
    second_sum = r.first[...] + project(r.cm[...], 4)
    r.second[...] = second_sum
    r.n3[...] = affine(norm_parts(second_sum)[0], 2)
    step(8)
    hidden_half = w[5].shape[-1]

    def up_tiles(start, width, tile):
        def body(i, carry):
            h, col = lax.div(i, width // tile), start + lax.rem(i, width // tile) * tile
            col = pl.multiple_of(col, tile)
            hidden = dot(r.n3[...], half_of(w[5], h, col, tile))
            cdf = 0.5 * (1.0 + lax.erf(hidden * (0.5**0.5)))
            density = jnp.exp(-0.5 * hidden * hidden) * ((2 * math.pi) ** -0.5)
            cols = pl.ds(pl.multiple_of(h * hidden_half + col, tile), tile)
            r.act[:, cols] = (hidden * cdf).astype(bf16)
            r.slope[:, cols] = (cdf + hidden * density).astype(bf16)
            return carry

        lax.fori_loop(0, 2 * (width // tile), body, 0)

    g.ready(5)
    up_tiles(0, 768, 256)
    step(9)
    g.ready(6)
    up_tiles(768, 768, 256)
    step(10)
    for q in (7, 8):
        g.ready(q)
        col = g.chunks[q][1]
        cols = slice(col, col + 384)
        down = sum(dot(r.act[:, h * hidden_half : (h + 1) * hidden_half], half_of(w[6], h, col, 384)) for h in range(2))
        r.out[:, cols] = (r.second[:, cols] + down).astype(bf16)
    first.wait_send()
    for cp in (kv_c, kv_y, kv_d):
        cp.wait_send()


class Refs:
    pass


NAMES_IN = ("shards", "w_down", "tokens", "prefix", "neighbours", "index", "rope")


def buffers(nz, quarter, length, width, hidden, slots, rows_n, row_block):
    heads2 = width // LANES
    halves = (3 * width // 2 + LANES, width, width // 2, width // 2, width // 2, hidden // 2)
    weights = [((2, nz, 4, row_block, h), bf16) for h in halves]
    weights.append(((2, nz, 4, hidden // (8 * nz), width), bf16))
    acts = dict(
        n1=((quarter, width), bf16),
        q=((quarter, width), bf16),
        kv=((4, quarter, 2 * width), bf16),
        att=((quarter, width), bf16),
        lse=((heads2, 1, 2 * quarter), f32),
        first=((quarter, width), f32),
        n2=((quarter, width), bf16),
        cq=((quarter, width), bf16),
        pool=((slots, rows_n, 2 * width), bf16),
        lse_cross=((heads2, 8, LANES), f32),
        cm=((quarter, width), bf16),
        second=((quarter, width), f32),
        n3=((quarter, width), bf16),
        act=((quarter, hidden), bf16),
        slope=((quarter, hidden), bf16),
        out=((quarter, width), bf16),
        vec=((2, 8, width), f32),
    )
    return weights, acts


CHUNKS = (
    (0, 0, 1280, 2),
    (1, 0, 768, 2),
    (2, 0, 384, 2),
    (3, 0, 384, 2),
    (4, 0, 384, 2),
    (5, 0, 768, 2),
    (5, 768, 768, 2),
    (6, 0, 384, 2),
    (6, 384, 384, 2),
)


def forward_kernel(nz, names, *args):
    n_in = len(NAMES_IN)
    r = Refs()
    for name, ref in zip(NAMES_IN, args[:n_in]):
        setattr(r, name, ref)
    r.w = args[n_in : n_in + 7]
    outs = args[n_in + 7 : n_in + 7 + len(names)]
    for name, ref in zip(names, outs):
        setattr(r, name, ref)
    r.beside, r.pair_sem, send, recv, kv_sem = args[n_in + 7 + len(names) :]
    p = Place(nz)
    barrier = pltpu.get_barrier_semaphore()
    friends = [*p.to_z, p.to_x, p.to_y, p.to_c]
    for device in friends:
        pl.semaphore_signal(barrier, inc=1, device_id=device, device_id_type=MESH)
    pl.semaphore_wait(barrier, len(friends))
    g = Gather(p, r.w, CHUNKS, send, recv)
    forward(p, r, g, kv_sem)
    for q in range(len(CHUNKS)):
        g.settle(q)


def rope_table(length):
    half = HEAD // 2
    freq = (10000.0 ** (-np.arange(half, dtype=np.float32) / half)).astype(np.float32)
    angles = np.arange(length, dtype=np.float32)[:, None] * freq[None, :]
    cosine, sine = np.cos(angles), np.sin(angles)
    table = np.concatenate([cosine] * 4 + [-sine, sine] * 2, 1)
    return table.astype(np.float32).reshape(4, -1, 2 * LANES)


def column_halves(v):
    return v[:, : v.shape[1] // 2], v[:, v.shape[1] // 2 :]


def shard_halves(w_qkv, w_cross_kv, w_out, w_cross_q, w_cross_out, w_up, gains, shifts, nz):
    rows = w_qkv.shape[0]
    up = jnp.swapaxes(w_up.reshape(rows, nz * 4, 2, -1), 1, 2).reshape(rows, -1)
    pads = [jnp.pad(jnp.stack(v, 1), ((0, 0), (0, LANES - 3))) for v in (gains, shifts)]
    parts = [column_halves(v) for v in (w_qkv, w_cross_kv, w_out, w_cross_q, w_cross_out, up)]
    return jnp.stack(
        [jnp.concatenate([parts[0][h], pads[h], *(v[h] for v in parts[1:])], 1) for h in range(2)]
    ).astype(f32)


def joined_halves(w):
    return jnp.concatenate([w[h].reshape(-1, w.shape[-1]) for h in range(2)], 1)


def local_fast(
    tokens,
    prefix_len,
    neighbours,
    neighbour_index,
    w_qkv,
    w_out,
    w_cross_q,
    w_cross_kv,
    w_cross_out,
    w_up,
    w_down,
    gain_one,
    shift_one,
    gain_two,
    shift_two,
    gain_three,
    shift_three,
    cotangent,
):
    nz = lax.axis_size("dp") // 2
    quarter, width = tokens.shape[1:]
    hidden = w_up.shape[1]
    slots, rows_n = neighbours.shape[1:3]
    length = quarter * 4
    shards = shard_halves(
        w_qkv, w_cross_kv, w_out, w_cross_q, w_cross_out, w_up,
        (gain_one, gain_two, gain_three), (shift_one, shift_two, shift_three), nz,
    )
    weights, acts = buffers(nz, quarter, length, width, hidden, slots, rows_n, 2 * w_qkv.shape[0])
    names = tuple(acts)
    vmem, smem = pl.BlockSpec(memory_space=pltpu.VMEM), pl.BlockSpec(memory_space=pltpu.SMEM)
    outs = pl.pallas_call(
        functools.partial(forward_kernel, nz, names),
        out_shape=[jax.ShapeDtypeStruct(*v) for v in [*weights, *acts.values()]],
        in_specs=[vmem, vmem, vmem, smem, vmem, smem, vmem],
        out_specs=[vmem] * (len(weights) + len(acts)),
        scratch_shapes=[
            pltpu.VMEM(shards.shape[1:], f32),
            pltpu.SemaphoreType.DMA((2,)),
            pltpu.SemaphoreType.DMA((len(CHUNKS), 12)),
            pltpu.SemaphoreType.DMA((len(CHUNKS), 12)),
            pltpu.SemaphoreType.DMA((6,)),
        ],
        compiler_params=pltpu.CompilerParams(
            collective_id=0, has_side_effects=True, vmem_limit_bytes=60 * 2**20
        ),
    )(
        shards, w_down, tokens[0], prefix_len, neighbours[0],
        neighbour_index.reshape(-1), jnp.asarray(rope_table(length)),
    )
    w, a = outs[:7], dict(zip(names, outs[7:]))
    full_qkv = jnp.concatenate([w[0][h].reshape(width, -1)[:, : 3 * width // 2] for h in range(2)], 1)
    full_cross_kv, full_out, full_cross_q, full_cross_out, full_up = (joined_halves(w[k]) for k in range(1, 6))
    full_down = w[6].reshape(hidden, width)
    gain_f1, gain_f2, gain_f3 = (a["vec"][0, i] for i in range(3))
    seq_here, heads = 1, width // HEAD
    seq_index = lax.axis_index("seq")
    query_pos = seq_index * quarter + jnp.arange(quarter)
    key_pos = jnp.arange(length)
    visible = (key_pos[None, None, :] <= query_pos[None, :, None]) | (
        key_pos[None, None, :] < prefix_len[:, None, None]
    )
    cosine, sine_part = rotary_tables(query_pos)
    unit_one, inv_one = plain_norm_parts(tokens.astype(f32))
    unit_two, inv_two = plain_norm_parts(a["first"][None])
    unit_three, inv_three = plain_norm_parts(a["second"][None])
    grad_act = input_grad(cotangent, full_down)
    grad_hidden = (grad_act * a["slope"]).astype(bf16)
    grad_normed_three = input_grad(grad_hidden, full_up)
    back_three, grad_gain_three, grad_shift_three = norm_back(grad_normed_three, unit_three, inv_three, gain_f3)
    grad_second = cotangent.astype(f32) + back_three
    grad_cross_branch = grad_second.astype(bf16)
    spans = slots // 2
    span_len = quarter // spans
    grad_mixed = input_grad(grad_cross_branch, full_cross_out).astype(bf16).reshape(1, spans, span_len, heads, HEAD)
    local_index = neighbour_index.reshape(1, slots) - seq_index * slots
    picked = pick_slots(a["pool"][None], local_index)
    picked = picked.reshape(1, spans, 2 * rows_n, 2 * width)
    cross_keys = picked[..., :width].reshape(1, spans, 2 * rows_n, heads, HEAD)
    cross_values = picked[..., width:].reshape(1, spans, 2 * rows_n, heads, HEAD)
    cross_queries = a["cq"].reshape(1, spans, span_len, heads, HEAD)
    cross_probs = jax.nn.softmax(
        jnp.einsum("scqhd,sckhd->schqk", cross_queries, cross_keys, preferred_element_type=f32) * HEAD ** (-0.5), -1
    )
    grad_cross_probs = jnp.einsum("scqhd,sckhd->schqk", grad_mixed, cross_values, preferred_element_type=f32)
    grad_cross_scores = (
        cross_probs * (grad_cross_probs - jnp.sum(cross_probs * grad_cross_probs, -1, keepdims=True))
    ).astype(bf16)
    grad_cross_query = (
        (jnp.einsum("schqk,sckhd->scqhd", grad_cross_scores, cross_keys, preferred_element_type=f32) * HEAD ** (-0.5))
        .astype(bf16)
        .reshape(1, quarter, width)
    )
    grad_cross_keys = jnp.einsum(
        "schqk,scqhd->sckhd", grad_cross_scores, cross_queries, preferred_element_type=f32
    ) * HEAD ** (-0.5)
    grad_cross_values = jnp.einsum(
        "schqk,scqhd->sckhd", cross_probs.astype(bf16), grad_mixed, preferred_element_type=f32
    )
    grad_picked = jnp.concatenate(
        [v.reshape(1, spans, 2 * rows_n, width) for v in (grad_cross_keys, grad_cross_values)], -1
    ).astype(bf16).reshape(slots, rows_n, 2 * width)
    grad_pool_kv = pick_slots(grad_picked[None], slot_places(local_index))
    grad_neighbours = input_grad(grad_pool_kv, full_cross_kv)
    grad_normed_two = input_grad(grad_cross_query, full_cross_q)
    back_two, grad_gain_two, grad_shift_two = norm_back(grad_normed_two, unit_two, inv_two, gain_f2)
    grad_first = grad_second + back_two
    grad_self_branch = grad_first.astype(bf16)
    grad_attended = input_grad(grad_self_branch, full_out).astype(bf16).reshape(1, quarter, heads, HEAD)
    key_heads = a["kv"].reshape(1, length, 2 * heads, HEAD)[:, :, :heads]
    value_heads = a["kv"].reshape(1, length, 2 * heads, HEAD)[:, :, heads:]
    logsum = jnp.swapaxes(a["lse"].reshape(heads // 2, 2, quarter).reshape(heads // 4, 1, 4, quarter), 0, 0)
    grad_query, grad_key_all, grad_value_all = lax.map(
        functools.partial(attend_back, visible),
        (
            grouped(a["q"].reshape(1, quarter, heads, HEAD)),
            grouped(key_heads),
            grouped(value_heads),
            grouped(grad_attended),
            logsum,
        ),
    )
    grad_query = ungrouped(grad_query)
    grad_key_all = ungrouped(grad_key_all).reshape(1, length, width)
    grad_value_all = ungrouped(grad_value_all).reshape(1, length, width)
    both = lax.psum_scatter(
        jnp.concatenate([grad_key_all, grad_value_all], -1).astype(bf16), "seq", scatter_dimension=1, tiled=True
    ).astype(f32)
    grad_joined = jnp.concatenate(
        [
            unrotate(grad_query, cosine, sine_part).reshape(1, quarter, width),
            unrotate(both[..., :width].reshape(1, quarter, heads, HEAD), cosine, sine_part).reshape(1, quarter, width),
            both[..., width:],
        ],
        -1,
    ).astype(bf16)
    grad_normed_one = input_grad(grad_joined, full_qkv)
    back_one, grad_gain_one, grad_shift_one = norm_back(grad_normed_one, unit_one, inv_one, gain_f1)
    grad_tokens = grad_first + back_one
    norm_grads = jnp.stack(
        [grad_gain_one, grad_shift_one, grad_gain_two, grad_shift_two, grad_gain_three, grad_shift_three], 1
    )
    width_owned = lax.psum_scatter(
        jnp.concatenate(
            [
                weight_grad(a["n1"], grad_joined).astype(bf16),
                weight_grad(a["att"], grad_self_branch).astype(bf16),
                weight_grad(a["n2"], grad_cross_query).astype(bf16),
                weight_grad(neighbours, grad_pool_kv).astype(bf16),
                weight_grad(a["cm"], grad_cross_branch).astype(bf16),
                weight_grad(a["n3"], grad_hidden).astype(bf16),
                norm_grads.astype(bf16),
            ],
            1,
        ),
        ("dp", "seq"),
        scatter_dimension=0,
        tiled=True,
    ).astype(f32)
    grad_down = weight_grad(a["act"], cotangent).astype(bf16)
    grad_down = jnp.swapaxes(grad_down.reshape(2, nz * 4, -1, width), 0, 1).reshape(hidden, width)
    down_owned = lax.psum_scatter(grad_down, ("dp", "seq"), scatter_dimension=0, tiled=True).astype(f32)
    column = 8 * width + hidden
    rows = width_owned.shape[0]
    grad_up = width_owned[:, 8 * width : column].reshape(rows, 2, nz * 4, -1)
    return (
        a["out"][None],
        grad_tokens,
        grad_neighbours,
        width_owned[:, : 3 * width],
        width_owned[:, 3 * width : 4 * width],
        width_owned[:, 4 * width : 5 * width],
        width_owned[:, 5 * width : 7 * width],
        width_owned[:, 7 * width : 8 * width],
        jnp.swapaxes(grad_up, 1, 2).reshape(rows, hidden),
        down_owned,
        *(width_owned[:, column + i] for i in range(6)),
    )


def pick_slots(pool, index):
    return jnp.stack(
        [
            jnp.concatenate([lax.dynamic_slice_in_dim(pool[s], index[s, j], 1, 0) for j in range(index.shape[1])], 0)
            for s in range(index.shape[0])
        ]
    )


def slot_places(index):
    slots = index.shape[1]
    same = index[:, :, None] == jnp.arange(slots)[None, None, :]
    return jnp.sum(jnp.where(same, jnp.arange(slots)[None, :, None], 0), 1)


def dense_dot(left_side, weight):
    return jnp.dot(left_side, weight, preferred_element_type=jnp.float32)


def input_grad(grad_out, weight):
    return lax.dot_general(
        grad_out,
        weight,
        (((grad_out.ndim - 1,), (1,)), ((), ())),
        preferred_element_type=jnp.float32,
    )


def weight_grad(left_side, grad_out):
    flat_left = left_side.reshape(-1, left_side.shape[-1])
    flat_grad = grad_out.reshape(-1, grad_out.shape[-1])
    return lax.dot_general(
        flat_left, flat_grad, (((0,), (0,)), ((), ())), preferred_element_type=jnp.float32
    )


def plain_norm_parts(array_in):
    avg_value = jnp.mean(array_in, -1, keepdims=True)
    centred = array_in - avg_value
    inv_std = lax.rsqrt(jnp.mean(centred * centred, -1, keepdims=True) + eps)
    return (centred * inv_std, inv_std)


def norm_back(grad_out, unit_part, inv_std, gain_f):
    scaled = grad_out * gain_f
    grad_in = inv_std * (
        scaled
        - jnp.mean(scaled, -1, keepdims=True)
        - unit_part * jnp.mean(scaled * unit_part, -1, keepdims=True)
    )
    return (grad_in, jnp.sum(grad_out * unit_part, (0, 1)), jnp.sum(grad_out, (0, 1)))


def rotary_tables(positions):
    half_size = HEAD // 2
    frequency = 10000.0 ** (-jnp.arange(half_size).astype(jnp.float32) / half_size)
    angles = positions.astype(jnp.float32)[:, None] * frequency[None, :]
    return (jnp.cos(angles)[:, None, :], jnp.sin(angles)[:, None, :])


def plain_rotate(array_in, cosine, sine_part):
    half_size = HEAD // 2
    first_half = array_in[..., :half_size]
    second = array_in[..., half_size:]
    return jnp.concatenate(
        [first_half * cosine - second * sine_part, second * cosine + first_half * sine_part], -1
    )


def unrotate(grad_in, cosine, sine_part):
    half_size = HEAD // 2
    first_half = grad_in[..., :half_size]
    second = grad_in[..., half_size:]
    return jnp.concatenate(
        [first_half * cosine + second * sine_part, second * cosine - first_half * sine_part], -1
    )


def grouped(array_in):
    split_heads = array_in.reshape(
        array_in.shape[0], array_in.shape[1], array_in.shape[2] // 4, 4, array_in.shape[3]
    )
    return jnp.moveaxis(split_heads, 2, 0)


def ungrouped(array_in):
    shifted_axes = jnp.moveaxis(array_in, 0, 2)
    return shifted_axes.reshape(
        shifted_axes.shape[0], shifted_axes.shape[1], -1, shifted_axes.shape[-1]
    )


def masked_scores(visible, queries, key_rows):
    scores = jnp.einsum(
        "sqhd,skhd->shqk", queries, key_rows, preferred_element_type=jnp.float32
    ) * HEAD ** (-0.5)
    return jnp.where(visible[:, None], scores, masked)


def attend_group(visible, packed):
    queries, key_rows, values = packed
    scores = masked_scores(visible, queries, key_rows)
    row_max = jnp.max(scores, -1, keepdims=True)
    exp_scores = jnp.exp(scores - row_max)
    row_total = jnp.sum(exp_scores, -1, keepdims=True)
    probabilities = (exp_scores / row_total).astype(jnp.bfloat16)
    mixed_out = jnp.einsum(
        "shqk,skhd->sqhd", probabilities, values, preferred_element_type=jnp.float32
    )
    return (mixed_out, (row_max + jnp.log(row_total))[..., 0])


def attend_back(visible, packed):
    queries, key_rows, values, grad_out, logsum = packed
    scores = masked_scores(visible, queries, key_rows)
    probabilities = jnp.exp(scores - logsum[..., None])
    grad_probs = jnp.einsum("sqhd,skhd->shqk", grad_out, values, preferred_element_type=jnp.float32)
    grad_scores = (
        probabilities * (grad_probs - jnp.sum(probabilities * grad_probs, -1, keepdims=True))
    ).astype(jnp.bfloat16)
    grad_query = jnp.einsum(
        "shqk,skhd->sqhd", grad_scores, key_rows, preferred_element_type=jnp.float32
    ) * HEAD ** (-0.5)
    grad_key = jnp.einsum(
        "shqk,sqhd->skhd", grad_scores, queries, preferred_element_type=jnp.float32
    ) * HEAD ** (-0.5)
    grad_value = jnp.einsum(
        "shqk,sqhd->skhd",
        probabilities.astype(jnp.bfloat16),
        grad_out,
        preferred_element_type=jnp.float32,
    )
    return (grad_query, grad_key, grad_value)


def local_plain(
    tokens,
    prefix_len,
    neighbours,
    neighbour_index,
    w_qkv,
    w_out,
    w_cross_q,
    w_cross_kv,
    w_cross_out,
    w_up,
    w_down,
    gain_one,
    shift_one,
    gain_two,
    shift_two,
    gain_three,
    shift_three,
    cotangent,
):
    forward_set = (
        lax.all_gather(w_qkv, ("dp", "seq"), axis=0, tiled=True),
        lax.all_gather(w_out, ("dp", "seq"), axis=0, tiled=True),
        lax.all_gather(w_cross_q, ("dp", "seq"), axis=0, tiled=True),
        lax.all_gather(w_cross_kv, ("dp", "seq"), axis=0, tiled=True),
        lax.all_gather(w_cross_out, ("dp", "seq"), axis=0, tiled=True),
        lax.all_gather(w_up, ("dp", "seq"), axis=0, tiled=True),
        lax.all_gather(w_down, ("dp", "seq"), axis=0, tiled=True),
        lax.all_gather(gain_one, ("dp", "seq"), axis=0, tiled=True),
        lax.all_gather(shift_one, ("dp", "seq"), axis=0, tiled=True),
        lax.all_gather(gain_two, ("dp", "seq"), axis=0, tiled=True),
        lax.all_gather(shift_two, ("dp", "seq"), axis=0, tiled=True),
        lax.all_gather(gain_three, ("dp", "seq"), axis=0, tiled=True),
        lax.all_gather(shift_three, ("dp", "seq"), axis=0, tiled=True),
    )
    (
        full_qkv,
        full_out,
        full_cross_q,
        full_cross_kv,
        full_cross_out,
        full_up,
        full_down,
        full_gain_one,
        full_shift_one,
        full_gain_two,
        full_shift_two,
        full_gain_three,
        full_shift_three,
    ) = forward_set
    seq_here, quarter, width = tokens.shape
    heads = width // HEAD
    hidden_width = full_up.shape[1]
    length = quarter * lax.axis_size("seq")
    seq_index = lax.axis_index("seq")
    query_pos = seq_index * quarter + jnp.arange(quarter)
    key_pos = jnp.arange(length)
    visible = (key_pos[None, None, :] <= query_pos[None, :, None]) | (
        key_pos[None, None, :] < prefix_len[:, None, None]
    )
    cosine, sine_part = rotary_tables(query_pos)
    gain_f1 = full_gain_one.astype(jnp.float32)
    gain_f2 = full_gain_two.astype(jnp.float32)
    gain_f3 = full_gain_three.astype(jnp.float32)
    resid_in = tokens.astype(jnp.float32)
    unit_one, inv_one = plain_norm_parts(resid_in)
    normed_one = (unit_one * gain_f1 + full_shift_one.astype(jnp.float32)).astype(jnp.bfloat16)
    joined = dense_dot(normed_one, full_qkv)
    query_rot = plain_rotate(
        joined[..., :width].reshape(seq_here, quarter, heads, HEAD), cosine, sine_part
    ).astype(jnp.bfloat16)
    key_local = (
        plain_rotate(
            joined[..., width : 2 * width].reshape(seq_here, quarter, heads, HEAD),
            cosine,
            sine_part,
        )
        .astype(jnp.bfloat16)
        .reshape(seq_here, quarter, width)
    )
    value_local = joined[..., 2 * width :].astype(jnp.bfloat16)
    key_all, value_all = (
        lax.all_gather(key_local, "seq", axis=1, tiled=True),
        lax.all_gather(value_local, "seq", axis=1, tiled=True),
    )
    key_heads = key_all.reshape(seq_here, length, heads, HEAD)
    value_heads = value_all.reshape(seq_here, length, heads, HEAD)
    attended, logsum = lax.map(
        functools.partial(attend_group, visible),
        (grouped(query_rot), grouped(key_heads), grouped(value_heads)),
    )
    attended = ungrouped(attended).reshape(seq_here, quarter, width).astype(jnp.bfloat16)
    first_sum = resid_in + dense_dot(attended, full_out)
    unit_two, inv_two = plain_norm_parts(first_sum)
    normed_two = (unit_two * gain_f2 + full_shift_two.astype(jnp.float32)).astype(jnp.bfloat16)
    cross_query = dense_dot(normed_two, full_cross_q).astype(jnp.bfloat16)
    pool_kv = dense_dot(neighbours, full_cross_kv).astype(jnp.bfloat16)
    slots = neighbours.shape[1]
    spans = slots // 2
    span_len = quarter // spans
    neighbour_rows = 2 * neighbours.shape[2]
    local_index = neighbour_index.reshape(seq_here, slots) - seq_index * slots
    picked = pick_slots(pool_kv, local_index)
    picked = picked.reshape(seq_here, spans, neighbour_rows, 2 * width)
    cross_keys = picked[..., :width].reshape(seq_here, spans, neighbour_rows, heads, HEAD)
    cross_values = picked[..., width:].reshape(seq_here, spans, neighbour_rows, heads, HEAD)
    cross_queries = cross_query.reshape(seq_here, spans, span_len, heads, HEAD)
    cross_scores = jnp.einsum(
        "scqhd,sckhd->schqk", cross_queries, cross_keys, preferred_element_type=jnp.float32
    ) * HEAD ** (-0.5)
    cross_probs = jax.nn.softmax(cross_scores, -1)
    cross_weights = cross_probs.astype(jnp.bfloat16)
    cross_mixed = jnp.einsum(
        "schqk,sckhd->scqhd", cross_weights, cross_values, preferred_element_type=jnp.float32
    )
    cross_mixed = cross_mixed.reshape(seq_here, quarter, width).astype(jnp.bfloat16)
    second_sum = first_sum + dense_dot(cross_mixed, full_cross_out)
    unit_three, inv_three = plain_norm_parts(second_sum)
    normed_three = (unit_three * gain_f3 + full_shift_three.astype(jnp.float32)).astype(
        jnp.bfloat16
    )
    hidden_pre = dense_dot(normed_three, full_up)
    activated = jax.nn.gelu(hidden_pre, approximate=False).astype(jnp.bfloat16)
    output = (second_sum + dense_dot(activated, full_down)).astype(jnp.bfloat16)
    grad_act = input_grad(cotangent, full_down)
    _, gelu_back = jax.vjp(functools.partial(jax.nn.gelu, approximate=False), hidden_pre)
    grad_hidden = gelu_back(grad_act)[0].astype(jnp.bfloat16)
    grad_normed_three = input_grad(grad_hidden, full_up)
    back_three, grad_gain_three, grad_shift_three = norm_back(
        grad_normed_three, unit_three, inv_three, full_gain_three.astype(jnp.float32)
    )
    grad_second = cotangent.astype(jnp.float32) + back_three
    grad_cross_branch = grad_second.astype(jnp.bfloat16)
    grad_mixed = (
        input_grad(grad_cross_branch, full_cross_out)
        .astype(jnp.bfloat16)
        .reshape(seq_here, spans, span_len, heads, HEAD)
    )
    grad_cross_probs = jnp.einsum(
        "scqhd,sckhd->schqk", grad_mixed, cross_values, preferred_element_type=jnp.float32
    )
    grad_cross_scores = (
        cross_probs
        * (grad_cross_probs - jnp.sum(cross_probs * grad_cross_probs, -1, keepdims=True))
    ).astype(jnp.bfloat16)
    grad_cross_query = (
        (
            jnp.einsum(
                "schqk,sckhd->scqhd",
                grad_cross_scores,
                cross_keys,
                preferred_element_type=jnp.float32,
            )
            * HEAD ** (-0.5)
        )
        .astype(jnp.bfloat16)
        .reshape(seq_here, quarter, width)
    )
    grad_cross_keys = jnp.einsum(
        "schqk,scqhd->sckhd", grad_cross_scores, cross_queries, preferred_element_type=jnp.float32
    ) * HEAD ** (-0.5)
    grad_cross_values = jnp.einsum(
        "schqk,scqhd->sckhd", cross_weights, grad_mixed, preferred_element_type=jnp.float32
    )
    grad_picked = jnp.concatenate(
        [
            grad_cross_keys.reshape(seq_here, spans, neighbour_rows, width),
            grad_cross_values.reshape(seq_here, spans, neighbour_rows, width),
        ],
        -1,
    )
    grad_picked = grad_picked.reshape(seq_here, slots, neighbours.shape[2], 2 * width)
    grad_pool_kv = pick_slots(grad_picked.astype(jnp.bfloat16), slot_places(local_index))
    grad_neighbours = input_grad(grad_pool_kv, full_cross_kv)
    grad_normed_two = input_grad(grad_cross_query, full_cross_q)
    back_two, grad_gain_two, grad_shift_two = norm_back(
        grad_normed_two, unit_two, inv_two, full_gain_two.astype(jnp.float32)
    )
    grad_first = grad_second + back_two
    grad_self_branch = grad_first.astype(jnp.bfloat16)
    grad_attended = (
        input_grad(grad_self_branch, full_out)
        .astype(jnp.bfloat16)
        .reshape(seq_here, quarter, heads, HEAD)
    )
    grad_query, grad_key_all, grad_value_all = lax.map(
        functools.partial(attend_back, visible),
        (
            grouped(query_rot),
            grouped(key_heads),
            grouped(value_heads),
            grouped(grad_attended),
            logsum,
        ),
    )
    grad_query = ungrouped(grad_query)
    grad_key_all = ungrouped(grad_key_all).reshape(seq_here, length, width)
    grad_value_all = ungrouped(grad_value_all).reshape(seq_here, length, width)
    grad_key, grad_value = (
        lax.psum_scatter(
            grad_key_all.astype(jnp.bfloat16), "seq", scatter_dimension=1, tiled=True
        ).astype(jnp.float32),
        lax.psum_scatter(
            grad_value_all.astype(jnp.bfloat16), "seq", scatter_dimension=1, tiled=True
        ).astype(jnp.float32),
    )
    grad_joined = jnp.concatenate(
        [
            unrotate(grad_query, cosine, sine_part).reshape(seq_here, quarter, width),
            unrotate(grad_key.reshape(seq_here, quarter, heads, HEAD), cosine, sine_part).reshape(
                seq_here, quarter, width
            ),
            grad_value,
        ],
        -1,
    ).astype(jnp.bfloat16)
    grad_normed_one = input_grad(grad_joined, full_qkv)
    back_one, grad_gain_one, grad_shift_one = norm_back(
        grad_normed_one, unit_one, inv_one, full_gain_one.astype(jnp.float32)
    )
    grad_tokens = grad_first + back_one
    norm_grads = jnp.stack(
        [
            grad_gain_one,
            grad_shift_one,
            grad_gain_two,
            grad_shift_two,
            grad_gain_three,
            grad_shift_three,
        ],
        1,
    )
    width_owned = lax.psum_scatter(
        jnp.concatenate(
            [
                weight_grad(normed_one, grad_joined),
                weight_grad(attended, grad_self_branch),
                weight_grad(normed_two, grad_cross_query),
                weight_grad(neighbours, grad_pool_kv),
                weight_grad(cross_mixed, grad_cross_branch),
                weight_grad(normed_three, grad_hidden),
                norm_grads,
            ],
            1,
        ),
        ("dp", "seq"),
        scatter_dimension=0,
        tiled=True,
    )
    down_owned = lax.psum_scatter(
        weight_grad(activated, cotangent), ("dp", "seq"), scatter_dimension=0, tiled=True
    )
    column = 8 * width + hidden_width
    return (
        output,
        grad_tokens,
        grad_neighbours,
        width_owned[:, : 3 * width],
        width_owned[:, 3 * width : 4 * width],
        width_owned[:, 4 * width : 5 * width],
        width_owned[:, 5 * width : 7 * width],
        width_owned[:, 7 * width : 8 * width],
        width_owned[:, 8 * width : column],
        down_owned,
        width_owned[:, column],
        width_owned[:, column + 1],
        width_owned[:, column + 2],
        width_owned[:, column + 3],
        width_owned[:, column + 4],
        width_owned[:, column + 5],
    )


def solution(mesh):
    sizes = dict(mesh.shape)
    fits = sizes == {"dp": 8, "seq": 4}
    return jax.shard_map(
        local_fast if fits else local_plain,
        mesh=mesh,
        in_specs=(
            P("dp", "seq", None),
            P("dp"),
            P("dp", "seq", None, None),
            P("dp", "seq", None),
            P(("dp", "seq"), None),
            P(("dp", "seq"), None),
            P(("dp", "seq"), None),
            P(("dp", "seq"), None),
            P(("dp", "seq"), None),
            P(("dp", "seq"), None),
            P(("dp", "seq"), None),
            P(("dp", "seq")),
            P(("dp", "seq")),
            P(("dp", "seq")),
            P(("dp", "seq")),
            P(("dp", "seq")),
            P(("dp", "seq")),
            P("dp", "seq", None),
        ),
        out_specs=(
            P("dp", "seq", None),
            P("dp", "seq", None),
            P("dp", "seq", None, None),
            P(("dp", "seq"), None),
            P(("dp", "seq"), None),
            P(("dp", "seq"), None),
            P(("dp", "seq"), None),
            P(("dp", "seq"), None),
            P(("dp", "seq"), None),
            P(("dp", "seq"), None),
            P(("dp", "seq")),
            P(("dp", "seq")),
            P(("dp", "seq")),
            P(("dp", "seq")),
            P(("dp", "seq")),
            P(("dp", "seq")),
        ),
        check_vma=False,
    )
```

```python
import functools
import math

import jax
import jax.numpy as jnp
import numpy as np
from jax import lax
from jax.experimental import pallas as pl
from jax.experimental.pallas import tpu as pltpu
from jax.sharding import PartitionSpec as P

HEAD = 64
eps = 1e-05
masked = -1e30
MESH = pl.DeviceIdType.MESH
bf16 = jnp.bfloat16
f32 = jnp.float32
NN = (((1,), (0,)), ((), ()))
NT = (((1,), (1,)), ((), ()))
TN = (((0,), (0,)), ((), ()))
LANES = 128


def dot(a, b, dims=NN):
    return lax.dot_general(a, b, dims, preferred_element_type=f32)


def norm_parts(v):
    centred = v - jnp.mean(v, -1, keepdims=True)
    inv = lax.rsqrt(jnp.mean(centred * centred, -1, keepdims=True) + eps)
    return centred * inv, inv


class Place:
    def __init__(self, nz):
        dp, s = lax.axis_index("dp"), lax.axis_index("seq")
        self.nz, self.dp, self.s = nz, dp, s
        self.z, self.x = lax.div(dp, 2), lax.rem(dp, 2)
        self.y, self.c = lax.div(s, 2), lax.rem(s, 2)
        x, y, z, c = self.x, self.y, self.z, self.c
        self.o = 1 - c
        self.own, self.at_x, self.at_y, self.at_d = (
            x * 2 + y,
            (1 - x) * 2 + y,
            x * 2 + 1 - y,
            (1 - x) * 2 + 1 - y,
        )
        self.to_z = [(lax.rem(z + j, nz) * 2 + x, s) for j in range(1, nz)]
        self.z_of = [lax.rem(z + j, nz) for j in range(1, nz)]
        self.z_from = [lax.rem(z - j + nz, nz) for j in range(1, nz)]
        self.to_x = (z * 2 + 1 - x, s)
        self.to_y = (dp, (1 - y) * 2 + c)
        self.to_c = (dp, y * 2 + 1 - c)
        self.s_y = (1 - y) * 2 + c
        self.s_c = y * 2 + 1 - c
        self.s_d = (1 - y) * 2 + 1 - c


def remote(src, dst, send, recv, device):
    return pltpu.make_async_remote_copy(
        src_ref=src, dst_ref=dst, send_sem=send, recv_sem=recv, device_id=device, device_id_type=MESH
    )


class Gather:
    def __init__(self, place, weights, chunks, send, recv):
        self.p, self.w, self.chunks, self.ss, self.rs = place, weights, chunks, send, recv
        self.sent = [[] for _ in chunks]

    def part(self, q, half, z, xy):
        k, start, width, _ = self.chunks[q]
        return self.w[k].at[half, z, xy, :, pl.ds(start, width)]

    def copy(self, q, j, ref, device):
        return remote(ref, ref, self.ss.at[q, j], self.rs.at[q, j], device)

    def send(self, q, j, ref, device):
        cp = self.copy(q, j, ref, device)
        cp.start()
        self.sent[q].append(cp)

    def wait(self, q, j, ref):
        self.copy(q, j, ref, self.p.to_c).wait_recv()

    def along_z(self, q):
        p = self.p
        for j, device in enumerate(p.to_z):
            self.send(q, j, self.part(q, p.c, p.z, p.own), device)

    def along_xy(self, q):
        p, allz = self.p, slice(None)
        for j, z in enumerate(p.z_from):
            self.wait(q, j, self.part(q, p.c, z, p.own))
        mine = self.part(q, p.c, allz, p.own)
        self.send(q, 3, mine, p.to_x)
        self.send(q, 4, mine, p.to_y)
        self.send(q, 7, mine, p.to_c)

    def across(self, q):
        p, allz, cut = self.p, slice(None), self.chunks[q][3]
        from_x, from_y = self.part(q, p.c, allz, p.at_x), self.part(q, p.c, allz, p.at_y)
        self.wait(q, 3, from_x)
        self.send(q, 5, self.part(q, p.c, pl.ds(0, cut), p.at_x), p.to_y)
        self.send(q, 8, from_x, p.to_c)
        self.wait(q, 4, from_y)
        self.send(q, 6, self.part(q, p.c, pl.ds(cut, p.nz - cut), p.at_y), p.to_x)
        self.send(q, 9, from_y, p.to_c)

    def last(self, q):
        p, cut = self.p, self.chunks[q][3]
        for j, z in ((5, pl.ds(0, cut)), (6, pl.ds(cut, p.nz - cut))):
            ref = self.part(q, p.c, z, p.at_d)
            self.wait(q, j, ref)
            self.send(q, j + 5, ref, p.to_c)

    def ready(self, q):
        p, allz, cut = self.p, slice(None), self.chunks[q][3]
        for j, z, xy in (
            (7, allz, p.own),
            (8, allz, p.at_x),
            (9, allz, p.at_y),
            (10, pl.ds(0, cut), p.at_d),
            (11, pl.ds(cut, p.nz - cut), p.at_d),
        ):
            self.wait(q, j, self.part(q, p.o, z, xy))

    def settle(self, q):
        for cp in self.sent[q]:
            cp.wait_send()
        self.sent[q] = []


def half_of(w, h, start=None, width=None):
    v = w[h] if start is None else w[h, :, :, :, pl.ds(start, width)]
    return v.reshape(-1, v.shape[-1])


def lane_masks():
    lane = lax.broadcasted_iota(jnp.int32, (1, LANES), 1)
    low = lane < HEAD
    return low, jnp.where(low, 1.0, 0.0).astype(bf16), jnp.where(low, 0.0, 1.0).astype(bf16)


def stacked(v, low, high):
    return jnp.concatenate([v * low, v * high], 0)


def swap_halves(v):
    lane = lax.broadcasted_iota(jnp.int32, v.shape, 1)
    first = lax.rem(lane, HEAD) < HEAD // 2
    return jnp.where(first, pltpu.roll(v, LANES - HEAD // 2, 1), pltpu.roll(v, HEAD // 2, 1))


def rotate(v, cosine, signed):
    return v * cosine + swap_halves(v) * signed


def forward(p, r, g, swap, kv_sem, pairs):
    n = len(g.chunks)
    c, z = p.c, p.z
    w = r.w

    def step(t):
        if t < n:
            g.along_xy(t)
        if t + 3 < n:
            g.along_z(t + 3)
        if 0 <= t - 1 < n:
            g.across(t - 1)
        if 0 <= t - 2 < n:
            g.last(t - 2)

    first = remote(r.shards.at[p.o], r.beside, r.pair_sem.at[0], r.pair_sem.at[1], p.to_c)
    first.start()
    rope = pltpu.make_async_copy(r.rope_table.at[p.s], r.rope, r.rope_sem)
    rope.start()
    w[6][c, z, p.own] = r.w_down[...]
    first.wait_recv()
    start = 0
    for k in range(6):
        width = w[k].shape[-1]
        mine, other = r.shards[c, :, start : start + width], r.beside[:, start : start + width]
        top, low = jnp.where(c == 0, mine, other), jnp.where(c == 0, other, mine)
        w[k][c, z, p.own] = jnp.concatenate([top, low], 0).astype(bf16)
        start += width
        for q in range(3):
            if g.chunks[q][0] == k:
                g.along_z(q)
    step(0)
    swap.send("cot", r.cotangent, r.by_cot)
    swap.send("nb", r.neighbours, r.by_neighbours)
    rope.wait()
    tokens = r.tokens[...].astype(f32)
    unit, _ = norm_parts(tokens)
    step(1)
    step(2)
    g.ready(0)
    qkv_half = 3 * 384
    for h in range(2):
        r.vec[h] = jnp.transpose(half_of(w[0], h, qkv_half, LANES).astype(f32))[:8]

    def affine(v, i):
        return (v * r.vec[0, i : i + 1] + r.vec[1, i : i + 1]).astype(bf16)

    r.n1[...] = affine(unit, 0)
    swap.send("n1", r.n1, r.by_n1)
    cosine, signed = r.rope[:, :LANES], r.rope[:, LANES:]
    for i in (2, 3, 4, 5, 0, 1):
        joined = dot(r.n1[...], half_of(w[0], i // 3, (i % 3) * 384, 384))
        if i < 4:
            joined = jnp.concatenate(
                [rotate(joined[:, b : b + LANES], cosine, signed) for b in range(0, 384, LANES)], 1
            )
        part = joined.astype(bf16)
        if i < 2:
            r.q[:, i * 384 : (i + 1) * 384] = part
        else:
            r.kv[p.s, :, (i - 2) * 384 : (i - 1) * 384] = part
            if i == 5:
                kv_c = remote(r.kv.at[p.s], r.kv.at[p.s], kv_sem.at[0], kv_sem.at[1], p.to_c)
                kv_y = remote(r.kv.at[p.s], r.kv.at[p.s], kv_sem.at[2], kv_sem.at[3], p.to_y)
                kv_y.start()
                kv_c.start()
    step(3)

    g.ready(1)

    def pool_rows(i, carry):
        rows = r.neighbours[pl.ds(i * 2, 2)].reshape(-1, r.neighbours.shape[2])
        for h in range(2):
            width = w[1].shape[-1]
            r.pool[pl.ds(i * 2, 2), :, h * width : (h + 1) * width] = (
                dot(rows, half_of(w[1], h)).astype(bf16).reshape(2, -1, width)
            )
        return carry

    lax.fori_loop(0, r.neighbours.shape[0] // 2, pool_rows, 0)
    landed = r.kv.at[p.s_y]
    remote(landed, landed, kv_sem.at[2], kv_sem.at[3], p.to_y).wait_recv()
    kv_d = remote(landed, landed, kv_sem.at[4], kv_sem.at[5], p.to_c)
    kv_d.start()
    step(4)
    for ref, j in ((r.kv.at[p.s_c], 1), (r.kv.at[p.s_d], 5)):
        remote(ref, ref, kv_sem.at[j - 1], kv_sem.at[j], p.to_c).wait_recv()

    low_lane, low, high = lane_masks()
    quarter = tokens.shape[0]
    place = lax.rem(lax.broadcasted_iota(jnp.int32, (1, 2 * quarter), 1), quarter) + p.s * quarter
    limit = jnp.maximum(place, r.prefix[0] - 1)

    def self_pair(i, carry):
        cols = pl.ds(pl.multiple_of(i * LANES, LANES), LANES)
        vcols = pl.ds(pl.multiple_of(i * LANES + w[1].shape[-1], LANES), LANES)
        queries = stacked(r.q[:, cols], low, high) * bf16(HEAD**-0.5)
        keys = r.kv[:, :, cols].reshape(-1, LANES)
        values = r.kv[:, :, vcols].reshape(-1, LANES)
        scores = dot(keys, queries, NT)
        key_place = lax.broadcasted_iota(jnp.int32, scores.shape, 0)
        scores = jnp.where(key_place <= limit, scores, masked)
        top = jnp.max(scores, 0, keepdims=True)
        e = jnp.exp(scores - top)
        total = jnp.sum(e, 0, keepdims=True)
        weights = (e * (1.0 / total)).astype(bf16)
        r.lse[i] = top + jnp.log(total)
        mixed = dot(weights, values, TN)
        r.att[:, cols] = jnp.where(low_lane, mixed[:quarter], mixed[quarter:]).astype(bf16)
        return carry

    lax.fori_loop(0, pairs // 2, self_pair, 0)
    step(5)
    lax.fori_loop(pairs // 2, pairs, self_pair, 0)
    g.ready(2)

    def project(v, k):
        return jnp.concatenate([dot(v, half_of(w[k], h)) for h in range(2)], 1)

    swap.send("att", r.att, r.by_att)
    first_sum = tokens + project(r.att[...], 2)
    r.first[...] = first_sum
    r.n2[...] = affine(norm_parts(first_sum)[0], 1)
    swap.send("n2", r.n2, r.by_n2)
    step(6)
    g.ready(3)
    r.cq[...] = project(r.n2[...], 3).astype(bf16)
    slots = r.neighbours.shape[0]
    span = quarter // (slots // 2)

    def cross_pair(i, carry):
        cols = pl.ds(pl.multiple_of(i * LANES, LANES), LANES)
        vcols = pl.ds(pl.multiple_of(i * LANES + w[1].shape[-1], LANES), LANES)
        for b in range(slots // 2):
            two = [lax.rem(r.index[2 * b + j], slots) for j in range(2)]
            rows = slice(b * span, (b + 1) * span)
            queries = stacked(r.cq[rows, cols], low, high) * bf16(HEAD**-0.5)
            keys = jnp.concatenate([r.pool[t, :, cols] for t in two], 0)
            values = jnp.concatenate([r.pool[t, :, vcols] for t in two], 0)
            scores = dot(keys, queries, NT)
            top = jnp.max(scores, 0, keepdims=True)
            e = jnp.exp(scores - top)
            total = jnp.sum(e, 0, keepdims=True)
            weights = (e * (1.0 / total)).astype(bf16)
            r.lse_cross[i, b : b + 1] = top + jnp.log(total)
            mixed = dot(weights, values, TN)
            r.cm[rows, cols] = jnp.where(low_lane, mixed[:span], mixed[span:]).astype(bf16)
        return carry

    lax.fori_loop(0, pairs, cross_pair, 0)
    step(7)
    g.ready(4)
    swap.send("cm", r.cm, r.by_cm)
    second_sum = r.first[...] + project(r.cm[...], 4)
    r.second[...] = second_sum
    r.n3[...] = affine(norm_parts(second_sum)[0], 2)
    swap.send("n3", r.n3, r.by_n3)
    step(8)
    hidden_half = w[5].shape[-1]

    def up_tiles(start, width, tile):
        def body(i, carry):
            h, col = lax.div(i, width // tile), start + lax.rem(i, width // tile) * tile
            col = pl.multiple_of(col, tile)
            hidden = dot(r.n3[...], half_of(w[5], h, col, tile))
            cdf = 0.5 * (1.0 + lax.erf(hidden * (0.5**0.5)))
            density = jnp.exp(-0.5 * hidden * hidden) * ((2 * math.pi) ** -0.5)
            cols = pl.ds(pl.multiple_of(h * hidden_half + col, tile), tile)
            r.act[:, cols] = (hidden * cdf).astype(bf16)
            r.slope[:, cols] = (cdf + hidden * density).astype(bf16)
            return carry

        lax.fori_loop(0, 2 * (width // tile), body, 0)

    g.ready(5)
    up_tiles(0, 768, 256)
    step(9)
    g.ready(6)
    up_tiles(768, 768, 256)
    swap.send("act", r.act.at[:, pl.ds(pl.multiple_of(p.o * hidden_half, LANES), hidden_half)], r.by_act)
    step(10)
    for q in (7, 8):
        g.ready(q)
        col = g.chunks[q][1]
        cols = slice(col, col + 384)
        down = sum(dot(r.act[:, h * hidden_half : (h + 1) * hidden_half], half_of(w[6], h, col, 384)) for h in range(2))
        r.out[:, cols] = (r.second[:, cols] + down).astype(bf16)
    first.wait_send()
    for cp in (kv_c, kv_y, kv_d):
        cp.wait_send()


class Reduce:
    def __init__(self, place, r, chunks, send, recv):
        self.p, self.r, self.w, self.chunks, self.ss, self.rs = place, r, r.w, chunks, send, recv
        self.sent, self.open, self.under_way = [], set(), {}
        self.starts = [sum(v.shape[-1] for v in r.w[:k]) for k in range(6)]

    def free(self, k):
        p = self.p
        for device in (p.to_x, p.to_y, *p.to_z):
            pl.semaphore_signal(self.r.credit.at[k], inc=1, device_id=device, device_id_type=MESH)

    def at(self, q, half, z, xy):
        k, start, width, _ = self.chunks[q]
        return self.w[k].at[half, z, xy, :, pl.ds(start, width)]

    def load(self, q, half, z, xy):
        k, start, width, _ = self.chunks[q]
        return self.w[k][half, z, xy, :, start : start + width].astype(f32)

    def save(self, q, half, z, xy, v):
        k, start, width, _ = self.chunks[q]
        self.w[k][half, z, xy, :, start : start + width] = v.astype(bf16)

    def copy(self, q, j, src, dst, device):
        cp = remote(src, dst, self.ss.at[q, j], self.rs.at[q, j], device)
        cp.start()
        self.sent.append(cp)

    def wait(self, q, j, ref):
        remote(ref, ref, self.ss.at[q, j], self.rs.at[q, j], self.p.to_c).wait_recv()

    def diagonal(self, q):
        p, (k, _, _, cut) = self.p, self.chunks[q]
        if k not in self.open:
            pl.semaphore_wait(self.r.credit.at[k], 1 + p.nz)
            self.open.add(k)
        for j, z, device in ((0, pl.ds(0, cut), p.to_y), (1, pl.ds(cut, p.nz - cut), p.to_x)):
            self.copy(q, j, self.at(q, p.c, z, p.at_d), self.at(q, p.o, z, 0), device)

    def across(self, q):
        p, cut, allz = self.p, self.chunks[q][3], slice(None)
        for j, zs, to in ((0, range(cut), p.at_x), (1, range(cut, p.nz), p.at_y)):
            self.wait(q, j, self.at(q, p.o, pl.ds(zs[0], len(zs)), 0))
            for z in zs:
                self.save(q, p.c, z, to, self.load(q, p.c, z, to) + self.load(q, p.o, z, 0))
        self.copy(q, 2, self.at(q, p.c, allz, p.at_x), self.at(q, p.o, allz, 1), p.to_x)
        self.copy(q, 3, self.at(q, p.c, allz, p.at_y), self.at(q, p.o, allz, 2), p.to_y)

    def along_z(self, q):
        p, allz = self.p, slice(None)
        self.wait(q, 2, self.at(q, p.o, allz, 1))
        self.wait(q, 3, self.at(q, p.o, allz, 2))
        for z in range(p.nz):
            total = self.load(q, p.c, z, p.own) + self.load(q, p.o, z, 1) + self.load(q, p.o, z, 2)
            self.save(q, p.c, z, p.own, total)
        for j, device in enumerate(p.to_z):
            self.copy(q, 4 + j, self.at(q, p.c, p.z_of[j], p.own), self.at(q, p.o, j, 3), device)

    def last(self, q):
        p, r, (k, start, width, _) = self.p, self.r, self.chunks[q]
        total = self.load(q, p.c, p.z, p.own)
        for j in range(p.nz - 1):
            self.wait(q, 4 + j, self.at(q, p.o, j, 3))
            total = total + self.load(q, p.o, j, 3)
        cols = slice(start, start + width)
        if k == 6:
            r.sums[6][:, cols] = total
            return
        rows = total.shape[0] // 2
        r.sums[k][p.c, :, cols] = jnp.where(p.c == 0, total[:rows], total[rows:])
        there = slice(self.starts[k] + start, self.starts[k] + start + width)
        r.beside[:, there] = jnp.where(p.c == 0, total[rows:], total[:rows])
        self.copy(q, 7, r.beside.at[:, there], r.sums[k].at[p.c, :, cols], p.to_c)

    def finish(self, q):
        p, (k, start, width, _) = self.p, self.chunks[q]
        if k != 6:
            self.wait(q, 7, self.r.sums[k].at[p.o, :, pl.ds(start, width)])

    def push(self, q=None):
        if q is not None:
            self.diagonal(q)
        for other in sorted(self.under_way, reverse=True):
            (self.across, self.along_z, self.last)[self.under_way[other]](other)
            self.under_way[other] += 1
            if self.under_way[other] == 3:
                del self.under_way[other]
        if q is not None:
            self.under_way[q] = 0

    def drain(self):
        while self.under_way:
            self.push()
        for q in range(len(self.chunks)):
            self.finish(q)


class Swap:
    def __init__(self, place, sems):
        self.p, self.sems, self.n, self.sent, self.landed = place, sems, 0, [], {}

    def send(self, name, src, dst):
        cp = remote(src, dst, self.sems.at[0, self.n], self.sems.at[1, self.n], self.p.to_c)
        cp.start()
        self.sent.append(cp)
        self.landed[name] = cp
        self.n += 1

    def wait(self, name):
        self.landed.pop(name).wait_recv()


def norm_back_at(grad, v, gain):
    unit, inv = norm_parts(v)
    scaled = grad * gain
    back = inv * (
        scaled - jnp.mean(scaled, -1, keepdims=True) - unit * jnp.mean(scaled * unit, -1, keepdims=True)
    )
    return back, jnp.sum(grad * unit, 0, keepdims=True), jnp.sum(grad, 0, keepdims=True)


def backward(p, r, g, swap, red, kv_sem, pairs):
    w, c, o = r.w, p.c, p.o
    quarter, width = r.tokens.shape
    hidden_half, pool_half = w[5].shape[-1], w[1].shape[-1]
    slots, rows_n = r.neighbours.shape[:2]
    low_lane, low, high = lane_masks()
    r.vec_sum[...] = jnp.zeros_like(r.vec_sum)

    def half(ref, h, size):
        return ref.at[:, pl.ds(pl.multiple_of(h * size, LANES), size)]

    def input_grad(ref, k, size):
        return sum(dot(ref[:, h * size : (h + 1) * size], half_of(w[k], h, 0, size), NT) for h in range(2))

    def weight_grad(k, left, left_beside, right, right_beside, size, tile=384, base=0, tiles=2):
        rows, per = w[k].shape[3], tile // (4 * w[k].shape[3])
        cut = size // 2 if size > 768 and size % 256 == 0 else size
        if size == 1152:
            cut = 384

        def body(i, carry):
            cols = pl.ds(pl.multiple_of(base + i * tile, LANES), tile)
            beside = pl.ds(pl.multiple_of(i * tile, LANES), tile)
            for start in range(0, size, cut):
                part = dot(left(cols), right(start, cut), TN) + dot(left_beside(beside), right_beside(start, cut), TN)
                w[k][c, pl.ds(i * per, per), :, :, start : start + cut] = part.astype(bf16).reshape(per, 4, rows, cut)
            return carry

        lax.fori_loop(0, tiles, body, 0)

    def plain_grad(k, left, left_beside, right, right_beside, size):
        weight_grad(
            k,
            lambda cols: left[:, cols],
            lambda cols: left_beside[:, cols],
            lambda start, n: right[:, pl.ds(pl.multiple_of(c * size + start, LANES), n)],
            lambda start, n: right_beside[:, start : start + n],
            size,
        )

    def gain(i):
        return r.vec[0, i : i + 1]

    def keep_vec(i, gain_sum, shift_sum):
        r.vec_sum[0, i : i + 1] = gain_sum
        r.vec_sum[1, i : i + 1] = shift_sum

    def act_tile(i, carry):
        h, z = lax.div(i, p.nz), lax.rem(i, p.nz)
        rows = w[6][h, z].reshape(-1, width)
        cols = pl.ds(pl.multiple_of(i * rows.shape[0], LANES), rows.shape[0])
        r.slope[:, cols] = (dot(r.cotangent[...], rows, NT) * r.slope[:, cols].astype(f32)).astype(bf16)
        return carry

    lax.fori_loop(0, 2 * p.nz, act_tile, 0)
    gh = r.slope
    red.free(6)
    swap.send("gh", half(gh, o, hidden_half), r.by_hidden_grad)
    for name in ("act", "cot"):
        swap.wait(name)
    for q in (7, 8):
        g.settle(q)
    down_rows = 4 * w[6].shape[3]
    weight_grad(
        6,
        lambda cols: r.act[:, cols],
        lambda cols: r.by_act[:, cols],
        lambda start, n: r.cotangent[:, start : start + n],
        lambda start, n: r.by_cot[:, start : start + n],
        width,
        tile=down_rows,
        base=c * hidden_half,
        tiles=p.nz,
    )
    red.push(0)
    red.push(1)
    grad_three = input_grad(gh, 5, hidden_half)
    red.free(5)
    for q in (5, 6):
        g.settle(q)
    back, dg, db = norm_back_at(grad_three, r.second[...], gain(2))
    keep_vec(2, dg, db)
    grad_second = r.cotangent[...].astype(f32) + back
    r.second[...] = grad_second
    r.branch[...] = grad_second.astype(bf16)
    swap.send("gcb", half(r.branch, o, width // 2), r.by_branch)
    r.mixed_grad[...] = input_grad(r.branch, 4, width // 2).astype(bf16)
    red.free(4)
    g.settle(4)
    for name in ("gh", "n3"):
        swap.wait(name)
    plain_grad(5, r.n3, r.by_n3, gh, r.by_hidden_grad, hidden_half)
    red.push(2)
    red.push(3)

    span = quarter // (slots // 2)

    def cross_pair(i, carry):
        cols = pl.ds(pl.multiple_of(i * LANES, LANES), LANES)
        vcols = pl.ds(pl.multiple_of(i * LANES + pool_half, LANES), LANES)
        for b in range(slots // 2):
            two = [lax.rem(r.index[2 * b + j], slots) for j in range(2)]
            rows = slice(b * span, (b + 1) * span)
            queries = stacked(r.cq[rows, cols], low, high) * bf16(HEAD**-0.5)
            grads = stacked(r.mixed_grad[rows, cols], low, high)
            keys = jnp.concatenate([r.pool[t, :, cols] for t in two], 0)
            values = jnp.concatenate([r.pool[t, :, vcols] for t in two], 0)
            probs = jnp.exp(dot(keys, queries, NT) - r.lse_cross[i, b : b + 1])
            grad_probs = dot(values, grads, NT)
            score_grad = (probs * (grad_probs - jnp.sum(probs * grad_probs, 0, keepdims=True))).astype(bf16)
            r.gkv[b, :, cols] = dot(score_grad, queries).astype(bf16)
            r.gkv[b, :, vcols] = dot(probs.astype(bf16), grads).astype(bf16)
            gq = dot(score_grad, keys, TN) * HEAD**-0.5
            r.cq_grad[rows, cols] = jnp.where(low_lane, gq[:span], gq[span:]).astype(bf16)
        return carry

    lax.fori_loop(0, pairs, cross_pair, 0)
    swap.send("gcq", half(r.cq_grad, o, width // 2), r.by_cq_grad)
    grad_two = input_grad(r.cq_grad, 3, width // 2)
    red.free(3)
    g.settle(3)
    back, dg, db = norm_back_at(grad_two, r.first[...], gain(1))
    keep_vec(1, dg, db)
    grad_first = r.second[...] + back
    r.first[...] = grad_first
    r.self_branch[...] = grad_first.astype(bf16)
    swap.send("gsb", half(r.self_branch, o, width // 2), r.by_self_branch)
    r.att_grad[...] = input_grad(r.self_branch, 2, width // 2).astype(bf16)
    red.free(2)
    g.settle(2)
    for s in range(slots):
        j = 0
        for k in range(slots):
            j = jnp.where(lax.rem(r.index[k], slots) == s, k, j)
        b, odd = lax.div(j, 2), lax.rem(j, 2)
        r.pool_grad[s] = jnp.where(odd == 0, r.gkv[b, :rows_n], r.gkv[b, rows_n:])
    swap.send("gp", r.pool_grad.at[:, :, pl.ds(pl.multiple_of(o * pool_half, LANES), pool_half)], r.by_pool_grad)
    swap.wait("gcb")
    swap.wait("cm")
    plain_grad(4, r.cm, r.by_cm, r.branch, r.by_branch, width // 2)
    red.push(4)

    cosine, signed = r.rope[:, :LANES], r.rope[:, LANES:]
    place = lax.rem(lax.broadcasted_iota(jnp.int32, (1, 2 * quarter), 1), quarter) + p.s * quarter
    limit = jnp.maximum(place, r.prefix[0] - 1)

    def self_pair(i, carry):
        cols = pl.ds(pl.multiple_of(i * LANES, LANES), LANES)
        vcols = pl.ds(pl.multiple_of(i * LANES + pool_half, LANES), LANES)
        queries = stacked(r.q[:, cols], low, high) * bf16(HEAD**-0.5)
        grads = stacked(r.att_grad[:, cols], low, high)
        keys = r.kv[:, :, cols].reshape(-1, LANES)
        values = r.kv[:, :, vcols].reshape(-1, LANES)
        scores = dot(keys, queries, NT)
        key_place = lax.broadcasted_iota(jnp.int32, scores.shape, 0)
        probs = jnp.exp(jnp.where(key_place <= limit, scores, masked) - r.lse[i])
        grad_probs = dot(values, grads, NT)
        score_grad = (probs * (grad_probs - jnp.sum(probs * grad_probs, 0, keepdims=True))).astype(bf16)
        r.gkv[:, :, cols] = dot(score_grad, queries).astype(bf16).reshape(4, quarter, LANES)
        r.gkv[:, :, vcols] = dot(probs.astype(bf16), grads).astype(bf16).reshape(4, quarter, LANES)
        gq = dot(score_grad, keys, TN) * HEAD**-0.5
        gq = jnp.where(low_lane, gq[:quarter], gq[quarter:])
        r.joined_grad[:, cols] = rotate(gq, cosine, -signed).astype(bf16)
        return carry

    lax.fori_loop(0, pairs // 2, self_pair, 0)
    red.push()
    lax.fori_loop(pairs // 2, pairs, self_pair, 0)
    swap.send("far", r.gkv.at[p.s_d], r.kv_far)
    swap.send("near", r.gkv.at[p.s_c], r.kv_near)
    swap.wait("gcq")
    swap.wait("n2")
    plain_grad(3, r.n2, r.by_n2, r.cq_grad, r.by_cq_grad, width // 2)
    swap.wait("far")
    r.gkv[p.s_y] = (r.gkv[p.s_y].astype(f32) + r.kv_far[...].astype(f32)).astype(bf16)
    far = remote(r.gkv.at[p.s_y], r.kv_y, kv_sem.at[6], kv_sem.at[7], p.to_y)
    far.start()
    red.push(5)
    swap.wait("gsb")
    swap.wait("att")
    plain_grad(2, r.att, r.by_att, r.self_branch, r.by_self_branch, width // 2)
    red.push(6)

    out = [None, None]
    for s in range(slots):
        rows = r.pool_grad[s]
        part = sum(
            dot(rows[:, h * pool_half : (h + 1) * pool_half], half_of(w[1], h), NT) for h in range(2)
        )
        if out[s % 2] is not None:
            out[s % 2].wait()
        r.stage[s % 2] = part
        out[s % 2] = pltpu.make_async_copy(r.stage.at[s % 2], r.neighbours_grad.at[s], r.out_sem.at[s % 2])
        out[s % 2].start()
    red.free(1)
    g.settle(1)
    swap.wait("gp")
    swap.wait("nb")
    size = slots * rows_n
    weight_grad(
        1,
        lambda cols: r.neighbours[:, :, cols].reshape(size, -1),
        lambda cols: r.by_neighbours[:, :, cols].reshape(size, -1),
        lambda start, n: r.pool_grad[:, :, pl.ds(pl.multiple_of(c * pool_half + start, LANES), n)].reshape(size, -1),
        lambda start, n: r.by_pool_grad[:, :, start : start + n].reshape(size, -1),
        pool_half,
    )
    red.push(7)
    remote(r.gkv.at[p.s_y], r.kv_y, kv_sem.at[6], kv_sem.at[7], p.to_y).wait_recv()
    swap.wait("near")
    for start in range(0, 2 * width, LANES):
        cols = slice(start, start + LANES)
        total = r.gkv[p.s, :, cols].astype(f32) + r.kv_near[:, cols].astype(f32) + r.kv_y[:, cols].astype(f32)
        if start < width:
            total = rotate(total, cosine, -signed)
        r.joined_grad[:, width + start : width + start + LANES] = total.astype(bf16)
    joined_half = 3 * width // 2
    swap.send("gj", half(r.joined_grad, o, joined_half), r.by_joined_grad)
    grad_one = input_grad(r.joined_grad, 0, joined_half)
    red.free(0)
    g.settle(0)
    back, dg, db = norm_back_at(grad_one, r.tokens[...].astype(f32), gain(0))
    keep_vec(0, dg, db)
    r.tokens_grad[...] = r.first[...] + back
    swap.send("vec", r.vec_sum.at[o], r.by_vec)
    swap.wait("gj")
    swap.wait("n1")
    plain_grad(0, r.n1, r.by_n1, r.joined_grad, r.by_joined_grad, joined_half)
    swap.wait("vec")
    vec = r.vec_sum[c] + r.by_vec[...]
    vec = jnp.concatenate([vec, jnp.zeros((LANES - 8, width), f32)], 0)
    w[0][c, :, :, :, joined_half:] = jnp.transpose(vec).astype(bf16).reshape(p.nz, 4, -1, LANES)
    for q in range(8, len(red.chunks)):
        red.push(q)
    red.drain()
    for cp in (*red.sent, *swap.sent, far):
        cp.wait_send()
    for cp in out:
        cp.wait()


def rope_table(length):
    half = HEAD // 2
    freq = (10000.0 ** (-np.arange(half, dtype=np.float32) / half)).astype(np.float32)
    angles = np.arange(length, dtype=np.float32)[:, None] * freq[None, :]
    cosine, sine = np.cos(angles), np.sin(angles)
    table = np.concatenate([cosine] * 4 + [-sine, sine] * 2, 1)
    return table.astype(np.float32).reshape(4, -1, 2 * LANES)


def column_halves(v):
    return v[:, : v.shape[1] // 2], v[:, v.shape[1] // 2 :]


def shard_halves(w_qkv, w_cross_kv, w_out, w_cross_q, w_cross_out, w_up, gains, shifts, nz):
    rows = w_qkv.shape[0]
    up = jnp.swapaxes(w_up.reshape(rows, nz * 4, 2, -1), 1, 2).reshape(rows, -1)
    pads = [jnp.pad(jnp.stack(v, 1), ((0, 0), (0, LANES - 3))) for v in (gains, shifts)]
    parts = [column_halves(v) for v in (w_qkv, w_cross_kv, w_out, w_cross_q, w_cross_out, up)]
    return jnp.stack(
        [jnp.concatenate([parts[0][h], pads[h], *(v[h] for v in parts[1:])], 1) for h in range(2)]
    ).astype(f32)


class Refs:
    def take(self, names, refs):
        for name, ref in zip(names, refs, strict=True):
            setattr(self, name, ref)


NAMES_IN = ("shards", "w_down", "tokens", "cotangent", "prefix", "neighbours", "index", "rope_table")
NAMES_OUT = ("out", "tokens_grad", "neighbours_grad")
GATHER = (
    (0, 0, 1280, 2),
    (1, 0, 768, 2),
    (2, 0, 384, 2),
    (3, 0, 384, 2),
    (4, 0, 384, 2),
    (5, 0, 768, 2),
    (5, 768, 768, 2),
    (6, 0, 384, 2),
    (6, 384, 384, 2),
)
REDUCE = (
    (6, 0, 384, 2),
    (6, 384, 384, 2),
    (5, 0, 768, 2),
    (5, 768, 768, 2),
    (4, 0, 384, 2),
    (3, 0, 384, 2),
    (2, 0, 384, 2),
    (1, 0, 768, 2),
    (0, 0, 640, 2),
    (0, 640, 640, 2),
)


def memory(nz, quarter, width, hidden, slots, rows_n, rows):
    halves = (3 * width // 2 + LANES, width, width // 2, width // 2, width // 2, hidden // 2)
    weights = [((2, nz, 4, 2 * rows, h), bf16) for h in halves]
    weights.append(((2, nz, 4, hidden // (8 * nz), width), bf16))
    sums = [((2, rows, h), f32) for h in halves]
    sums.append(((hidden // (8 * nz), width), f32))
    tok, half_tok = ((quarter, width), bf16), ((quarter, width // 2), bf16)
    half_hidden = ((quarter, hidden // 2), bf16)
    pool_half = ((slots, rows_n, width), bf16)
    kv = ((quarter, 2 * width), bf16)
    arrays = dict(
        beside=((rows, sum(halves)), f32),
        rope=((quarter, 2 * LANES), f32),
        n1=tok,
        q=tok,
        kv=((4, *kv[0]), bf16),
        att=tok,
        lse=((width // LANES, 1, 2 * quarter), f32),
        first=((quarter, width), f32),
        n2=tok,
        cq=tok,
        pool=((slots, rows_n, 2 * width), bf16),
        lse_cross=((width // LANES, 8, LANES), f32),
        cm=tok,
        second=((quarter, width), f32),
        n3=tok,
        act=((quarter, hidden), bf16),
        slope=((quarter, hidden), bf16),
        vec=((2, 8, width), f32),
        branch=tok,
        mixed_grad=tok,
        cq_grad=tok,
        self_branch=tok,
        att_grad=tok,
        joined_grad=((quarter, 3 * width), bf16),
        pool_grad=((slots, rows_n, 2 * width), bf16),
        gkv=((4, *kv[0]), bf16),
        kv_far=kv,
        kv_near=kv,
        kv_y=kv,
        stage=((2, rows_n, width), f32),
        vec_sum=((2, 8, width), f32),
        by_act=half_hidden,
        by_cot=tok,
        by_n3=tok,
        by_hidden_grad=half_hidden,
        by_cm=tok,
        by_branch=half_tok,
        by_neighbours=pool_half,
        by_pool_grad=pool_half,
        by_n2=tok,
        by_cq_grad=half_tok,
        by_att=tok,
        by_self_branch=half_tok,
        by_n1=tok,
        by_joined_grad=((quarter, 3 * width // 2), bf16),
        by_vec=((8, width), f32),
    )
    return weights, arrays, sums


def layer_kernel(nz, names, *refs):
    refs = list(refs)
    r = Refs()

    def some(n):
        taken = refs[:n]
        del refs[:n]
        return taken

    r.take(NAMES_IN, some(len(NAMES_IN)))
    r.take(NAMES_OUT, some(len(NAMES_OUT)))
    r.sums, r.w = some(7), some(7)
    r.take(names, some(len(names)))
    r.pair_sem, r.rope_sem, r.out_sem, kv_sem, swap_sem, g_send, g_recv, r_send, r_recv, r.credit = refs
    p = Place(nz)
    barrier = pltpu.get_barrier_semaphore()
    friends = [*p.to_z, p.to_x, p.to_y, p.to_c]
    for device in friends:
        pl.semaphore_signal(barrier, inc=1, device_id=device, device_id_type=MESH)
    pl.semaphore_wait(barrier, len(friends))
    g = Gather(p, r.w, GATHER, g_send, g_recv)
    swap = Swap(p, swap_sem)
    pairs = r.tokens.shape[1] // LANES
    forward(p, r, g, swap, kv_sem, pairs)
    red = Reduce(p, r, REDUCE, r_send, r_recv)
    backward(p, r, g, swap, red, kv_sem, pairs)


def local_fast(
    tokens,
    prefix_len,
    neighbours,
    neighbour_index,
    w_qkv,
    w_out,
    w_cross_q,
    w_cross_kv,
    w_cross_out,
    w_up,
    w_down,
    gain_one,
    shift_one,
    gain_two,
    shift_two,
    gain_three,
    shift_three,
    cotangent,
):
    nz = lax.axis_size("dp") // 2
    quarter, width = tokens.shape[1:]
    rows, hidden = w_up.shape
    slots, rows_n = neighbours.shape[1:3]
    shards = shard_halves(
        w_qkv, w_cross_kv, w_out, w_cross_q, w_cross_out, w_up,
        (gain_one, gain_two, gain_three), (shift_one, shift_two, shift_three), nz,
    )
    weights, arrays, sums = memory(nz, quarter, width, hidden, slots, rows_n, rows)
    vmem, smem, anywhere = (pl.BlockSpec(memory_space=m) for m in (pltpu.VMEM, pltpu.SMEM, pl.ANY))
    made = [((quarter, width), bf16), ((quarter, width), f32), ((slots, rows_n, width), f32), *sums]
    dma = pltpu.SemaphoreType.DMA
    out, tokens_grad, neighbours_grad, *summed = pl.pallas_call(
        functools.partial(layer_kernel, nz, tuple(arrays)),
        out_shape=[jax.ShapeDtypeStruct(*v) for v in made],
        in_specs=[vmem, vmem, vmem, vmem, smem, vmem, smem, anywhere],
        out_specs=[vmem, vmem, anywhere] + [vmem] * len(sums),
        scratch_shapes=[pltpu.VMEM(*v) for v in (*weights, *arrays.values())]
        + [
            dma((2,)),
            dma,
            dma((2,)),
            dma((8,)),
            dma((2, 20)),
            dma((len(GATHER), 12)),
            dma((len(GATHER), 12)),
            dma((len(REDUCE), 8)),
            dma((len(REDUCE), 8)),
            pltpu.SemaphoreType.REGULAR((7,)),
        ],
        compiler_params=pltpu.CompilerParams(
            collective_id=0, has_side_effects=True, vmem_limit_bytes=64 * 2**20 - 2**17
        ),
    )(
        shards, w_down, tokens[0], cotangent[0], prefix_len, neighbours[0],
        neighbour_index.reshape(-1), jnp.asarray(rope_table(4 * quarter)),
    )
    whole = [jnp.concatenate([v[0], v[1]], 1) for v in summed[1:5]]
    half = 3 * width // 2
    up = jnp.concatenate([v.reshape(rows, 4 * nz, 1, -1) for v in summed[5]], 2)
    vectors = [summed[0][h, :, half + i] for i in range(3) for h in range(2)]
    return (
        out[None],
        tokens_grad[None],
        neighbours_grad[None],
        jnp.concatenate([summed[0][0, :, :half], summed[0][1, :, :half]], 1),
        whole[1],
        whole[2],
        whole[0],
        whole[3],
        up.reshape(rows, hidden),
        summed[6],
        *vectors,
    )


def pick_slots(pool, index):
    return jnp.stack(
        [
            jnp.concatenate([lax.dynamic_slice_in_dim(pool[s], index[s, j], 1, 0) for j in range(index.shape[1])], 0)
            for s in range(index.shape[0])
        ]
    )


def slot_places(index):
    slots = index.shape[1]
    same = index[:, :, None] == jnp.arange(slots)[None, None, :]
    return jnp.sum(jnp.where(same, jnp.arange(slots)[None, :, None], 0), 1)


def dense_dot(left_side, weight):
    return jnp.dot(left_side, weight, preferred_element_type=jnp.float32)


def input_grad(grad_out, weight):
    return lax.dot_general(
        grad_out,
        weight,
        (((grad_out.ndim - 1,), (1,)), ((), ())),
        preferred_element_type=jnp.float32,
    )


def weight_grad(left_side, grad_out):
    flat_left = left_side.reshape(-1, left_side.shape[-1])
    flat_grad = grad_out.reshape(-1, grad_out.shape[-1])
    return lax.dot_general(
        flat_left, flat_grad, (((0,), (0,)), ((), ())), preferred_element_type=jnp.float32
    )


def plain_norm_parts(array_in):
    avg_value = jnp.mean(array_in, -1, keepdims=True)
    centred = array_in - avg_value
    inv_std = lax.rsqrt(jnp.mean(centred * centred, -1, keepdims=True) + eps)
    return (centred * inv_std, inv_std)


def norm_back(grad_out, unit_part, inv_std, gain_f):
    scaled = grad_out * gain_f
    grad_in = inv_std * (
        scaled
        - jnp.mean(scaled, -1, keepdims=True)
        - unit_part * jnp.mean(scaled * unit_part, -1, keepdims=True)
    )
    return (grad_in, jnp.sum(grad_out * unit_part, (0, 1)), jnp.sum(grad_out, (0, 1)))


def rotary_tables(positions):
    half_size = HEAD // 2
    frequency = 10000.0 ** (-jnp.arange(half_size).astype(jnp.float32) / half_size)
    angles = positions.astype(jnp.float32)[:, None] * frequency[None, :]
    return (jnp.cos(angles)[:, None, :], jnp.sin(angles)[:, None, :])


def plain_rotate(array_in, cosine, sine_part):
    half_size = HEAD // 2
    first_half = array_in[..., :half_size]
    second = array_in[..., half_size:]
    return jnp.concatenate(
        [first_half * cosine - second * sine_part, second * cosine + first_half * sine_part], -1
    )


def unrotate(grad_in, cosine, sine_part):
    half_size = HEAD // 2
    first_half = grad_in[..., :half_size]
    second = grad_in[..., half_size:]
    return jnp.concatenate(
        [first_half * cosine + second * sine_part, second * cosine - first_half * sine_part], -1
    )


def grouped(array_in):
    split_heads = array_in.reshape(
        array_in.shape[0], array_in.shape[1], array_in.shape[2] // 4, 4, array_in.shape[3]
    )
    return jnp.moveaxis(split_heads, 2, 0)


def ungrouped(array_in):
    shifted_axes = jnp.moveaxis(array_in, 0, 2)
    return shifted_axes.reshape(
        shifted_axes.shape[0], shifted_axes.shape[1], -1, shifted_axes.shape[-1]
    )


def masked_scores(visible, queries, key_rows):
    scores = jnp.einsum(
        "sqhd,skhd->shqk", queries, key_rows, preferred_element_type=jnp.float32
    ) * HEAD ** (-0.5)
    return jnp.where(visible[:, None], scores, masked)


def attend_group(visible, packed):
    queries, key_rows, values = packed
    scores = masked_scores(visible, queries, key_rows)
    row_max = jnp.max(scores, -1, keepdims=True)
    exp_scores = jnp.exp(scores - row_max)
    row_total = jnp.sum(exp_scores, -1, keepdims=True)
    probabilities = (exp_scores / row_total).astype(jnp.bfloat16)
    mixed_out = jnp.einsum(
        "shqk,skhd->sqhd", probabilities, values, preferred_element_type=jnp.float32
    )
    return (mixed_out, (row_max + jnp.log(row_total))[..., 0])


def attend_back(visible, packed):
    queries, key_rows, values, grad_out, logsum = packed
    scores = masked_scores(visible, queries, key_rows)
    probabilities = jnp.exp(scores - logsum[..., None])
    grad_probs = jnp.einsum("sqhd,skhd->shqk", grad_out, values, preferred_element_type=jnp.float32)
    grad_scores = (
        probabilities * (grad_probs - jnp.sum(probabilities * grad_probs, -1, keepdims=True))
    ).astype(jnp.bfloat16)
    grad_query = jnp.einsum(
        "shqk,skhd->sqhd", grad_scores, key_rows, preferred_element_type=jnp.float32
    ) * HEAD ** (-0.5)
    grad_key = jnp.einsum(
        "shqk,sqhd->skhd", grad_scores, queries, preferred_element_type=jnp.float32
    ) * HEAD ** (-0.5)
    grad_value = jnp.einsum(
        "shqk,sqhd->skhd",
        probabilities.astype(jnp.bfloat16),
        grad_out,
        preferred_element_type=jnp.float32,
    )
    return (grad_query, grad_key, grad_value)


def local_plain(
    tokens,
    prefix_len,
    neighbours,
    neighbour_index,
    w_qkv,
    w_out,
    w_cross_q,
    w_cross_kv,
    w_cross_out,
    w_up,
    w_down,
    gain_one,
    shift_one,
    gain_two,
    shift_two,
    gain_three,
    shift_three,
    cotangent,
):
    forward_set = (
        lax.all_gather(w_qkv, ("dp", "seq"), axis=0, tiled=True),
        lax.all_gather(w_out, ("dp", "seq"), axis=0, tiled=True),
        lax.all_gather(w_cross_q, ("dp", "seq"), axis=0, tiled=True),
        lax.all_gather(w_cross_kv, ("dp", "seq"), axis=0, tiled=True),
        lax.all_gather(w_cross_out, ("dp", "seq"), axis=0, tiled=True),
        lax.all_gather(w_up, ("dp", "seq"), axis=0, tiled=True),
        lax.all_gather(w_down, ("dp", "seq"), axis=0, tiled=True),
        lax.all_gather(gain_one, ("dp", "seq"), axis=0, tiled=True),
        lax.all_gather(shift_one, ("dp", "seq"), axis=0, tiled=True),
        lax.all_gather(gain_two, ("dp", "seq"), axis=0, tiled=True),
        lax.all_gather(shift_two, ("dp", "seq"), axis=0, tiled=True),
        lax.all_gather(gain_three, ("dp", "seq"), axis=0, tiled=True),
        lax.all_gather(shift_three, ("dp", "seq"), axis=0, tiled=True),
    )
    (
        full_qkv,
        full_out,
        full_cross_q,
        full_cross_kv,
        full_cross_out,
        full_up,
        full_down,
        full_gain_one,
        full_shift_one,
        full_gain_two,
        full_shift_two,
        full_gain_three,
        full_shift_three,
    ) = forward_set
    seq_here, quarter, width = tokens.shape
    heads = width // HEAD
    hidden_width = full_up.shape[1]
    length = quarter * lax.axis_size("seq")
    seq_index = lax.axis_index("seq")
    query_pos = seq_index * quarter + jnp.arange(quarter)
    key_pos = jnp.arange(length)
    visible = (key_pos[None, None, :] <= query_pos[None, :, None]) | (
        key_pos[None, None, :] < prefix_len[:, None, None]
    )
    cosine, sine_part = rotary_tables(query_pos)
    gain_f1 = full_gain_one.astype(jnp.float32)
    gain_f2 = full_gain_two.astype(jnp.float32)
    gain_f3 = full_gain_three.astype(jnp.float32)
    resid_in = tokens.astype(jnp.float32)
    unit_one, inv_one = plain_norm_parts(resid_in)
    normed_one = (unit_one * gain_f1 + full_shift_one.astype(jnp.float32)).astype(jnp.bfloat16)
    joined = dense_dot(normed_one, full_qkv)
    query_rot = plain_rotate(
        joined[..., :width].reshape(seq_here, quarter, heads, HEAD), cosine, sine_part
    ).astype(jnp.bfloat16)
    key_local = (
        plain_rotate(
            joined[..., width : 2 * width].reshape(seq_here, quarter, heads, HEAD),
            cosine,
            sine_part,
        )
        .astype(jnp.bfloat16)
        .reshape(seq_here, quarter, width)
    )
    value_local = joined[..., 2 * width :].astype(jnp.bfloat16)
    key_all, value_all = (
        lax.all_gather(key_local, "seq", axis=1, tiled=True),
        lax.all_gather(value_local, "seq", axis=1, tiled=True),
    )
    key_heads = key_all.reshape(seq_here, length, heads, HEAD)
    value_heads = value_all.reshape(seq_here, length, heads, HEAD)
    attended, logsum = lax.map(
        functools.partial(attend_group, visible),
        (grouped(query_rot), grouped(key_heads), grouped(value_heads)),
    )
    attended = ungrouped(attended).reshape(seq_here, quarter, width).astype(jnp.bfloat16)
    first_sum = resid_in + dense_dot(attended, full_out)
    unit_two, inv_two = plain_norm_parts(first_sum)
    normed_two = (unit_two * gain_f2 + full_shift_two.astype(jnp.float32)).astype(jnp.bfloat16)
    cross_query = dense_dot(normed_two, full_cross_q).astype(jnp.bfloat16)
    pool_kv = dense_dot(neighbours, full_cross_kv).astype(jnp.bfloat16)
    slots = neighbours.shape[1]
    spans = slots // 2
    span_len = quarter // spans
    neighbour_rows = 2 * neighbours.shape[2]
    local_index = neighbour_index.reshape(seq_here, slots) - seq_index * slots
    picked = pick_slots(pool_kv, local_index)
    picked = picked.reshape(seq_here, spans, neighbour_rows, 2 * width)
    cross_keys = picked[..., :width].reshape(seq_here, spans, neighbour_rows, heads, HEAD)
    cross_values = picked[..., width:].reshape(seq_here, spans, neighbour_rows, heads, HEAD)
    cross_queries = cross_query.reshape(seq_here, spans, span_len, heads, HEAD)
    cross_scores = jnp.einsum(
        "scqhd,sckhd->schqk", cross_queries, cross_keys, preferred_element_type=jnp.float32
    ) * HEAD ** (-0.5)
    cross_probs = jax.nn.softmax(cross_scores, -1)
    cross_weights = cross_probs.astype(jnp.bfloat16)
    cross_mixed = jnp.einsum(
        "schqk,sckhd->scqhd", cross_weights, cross_values, preferred_element_type=jnp.float32
    )
    cross_mixed = cross_mixed.reshape(seq_here, quarter, width).astype(jnp.bfloat16)
    second_sum = first_sum + dense_dot(cross_mixed, full_cross_out)
    unit_three, inv_three = plain_norm_parts(second_sum)
    normed_three = (unit_three * gain_f3 + full_shift_three.astype(jnp.float32)).astype(
        jnp.bfloat16
    )
    hidden_pre = dense_dot(normed_three, full_up)
    activated = jax.nn.gelu(hidden_pre, approximate=False).astype(jnp.bfloat16)
    output = (second_sum + dense_dot(activated, full_down)).astype(jnp.bfloat16)
    grad_act = input_grad(cotangent, full_down)
    _, gelu_back = jax.vjp(functools.partial(jax.nn.gelu, approximate=False), hidden_pre)
    grad_hidden = gelu_back(grad_act)[0].astype(jnp.bfloat16)
    grad_normed_three = input_grad(grad_hidden, full_up)
    back_three, grad_gain_three, grad_shift_three = norm_back(
        grad_normed_three, unit_three, inv_three, full_gain_three.astype(jnp.float32)
    )
    grad_second = cotangent.astype(jnp.float32) + back_three
    grad_cross_branch = grad_second.astype(jnp.bfloat16)
    grad_mixed = (
        input_grad(grad_cross_branch, full_cross_out)
        .astype(jnp.bfloat16)
        .reshape(seq_here, spans, span_len, heads, HEAD)
    )
    grad_cross_probs = jnp.einsum(
        "scqhd,sckhd->schqk", grad_mixed, cross_values, preferred_element_type=jnp.float32
    )
    grad_cross_scores = (
        cross_probs
        * (grad_cross_probs - jnp.sum(cross_probs * grad_cross_probs, -1, keepdims=True))
    ).astype(jnp.bfloat16)
    grad_cross_query = (
        (
            jnp.einsum(
                "schqk,sckhd->scqhd",
                grad_cross_scores,
                cross_keys,
                preferred_element_type=jnp.float32,
            )
            * HEAD ** (-0.5)
        )
        .astype(jnp.bfloat16)
        .reshape(seq_here, quarter, width)
    )
    grad_cross_keys = jnp.einsum(
        "schqk,scqhd->sckhd", grad_cross_scores, cross_queries, preferred_element_type=jnp.float32
    ) * HEAD ** (-0.5)
    grad_cross_values = jnp.einsum(
        "schqk,scqhd->sckhd", cross_weights, grad_mixed, preferred_element_type=jnp.float32
    )
    grad_picked = jnp.concatenate(
        [
            grad_cross_keys.reshape(seq_here, spans, neighbour_rows, width),
            grad_cross_values.reshape(seq_here, spans, neighbour_rows, width),
        ],
        -1,
    )
    grad_picked = grad_picked.reshape(seq_here, slots, neighbours.shape[2], 2 * width)
    grad_pool_kv = pick_slots(grad_picked.astype(jnp.bfloat16), slot_places(local_index))
    grad_neighbours = input_grad(grad_pool_kv, full_cross_kv)
    grad_normed_two = input_grad(grad_cross_query, full_cross_q)
    back_two, grad_gain_two, grad_shift_two = norm_back(
        grad_normed_two, unit_two, inv_two, full_gain_two.astype(jnp.float32)
    )
    grad_first = grad_second + back_two
    grad_self_branch = grad_first.astype(jnp.bfloat16)
    grad_attended = (
        input_grad(grad_self_branch, full_out)
        .astype(jnp.bfloat16)
        .reshape(seq_here, quarter, heads, HEAD)
    )
    grad_query, grad_key_all, grad_value_all = lax.map(
        functools.partial(attend_back, visible),
        (
            grouped(query_rot),
            grouped(key_heads),
            grouped(value_heads),
            grouped(grad_attended),
            logsum,
        ),
    )
    grad_query = ungrouped(grad_query)
    grad_key_all = ungrouped(grad_key_all).reshape(seq_here, length, width)
    grad_value_all = ungrouped(grad_value_all).reshape(seq_here, length, width)
    grad_key, grad_value = (
        lax.psum_scatter(
            grad_key_all.astype(jnp.bfloat16), "seq", scatter_dimension=1, tiled=True
        ).astype(jnp.float32),
        lax.psum_scatter(
            grad_value_all.astype(jnp.bfloat16), "seq", scatter_dimension=1, tiled=True
        ).astype(jnp.float32),
    )
    grad_joined = jnp.concatenate(
        [
            unrotate(grad_query, cosine, sine_part).reshape(seq_here, quarter, width),
            unrotate(grad_key.reshape(seq_here, quarter, heads, HEAD), cosine, sine_part).reshape(
                seq_here, quarter, width
            ),
            grad_value,
        ],
        -1,
    ).astype(jnp.bfloat16)
    grad_normed_one = input_grad(grad_joined, full_qkv)
    back_one, grad_gain_one, grad_shift_one = norm_back(
        grad_normed_one, unit_one, inv_one, full_gain_one.astype(jnp.float32)
    )
    grad_tokens = grad_first + back_one
    norm_grads = jnp.stack(
        [
            grad_gain_one,
            grad_shift_one,
            grad_gain_two,
            grad_shift_two,
            grad_gain_three,
            grad_shift_three,
        ],
        1,
    )
    width_owned = lax.psum_scatter(
        jnp.concatenate(
            [
                weight_grad(normed_one, grad_joined),
                weight_grad(attended, grad_self_branch),
                weight_grad(normed_two, grad_cross_query),
                weight_grad(neighbours, grad_pool_kv),
                weight_grad(cross_mixed, grad_cross_branch),
                weight_grad(normed_three, grad_hidden),
                norm_grads,
            ],
            1,
        ),
        ("dp", "seq"),
        scatter_dimension=0,
        tiled=True,
    )
    down_owned = lax.psum_scatter(
        weight_grad(activated, cotangent), ("dp", "seq"), scatter_dimension=0, tiled=True
    )
    column = 8 * width + hidden_width
    return (
        output,
        grad_tokens,
        grad_neighbours,
        width_owned[:, : 3 * width],
        width_owned[:, 3 * width : 4 * width],
        width_owned[:, 4 * width : 5 * width],
        width_owned[:, 5 * width : 7 * width],
        width_owned[:, 7 * width : 8 * width],
        width_owned[:, 8 * width : column],
        down_owned,
        width_owned[:, column],
        width_owned[:, column + 1],
        width_owned[:, column + 2],
        width_owned[:, column + 3],
        width_owned[:, column + 4],
        width_owned[:, column + 5],
    )


def solution(mesh):
    sizes = dict(mesh.shape)
    fits = sizes == {"dp": 8, "seq": 4}
    return jax.shard_map(
        local_fast if fits else local_plain,
        mesh=mesh,
        in_specs=(
            P("dp", "seq", None),
            P("dp"),
            P("dp", "seq", None, None),
            P("dp", "seq", None),
            P(("dp", "seq"), None),
            P(("dp", "seq"), None),
            P(("dp", "seq"), None),
            P(("dp", "seq"), None),
            P(("dp", "seq"), None),
            P(("dp", "seq"), None),
            P(("dp", "seq"), None),
            P(("dp", "seq")),
            P(("dp", "seq")),
            P(("dp", "seq")),
            P(("dp", "seq")),
            P(("dp", "seq")),
            P(("dp", "seq")),
            P("dp", "seq", None),
        ),
        out_specs=(
            P("dp", "seq", None),
            P("dp", "seq", None),
            P("dp", "seq", None, None),
            P(("dp", "seq"), None),
            P(("dp", "seq"), None),
            P(("dp", "seq"), None),
            P(("dp", "seq"), None),
            P(("dp", "seq"), None),
            P(("dp", "seq"), None),
            P(("dp", "seq"), None),
            P(("dp", "seq")),
            P(("dp", "seq")),
            P(("dp", "seq")),
            P(("dp", "seq")),
            P(("dp", "seq")),
            P(("dp", "seq")),
        ),
        check_vma=False,
    )
```

```python
import functools
import math

import jax
import jax.numpy as jnp
import numpy as np
from jax import lax
from jax.experimental import pallas as pl
from jax.experimental.pallas import tpu as pltpu
from jax.sharding import PartitionSpec as P

HEAD = 64
eps = 1e-05
masked = -1e30
MESH = pl.DeviceIdType.MESH
bf16 = jnp.bfloat16
f32 = jnp.float32
NN = (((1,), (0,)), ((), ()))
NT = (((1,), (1,)), ((), ()))
TN = (((0,), (0,)), ((), ()))
LANES = 128
AHEAD = 2
TICKS_KV = 0


def dot(a, b, dims=NN):
    return lax.dot_general(a, b, dims, preferred_element_type=f32)


def norm_parts(v):
    centred = v - jnp.mean(v, -1, keepdims=True)
    inv = lax.rsqrt(jnp.mean(centred * centred, -1, keepdims=True) + eps)
    return centred * inv, inv


class Place:
    def __init__(self, nz):
        dp, s = lax.axis_index("dp"), lax.axis_index("seq")
        self.nz, self.dp, self.s = nz, dp, s
        self.z, self.x = lax.div(dp, 2), lax.rem(dp, 2)
        self.y, self.c = lax.div(s, 2), lax.rem(s, 2)
        x, y, z, c = self.x, self.y, self.z, self.c
        self.o = 1 - c
        self.own, self.at_x, self.at_y, self.at_d = (
            x * 2 + y,
            (1 - x) * 2 + y,
            x * 2 + 1 - y,
            (1 - x) * 2 + 1 - y,
        )
        self.to_z = [(lax.rem(z + j, nz) * 2 + x, s) for j in range(1, nz)]
        self.z_of = [lax.rem(z + j, nz) for j in range(1, nz)]
        self.z_from = [lax.rem(z - j + nz, nz) for j in range(1, nz)]
        self.to_x = (z * 2 + 1 - x, s)
        self.to_y = (dp, (1 - y) * 2 + c)
        self.to_c = (dp, y * 2 + 1 - c)
        self.s_y = (1 - y) * 2 + c
        self.s_c = y * 2 + 1 - c
        self.s_d = (1 - y) * 2 + 1 - c

    def meet(self):
        barrier = pltpu.get_barrier_semaphore()
        friends = [*self.to_z, self.to_x, self.to_y, self.to_c]
        for device in friends:
            pl.semaphore_signal(barrier, inc=1, device_id=device, device_id_type=MESH)
        pl.semaphore_wait(barrier, len(friends))


def remote(src, dst, send, recv, device):
    return pltpu.make_async_remote_copy(
        src_ref=src, dst_ref=dst, send_sem=send, recv_sem=recv, device_id=device, device_id_type=MESH
    )


class Gather:
    def __init__(self, place, weights, chunks, send, recv):
        self.p, self.w, self.chunks, self.ss, self.rs = place, weights, chunks, send, recv
        self.sent = [[] for _ in chunks]
        self.t, self.have = 0, set()

    def chunks_of(self, k):
        return [q for q, v in enumerate(self.chunks) if v[0] == k]

    def begin(self):
        self.along_z(0)

    def tick(self):
        t, n = self.t, len(self.chunks)
        if t >= n + 2:
            return
        if t == 0:
            for q in range(1, AHEAD):
                self.along_z(q)
        if t < n:
            self.along_xy(t)
        if t + AHEAD < n:
            self.along_z(t + AHEAD)
        if 0 <= t - 1 < n:
            self.across(t - 1)
        if 0 <= t - 2 < n:
            self.last(t - 2)
        self.t += 1

    def need(self, q):
        while self.t <= q + 2:
            self.tick()
        if q not in self.have:
            self.have.add(q)
            self.ready(q)

    def part(self, q, half, z, xy):
        k, start, width, _ = self.chunks[q]
        return self.w[k].at[half, z, xy, :, pl.ds(start, width)]

    def copy(self, q, j, ref, device):
        return remote(ref, ref, self.ss.at[q, j], self.rs.at[q, j], device)

    def send(self, q, j, ref, device):
        cp = self.copy(q, j, ref, device)
        cp.start()
        self.sent[q].append(cp)

    def wait(self, q, j, ref):
        self.copy(q, j, ref, self.p.to_c).wait_recv()

    def along_z(self, q):
        p = self.p
        for j, device in enumerate(p.to_z):
            self.send(q, j, self.part(q, p.c, p.z, p.own), device)

    def along_xy(self, q):
        p, allz = self.p, slice(None)
        for j, z in enumerate(p.z_from):
            self.wait(q, j, self.part(q, p.c, z, p.own))
        mine = self.part(q, p.c, allz, p.own)
        self.send(q, 3, mine, p.to_x)
        self.send(q, 4, mine, p.to_y)
        self.send(q, 7, mine, p.to_c)

    def across(self, q):
        p, allz, cut = self.p, slice(None), self.chunks[q][3]
        from_x, from_y = self.part(q, p.c, allz, p.at_x), self.part(q, p.c, allz, p.at_y)
        self.wait(q, 3, from_x)
        self.send(q, 5, self.part(q, p.c, pl.ds(0, cut), p.at_x), p.to_y)
        self.send(q, 8, from_x, p.to_c)
        self.wait(q, 4, from_y)
        self.send(q, 6, self.part(q, p.c, pl.ds(cut, p.nz - cut), p.at_y), p.to_x)
        self.send(q, 9, from_y, p.to_c)

    def last(self, q):
        p, cut = self.p, self.chunks[q][3]
        for j, z in ((5, pl.ds(0, cut)), (6, pl.ds(cut, p.nz - cut))):
            ref = self.part(q, p.c, z, p.at_d)
            self.wait(q, j, ref)
            self.send(q, j + 5, ref, p.to_c)

    def ready(self, q):
        p, allz, cut = self.p, slice(None), self.chunks[q][3]
        for j, z, xy in (
            (7, allz, p.own),
            (8, allz, p.at_x),
            (9, allz, p.at_y),
            (10, pl.ds(0, cut), p.at_d),
            (11, pl.ds(cut, p.nz - cut), p.at_d),
        ):
            self.wait(q, j, self.part(q, p.o, z, xy))

    def settle(self, q):
        for cp in self.sent[q]:
            cp.wait_send()
        self.sent[q] = []


def half_of(w, h, start=None, width=None):
    v = w[h] if start is None else w[h, :, :, :, pl.ds(start, width)]
    return v.reshape(-1, v.shape[-1])


def lane_masks():
    lane = lax.broadcasted_iota(jnp.int32, (1, LANES), 1)
    low = lane < HEAD
    return low, jnp.where(low, 1.0, 0.0).astype(bf16), jnp.where(low, 0.0, 1.0).astype(bf16)


def stacked(v, low, high):
    return jnp.concatenate([v * low, v * high], 0)


def swap_halves(v):
    lane = lax.broadcasted_iota(jnp.int32, v.shape, 1)
    first = lax.rem(lane, HEAD) < HEAD // 2
    return jnp.where(first, pltpu.roll(v, LANES - HEAD // 2, 1), pltpu.roll(v, HEAD // 2, 1))


def rotate(v, cosine, signed):
    return v * cosine + swap_halves(v) * signed


def forward(p, r, g, swap, kv_sem, pairs):
    n = len(g.chunks)
    c, z = p.c, p.z
    w = r.w

    vectors = r.vectors[...].astype(f32)
    start = 0
    for k, ref in enumerate((r.w_qkv, r.w_cross_kv, r.w_out, r.w_cross_q, r.w_cross_out, r.w_up)):
        rows = ref[...].astype(f32)
        size = rows.shape[1] // 2
        for h in range(2):
            parts = 3 if k == 0 else 1
            part = size // parts
            for i in range(parts):
                source = i * 2 * part + h * part
                r.pack[h, :, start + i * part : start + (i + 1) * part] = rows[:, source : source + part]
            if k == 0:
                r.pack[h, :, start + size : start + size + LANES] = jnp.zeros((rows.shape[0], LANES), f32)
                r.pack[h, :, start + size : start + size + vectors.shape[1]] = vectors
        start += w[k].shape[-1]
    p.meet()
    first = remote(r.pack.at[p.o], r.beside, r.pair_sem.at[0], r.pair_sem.at[1], p.to_c)
    first.start()
    down_rows, down_half = r.w_down.shape[0], w[6].shape[-1]
    down_at = pl.ds(pl.multiple_of(c * down_rows, 16), down_rows)
    down = remote(
        r.w_down.at[:, pl.ds(pl.multiple_of(p.o * down_half, LANES), down_half)],
        w[6].at[p.o, z, p.own, down_at],
        r.pair_sem.at[2],
        r.pair_sem.at[3],
        p.to_c,
    )
    down.start()
    tokens_y = remote(r.tokens, r.branch, r.pair_sem.at[4], r.pair_sem.at[5], p.to_y)
    tokens_y.start()
    ropes = [pltpu.make_async_copy(r.rope_table.at[s], r.rope.at[i], r.rope_sem.at[i]) for i, s in enumerate((p.s, p.s_y))]
    for rope in ropes:
        rope.start()
    w[6][c, z, p.own, down_at] = r.w_down[:, pl.ds(pl.multiple_of(c * down_half, LANES), down_half)]
    first.wait_recv()
    start = 0
    for k in range(6):
        width = w[k].shape[-1]
        mine, other = r.pack[c, :, start : start + width], r.beside[:, start : start + width]
        top, low = jnp.where(c == 0, mine, other), jnp.where(c == 0, other, mine)
        w[k][c, z, p.own] = jnp.concatenate([top, low], 0).astype(bf16)
        start += width
        if k == 0:
            g.begin()
    down.wait_recv()
    g.tick()
    swap.send("cot", r.cotangent.at[:, pl.ds(pl.multiple_of(p.o * down_half, LANES), down_half)], r.by_cot)
    swap.send("nb", r.neighbours, r.by_neighbours)
    for rope in ropes:
        rope.wait()
    tokens = r.tokens[...].astype(f32)
    quarter, width = tokens.shape
    unit, _ = norm_parts(tokens)
    g.tick()
    tokens_y.wait_recv()
    unit_y, _ = norm_parts(r.branch[...].astype(f32))
    g.need(0)
    part = width // 2
    r.vec[...] = jnp.transpose(half_of(w[0], 0, 3 * part, LANES).astype(f32))[:8]

    def affine(v, i):
        return (v * r.vec[i : i + 1] + r.vec[3 + i : 4 + i]).astype(bf16)

    r.n1[:quarter] = affine(unit, 0)
    r.n1[quarter:] = affine(unit_y, 0)
    swap.send("n1", r.n1, r.by_n1)
    for h in range(2):
        value = dot(r.n1[...], half_of(w[0], h, 2 * part, part)).astype(bf16)
        cols = slice(width + h * part, width + (h + 1) * part)
        r.kv[p.s, :, cols] = value[:quarter]
        r.kv[p.s_y, :, cols] = value[quarter:]

    def turned(v, i, sign=1):
        cosine, signed = r.rope[i, :, :LANES], r.rope[i, :, LANES:]
        return jnp.concatenate(
            [rotate(v[:, b : b + LANES], cosine, sign * signed) for b in range(0, v.shape[1], LANES)], 1
        )

    g.need(1)
    for h in range(2):
        key = dot(r.n1[...], half_of(w[0], h, part, part))
        cols = slice(h * part, (h + 1) * part)
        r.kv[p.s, :, cols] = turned(key[:quarter], 0).astype(bf16)
        r.kv[p.s_y, :, cols] = turned(key[quarter:], 1).astype(bf16)
    kv_sent = [
        remote(r.kv.at[s], r.kv.at[s], kv_sem.at[0, i], kv_sem.at[1, i], p.to_c) for i, s in enumerate((p.s, p.s_y))
    ]
    for cp in kv_sent:
        cp.start()
    g.need(2)
    for h in range(2):
        query = dot(r.n1[:quarter], half_of(w[0], h, 0, part))
        r.q[:, h * part : (h + 1) * part] = turned(query, 0).astype(bf16)
    g.need(3)
    g.need(4)

    def pool_rows(i, carry):
        rows = r.neighbours[pl.ds(i * 2, 2)].reshape(-1, r.neighbours.shape[2])
        for h in range(2):
            width = w[1].shape[-1]
            r.pool[pl.ds(i * 2, 2), :, h * width : (h + 1) * width] = (
                dot(rows, half_of(w[1], h)).astype(bf16).reshape(2, -1, width)
            )
        return carry

    lax.fori_loop(0, 2, pool_rows, 0)
    g.tick()
    lax.fori_loop(2, r.neighbours.shape[0] // 2, pool_rows, 0)
    for i, s in enumerate((p.s_c, p.s_d)):
        remote(r.kv.at[s], r.kv.at[s], kv_sem.at[0, i], kv_sem.at[1, i], p.to_c).wait_recv()

    low_lane, low, high = lane_masks()
    place = lax.rem(lax.broadcasted_iota(jnp.int32, (1, 2 * quarter), 1), quarter) + p.s * quarter
    limit = jnp.maximum(place, r.prefix[0] - 1)

    def self_pair(i, carry):
        cols = pl.ds(pl.multiple_of(i * LANES, LANES), LANES)
        vcols = pl.ds(pl.multiple_of(i * LANES + w[1].shape[-1], LANES), LANES)
        queries = stacked(r.q[:, cols], low, high) * bf16(HEAD**-0.5)
        keys = r.kv[:, :, cols].reshape(-1, LANES)
        values = r.kv[:, :, vcols].reshape(-1, LANES)
        scores = dot(keys, queries, NT)
        key_place = lax.broadcasted_iota(jnp.int32, scores.shape, 0)
        scores = jnp.where(key_place <= limit, scores, masked)
        top = jnp.max(scores, 0, keepdims=True)
        e = jnp.exp(scores - top)
        total = jnp.sum(e, 0, keepdims=True)
        weights = (e * (1.0 / total)).astype(bf16)
        r.lse[i] = top + jnp.log(total)
        mixed = dot(weights, values, TN)
        r.att[:, cols] = jnp.where(low_lane, mixed[:quarter], mixed[quarter:]).astype(bf16)
        return carry

    for i in range(0, pairs, 2):
        lax.fori_loop(i, i + 2, self_pair, 0)
        g.tick()
    g.need(5)

    def project(v, k):
        return jnp.concatenate([dot(v, half_of(w[k], h)) for h in range(2)], 1)

    swap.send("att", r.att, r.by_att)
    first_sum = tokens + project(r.att[...], 2)
    r.first[...] = first_sum
    r.n2[...] = affine(norm_parts(first_sum)[0], 1)
    swap.send("n2", r.n2, r.by_n2)
    g.need(6)
    r.cq[...] = project(r.n2[...], 3).astype(bf16)
    slots = r.neighbours.shape[0]
    span = quarter // (slots // 2)

    def cross_pair(i, carry):
        cols = pl.ds(pl.multiple_of(i * LANES, LANES), LANES)
        vcols = pl.ds(pl.multiple_of(i * LANES + w[1].shape[-1], LANES), LANES)
        for b in range(slots // 2):
            two = [lax.rem(r.index[2 * b + j], slots) for j in range(2)]
            rows = slice(b * span, (b + 1) * span)
            queries = stacked(r.cq[rows, cols], low, high) * bf16(HEAD**-0.5)
            keys = jnp.concatenate([r.pool[t, :, cols] for t in two], 0)
            values = jnp.concatenate([r.pool[t, :, vcols] for t in two], 0)
            scores = dot(keys, queries, NT)
            top = jnp.max(scores, 0, keepdims=True)
            e = jnp.exp(scores - top)
            total = jnp.sum(e, 0, keepdims=True)
            weights = (e * (1.0 / total)).astype(bf16)
            r.lse_cross[i, b : b + 1] = top + jnp.log(total)
            mixed = dot(weights, values, TN)
            r.cm[rows, cols] = jnp.where(low_lane, mixed[:span], mixed[span:]).astype(bf16)
        return carry

    lax.fori_loop(0, pairs // 2, cross_pair, 0)
    g.tick()
    lax.fori_loop(pairs // 2, pairs, cross_pair, 0)
    g.need(7)
    swap.send("cm", r.cm, r.by_cm)
    second_sum = r.first[...] + project(r.cm[...], 4)
    r.second[...] = second_sum
    r.n3[...] = affine(norm_parts(second_sum)[0], 2)
    swap.send("n3", r.n3, r.by_n3)
    hidden_half = w[5].shape[-1]

    def up_tile(start, size):
        def body(h, carry):
            hidden = dot(r.n3[...], half_of(w[5], h, start, size))
            cdf = 0.5 * (1.0 + lax.erf(hidden * (0.5**0.5)))
            density = jnp.exp(-0.5 * hidden * hidden) * ((2 * math.pi) ** -0.5)
            cols = pl.ds(pl.multiple_of(h * hidden_half + start, LANES), size)
            r.act[:, cols] = (hidden * cdf).astype(bf16)
            r.slope[:, cols] = (cdf + hidden * density).astype(bf16)
            return carry

        lax.fori_loop(0, 2, body, 0)

    for q, (k, start, size, _) in enumerate(g.chunks):
        if k == 5:
            g.need(q)
            up_tile(start, size)
    swap.send("act", r.act, r.by_act)

    def down_part(q):
        _, start, size, _ = g.chunks[q]
        for h in range(2):
            cols = slice(h * down_half + start, h * down_half + start + size)
            r.out[:, cols] = (r.second[:, cols] + dot(r.act[...], half_of(w[6], h, start, size))).astype(bf16)

    return down_part, turned, (first, down, tokens_y, *kv_sent)


LAG = 3


class Reduce:
    def __init__(self, place, r, chunks, send, recv):
        self.p, self.r, self.w, self.chunks, self.ss, self.rs = place, r, r.w, chunks, send, recv
        self.sent, self.open, self.under_way, self.next = [], set(), {}, 0
        self.starts = [sum(v.shape[-1] for v in r.w[:k]) for k in range(7)]

    def free(self, k):
        p = self.p
        for device in (p.to_x, p.to_y, *p.to_z):
            pl.semaphore_signal(self.r.credit.at[k], inc=1, device_id=device, device_id_type=MESH)

    def array(self, k, half):
        return (self.r.down_sum, 0) if k == 6 and half is self.p.c else (self.w[k], half)

    def at(self, q, half, z, xy):
        k, start, width, _ = self.chunks[q]
        ref, lead = self.array(k, half)
        return ref.at[lead, z, xy, :, pl.ds(start, width)]

    def load(self, q, half, z, xy):
        k, start, width, _ = self.chunks[q]
        ref, lead = self.array(k, half)
        return ref[lead, z, xy, :, start : start + width].astype(f32)

    def save(self, q, half, z, xy, v):
        k, start, width, _ = self.chunks[q]
        ref, lead = self.array(k, half)
        ref[lead, z, xy, :, start : start + width] = v.astype(bf16)

    def copy(self, q, j, src, dst, device):
        cp = remote(src, dst, self.ss.at[q, j], self.rs.at[q, j], device)
        cp.start()
        self.sent.append(cp)

    def wait(self, q, j, ref):
        remote(ref, ref, self.ss.at[q, j], self.rs.at[q, j], self.p.to_c).wait_recv()

    def diagonal(self, q):
        p, (k, _, _, cut) = self.p, self.chunks[q]
        if k not in self.open:
            pl.semaphore_wait(self.r.credit.at[k], 1 + p.nz)
            self.open.add(k)
        for j, z, device in ((0, pl.ds(0, cut), p.to_y), (1, pl.ds(cut, p.nz - cut), p.to_x)):
            self.copy(q, j, self.at(q, p.c, z, p.at_d), self.at(q, p.o, z, 0), device)

    def across(self, q):
        p, cut, allz = self.p, self.chunks[q][3], slice(None)
        for j, zs, to in ((0, range(cut), p.at_x), (1, range(cut, p.nz), p.at_y)):
            self.wait(q, j, self.at(q, p.o, pl.ds(zs[0], len(zs)), 0))
            for z in zs:
                self.save(q, p.c, z, to, self.load(q, p.c, z, to) + self.load(q, p.o, z, 0))
        self.copy(q, 2, self.at(q, p.c, allz, p.at_x), self.at(q, p.o, allz, 1), p.to_x)
        self.copy(q, 3, self.at(q, p.c, allz, p.at_y), self.at(q, p.o, allz, 2), p.to_y)

    def along_z(self, q):
        p, allz = self.p, slice(None)
        self.wait(q, 2, self.at(q, p.o, allz, 1))
        self.wait(q, 3, self.at(q, p.o, allz, 2))
        for z in range(p.nz):
            total = self.load(q, p.c, z, p.own) + self.load(q, p.o, z, 1) + self.load(q, p.o, z, 2)
            self.save(q, p.c, z, p.own, total)
        for j, device in enumerate(p.to_z):
            self.copy(q, 4 + j, self.at(q, p.c, p.z_of[j], p.own), self.at(q, p.o, j, 3), device)

    def last(self, q):
        p, r, (k, start, width, _) = self.p, self.r, self.chunks[q]
        total = self.load(q, p.c, p.z, p.own)
        for j in range(p.nz - 1):
            self.wait(q, 4 + j, self.at(q, p.o, j, 3))
            total = total + self.load(q, p.o, j, 3)
        cols = slice(start, start + width)
        rows = total.shape[0] // 2
        r.sums[k][p.c, :, cols] = jnp.where(p.c == 0, total[:rows], total[rows:])
        if k == 6:
            mine = r.down_beside.at[:, cols]
        else:
            mine = r.beside.at[:, self.starts[k] + start : self.starts[k] + start + width]
        mine[...] = jnp.where(p.c == 0, total[rows:], total[:rows])
        self.copy(q, 7, mine, r.sums[k].at[p.c, :, cols], p.to_c)

    def finish(self, q):
        p, (k, start, width, _) = self.p, self.chunks[q]
        self.wait(q, 7, self.r.sums[k].at[p.o, :, pl.ds(start, width)])

    def push(self, q=None, lag=LAG):
        for other in list(self.under_way):
            stage, age = self.under_way[other]
            if age + 1 < lag:
                self.under_way[other] = stage, age + 1
                continue
            (self.across, self.along_z, self.last)[stage](other)
            self.under_way[other] = stage + 1, 0
            if stage == 2:
                del self.under_way[other]
        if q is not None:
            self.diagonal(q)
            self.under_way[q] = 0, 0

    def chunks_of(self, k):
        return [q for q, v in enumerate(self.chunks) if v[0] == k]

    def drain(self):
        while self.under_way:
            self.push(None, 1)
        for q in range(len(self.chunks)):
            self.finish(q)


class Swap:
    def __init__(self, place, sems):
        self.p, self.sems, self.n, self.sent, self.landed = place, sems, 0, [], {}

    def send(self, name, src, dst):
        cp = remote(src, dst, self.sems.at[0, self.n], self.sems.at[1, self.n], self.p.to_c)
        cp.start()
        self.sent.append(cp)
        self.landed[name] = cp
        self.n += 1

    def wait(self, name):
        self.landed.pop(name).wait_recv()


def norm_back_at(grad, v, gain):
    unit, inv = norm_parts(v)
    scaled = grad * gain
    back = inv * (
        scaled - jnp.mean(scaled, -1, keepdims=True) - unit * jnp.mean(scaled * unit, -1, keepdims=True)
    )
    return back, jnp.sum(grad * unit, 0, keepdims=True), jnp.sum(grad, 0, keepdims=True)


def backward(p, r, g, swap, red, kv_sem, pairs, down_part, turned):
    w, c, o = r.w, p.c, p.o
    quarter, width = r.tokens.shape
    hidden_half, pool_half = w[5].shape[-1], w[1].shape[-1]
    slots, rows_n = r.neighbours.shape[:2]
    low_lane, low, high = lane_masks()
    r.vec_sum[...] = jnp.zeros_like(r.vec_sum)

    def half(ref, h, size):
        return ref.at[:, pl.ds(pl.multiple_of(h * size, LANES), size)]

    def input_grad(ref, k, size):
        return sum(dot(ref[:, h * size : (h + 1) * size], half_of(w[k], h, 0, size), NT) for h in range(2))

    def weight_grad(k, left, left_beside, right, right_beside, size, tile=384, chunks=None, push=True):
        into, lead = red.array(k, c)
        rows = into.shape[3]
        per = tile // (4 * rows)
        for q in red.chunks_of(k) if chunks is None else chunks:
            _, start, n, _ = red.chunks[q]
            n = min(n, size - start)

            def body(i, carry, start=start, n=n):
                cols = pl.ds(pl.multiple_of(i * tile, LANES), tile)
                part = dot(left(cols), right(start, n), TN) + dot(left_beside(cols), right_beside(start, n), TN)
                into[lead, pl.ds(i * per, per), :, :, start : start + n] = part.astype(bf16).reshape(per, 4, rows, n)
                return carry

            lax.fori_loop(0, p.nz // per, body, 0)
            if push:
                red.push(q)

    def plain_grad(k, left, left_beside, right, right_beside, size, tile=384, chunks=None, push=True):
        weight_grad(
            k,
            lambda cols: left[:, cols],
            lambda cols: left_beside[:, cols],
            lambda start, n: right[:, pl.ds(pl.multiple_of(c * size + start, LANES), n)],
            lambda start, n: right_beside[:, start : start + n],
            size,
            tile,
            chunks,
            push,
        )

    def gain(i):
        return r.vec[i : i + 1]

    def keep_vec(i, gain_sum, shift_sum):
        r.vec_sum[i : i + 1] = gain_sum
        r.vec_sum[3 + i : 4 + i] = shift_sum

    for q in g.chunks_of(6):
        g.tick()
    for name in ("cot", "act"):
        swap.wait(name)
    plain_grad(6, r.act, r.by_act, r.cotangent, r.by_cot, w[6].shape[-1], 4 * w[6].shape[3], push=False)
    for q in g.chunks_of(6):
        g.need(q)
    down_half = w[6].shape[-1]

    def act_tile(z, carry):
        rows = 4 * w[6].shape[3]
        cols = pl.ds(pl.multiple_of(z * rows, LANES), rows)
        act_grad = sum(
            dot(r.cotangent[:, h * down_half : (h + 1) * down_half], w[6][h, z].reshape(rows, down_half), NT)
            for h in range(2)
        )
        r.slope[:, cols] = (act_grad * r.slope[:, cols].astype(f32)).astype(bf16)
        return carry

    lax.fori_loop(0, p.nz, act_tile, 0)
    gh = r.slope
    swap.send("gh", half(gh, o, hidden_half), r.by_hidden_grad)
    for q in g.chunks_of(6):
        down_part(q)
        g.settle(q)
    red.free(6)
    for q in red.chunks_of(6):
        red.push(q)
    grad_three = input_grad(gh, 5, hidden_half)
    red.free(5)
    red.push()
    for q in g.chunks_of(5):
        g.settle(q)
    back, dg, db = norm_back_at(grad_three, r.second[...], gain(2))
    keep_vec(2, dg, db)
    grad_second = r.cotangent[...].astype(f32) + back
    r.second[...] = grad_second
    r.branch[...] = grad_second.astype(bf16)
    swap.send("gcb", half(r.branch, o, width // 2), r.by_branch)
    for name in ("gh", "n3"):
        swap.wait(name)
    plain_grad(5, r.n3, r.by_n3, gh, r.by_hidden_grad, hidden_half)
    r.mixed_grad[...] = input_grad(r.branch, 4, width // 2).astype(bf16)
    red.free(4)
    for q in g.chunks_of(4):
        g.settle(q)

    span = quarter // (slots // 2)

    def cross_pair(i, carry):
        cols = pl.ds(pl.multiple_of(i * LANES, LANES), LANES)
        vcols = pl.ds(pl.multiple_of(i * LANES + pool_half, LANES), LANES)
        for b in range(slots // 2):
            two = [lax.rem(r.index[2 * b + j], slots) for j in range(2)]
            rows = slice(b * span, (b + 1) * span)
            queries = stacked(r.cq[rows, cols], low, high) * bf16(HEAD**-0.5)
            grads = stacked(r.mixed_grad[rows, cols], low, high)
            keys = jnp.concatenate([r.pool[t, :, cols] for t in two], 0)
            values = jnp.concatenate([r.pool[t, :, vcols] for t in two], 0)
            probs = jnp.exp(dot(keys, queries, NT) - r.lse_cross[i, b : b + 1])
            grad_probs = dot(values, grads, NT)
            score_grad = (probs * (grad_probs - jnp.sum(probs * grad_probs, 0, keepdims=True))).astype(bf16)
            r.gkv[b, :, cols] = dot(score_grad, queries).astype(bf16)
            r.gkv[b, :, vcols] = dot(probs.astype(bf16), grads).astype(bf16)
            gq = dot(score_grad, keys, TN) * HEAD**-0.5
            r.cq_grad[rows, cols] = jnp.where(low_lane, gq[:span], gq[span:]).astype(bf16)
        return carry

    for i in range(0, pairs, 2):
        lax.fori_loop(i, i + 2, cross_pair, 0)
        red.push()
    swap.send("gcq", half(r.cq_grad, o, width // 2), r.by_cq_grad)
    grad_two = input_grad(r.cq_grad, 3, width // 2)
    red.free(3)
    for q in g.chunks_of(3):
        g.settle(q)
    back, dg, db = norm_back_at(grad_two, r.first[...], gain(1))
    keep_vec(1, dg, db)
    grad_first = r.second[...] + back
    r.first[...] = grad_first
    r.self_branch[...] = grad_first.astype(bf16)
    swap.send("gsb", half(r.self_branch, o, width // 2), r.by_self_branch)
    r.mixed_grad[...] = input_grad(r.self_branch, 2, width // 2).astype(bf16)
    red.free(2)
    for q in g.chunks_of(2):
        g.settle(q)
    swap.wait("gcb")
    swap.wait("cm")
    plain_grad(4, r.cm, r.by_cm, r.branch, r.by_branch, width // 2)
    for s in range(slots):
        j = 0
        for k in range(slots):
            j = jnp.where(lax.rem(r.index[k], slots) == s, k, j)
        b, odd = lax.div(j, 2), lax.rem(j, 2)
        r.pool[s] = jnp.where(odd == 0, r.gkv[b, :rows_n], r.gkv[b, rows_n:])
    swap.send("gp", r.pool.at[:, :, pl.ds(pl.multiple_of(o * pool_half, LANES), pool_half)], r.by_pool_grad)

    cosine, signed = r.rope[0, :, :LANES], r.rope[0, :, LANES:]
    place = lax.rem(lax.broadcasted_iota(jnp.int32, (1, 2 * quarter), 1), quarter) + p.s * quarter
    limit = jnp.maximum(place, r.prefix[0] - 1)
    group, groups = width, 2
    each = pairs // groups

    def self_pair(i, carry):
        cols = pl.ds(pl.multiple_of(i * LANES, LANES), LANES)
        vcols = pl.ds(pl.multiple_of(i * LANES + pool_half, LANES), LANES)
        start = lax.div(i, each) * group + lax.rem(i, each) * LANES
        queries = stacked(r.q[:, cols], low, high) * bf16(HEAD**-0.5)
        grads = stacked(r.mixed_grad[:, cols], low, high)
        keys = r.kv[:, :, cols].reshape(-1, LANES)
        values = r.kv[:, :, vcols].reshape(-1, LANES)
        scores = dot(keys, queries, NT)
        key_place = lax.broadcasted_iota(jnp.int32, scores.shape, 0)
        probs = jnp.exp(jnp.where(key_place <= limit, scores, masked) - r.lse[i])
        grad_probs = dot(values, grads, NT)
        score_grad = (probs * (grad_probs - jnp.sum(probs * grad_probs, 0, keepdims=True))).astype(bf16)
        for offset, part in ((0, dot(score_grad, queries)), (group // 2, dot(probs.astype(bf16), grads))):
            there = pl.ds(pl.multiple_of(start + offset, LANES), LANES)
            r.gkv[:, :, there] = part.astype(bf16).reshape(4, quarter, LANES)
        gq = dot(score_grad, keys, TN) * HEAD**-0.5
        gq = jnp.where(low_lane, gq[:quarter], gq[quarter:])
        r.q_grad[:, cols] = rotate(gq, cosine, -signed).astype(bf16)
        return carry

    for i in range(groups):
        for j in range(each):
            lax.fori_loop(i * each + j, i * each + j + 1, self_pair, 0)
            red.push()
        cols = pl.ds(i * group, group)
        swap.send(f"far{i}", r.gkv.at[p.s_d, :, cols], r.by_act.at[:, cols])
        swap.send(f"near{i}", r.gkv.at[p.s_c, :, cols], r.by_act.at[:, pl.ds((groups + i) * group, group)])
    swap.send("gq", half(r.q_grad, o, width // 2), r.by_q_grad)
    swap.wait("gcq")
    swap.wait("n2")
    plain_grad(3, r.n2, r.by_n2, r.cq_grad, r.by_cq_grad, width // 2)
    for i in range(groups):
        cols = slice(i * group, (i + 1) * group)
        for j, (name, s, other) in enumerate((("near", p.s, groups + i), ("far", p.s_y, i))):
            swap.wait(f"{name}{i}")
            total = r.gkv[s, :, cols].astype(f32) + r.by_act[:, other * group : (other + 1) * group].astype(f32)
            total = jnp.concatenate([turned(total[:, : group // 2], j, -1), total[:, group // 2 :]], 1)
            r.gkv[s, :, cols] = total.astype(bf16)
    half_kv = pl.ds(pl.multiple_of(o * group, LANES), group)
    for j, (name, s) in enumerate((("gkv", p.s), ("gkvy", p.s_y))):
        swap.send(name, r.gkv.at[s, :, half_kv], r.by_kv_grad.at[pl.ds(j * quarter, quarter)])
    red.push()
    part = width // 2

    def kv_grads(cols):
        return jnp.concatenate([r.gkv[s, :, cols] for s in (p.s, p.s_y)], 0)

    grad_one = sum(dot(kv_grads(slice(h * group, (h + 1) * group)), half_of(w[0], h, part, group), NT) for h in range(2))
    r.mixed_grad[...] = grad_one[quarter:].astype(bf16)
    to_y = remote(r.mixed_grad, r.one_y, kv_sem.at[0], kv_sem.at[1], p.to_y)
    to_y.start()
    r.second[...] = grad_one[:quarter] + sum(
        dot(r.q_grad[:, h * part : (h + 1) * part], half_of(w[0], h, 0, part), NT) for h in range(2)
    )
    red.free(0)
    for q in g.chunks_of(0):
        g.settle(q)
    for name in ("gq", "n1", "gkv", "gkvy"):
        swap.wait(name)
    first_chunk, *kv_chunks, vec_chunk = red.chunks_of(0)
    plain_grad(0, r.n1.at[:quarter], r.by_n1.at[:quarter], r.q_grad, r.by_q_grad, part, chunks=[first_chunk])
    weight_grad(
        0,
        lambda cols: r.n1[:, cols],
        lambda cols: r.by_n1[:, cols],
        lambda start, n: kv_grads(pl.ds(pl.multiple_of(c * group + start - part, LANES), n)),
        lambda start, n: r.by_kv_grad[:, start - part : start - part + n],
        3 * part,
        chunks=kv_chunks,
    )
    swap.wait("gsb")
    swap.wait("att")
    plain_grad(2, r.att, r.by_att, r.self_branch, r.by_self_branch, width // 2)

    out = [None, None]
    for s in range(slots):
        rows = r.pool[s]
        slot_grad = sum(
            dot(rows[:, h * pool_half : (h + 1) * pool_half], half_of(w[1], h), NT) for h in range(2)
        )
        if out[s % 2] is not None:
            out[s % 2].wait()
        stage = r.stage.at[s % 2]
        stage[...] = slot_grad
        out[s % 2] = pltpu.make_async_copy(stage, r.neighbours_grad.at[s], r.out_sem.at[s % 2])
        out[s % 2].start()
        if s == slots // 2:
            red.push()
    red.free(1)
    for q in g.chunks_of(1):
        g.settle(q)
    swap.wait("gp")
    swap.wait("nb")
    size = slots * rows_n
    weight_grad(
        1,
        lambda cols: r.neighbours[:, :, cols].reshape(size, -1),
        lambda cols: r.by_neighbours[:, :, cols].reshape(size, -1),
        lambda start, n: r.pool[:, :, pl.ds(pl.multiple_of(c * pool_half + start, LANES), n)].reshape(size, -1),
        lambda start, n: r.by_pool_grad[:, :, start : start + n].reshape(size, -1),
        pool_half,
    )
    to_y.wait_recv()
    grad_one = r.second[...] + r.one_y[...].astype(f32)
    back, dg, db = norm_back_at(grad_one, r.tokens[...].astype(f32), gain(0))
    keep_vec(0, dg, db)
    r.tokens_grad[...] = r.first[...] + back
    swap.send("vec", r.vec_sum, r.by_vec)
    swap.wait("vec")
    vec = jnp.concatenate([r.vec_sum[...] + r.by_vec[...], jnp.zeros((LANES - 8, width), f32)], 0)
    w[0][c, :, :, :, 3 * part :] = jnp.transpose(vec).astype(bf16).reshape(p.nz, 4, -1, LANES)
    red.push(vec_chunk)
    red.drain()
    for cp in (*red.sent, *swap.sent, to_y):
        cp.wait_send()
    for cp in out:
        cp.wait()


def rope_table(length):
    half = HEAD // 2
    freq = (10000.0 ** (-np.arange(half, dtype=np.float32) / half)).astype(np.float32)
    angles = np.arange(length, dtype=np.float32)[:, None] * freq[None, :]
    cosine, sine = np.cos(angles), np.sin(angles)
    table = np.concatenate([cosine] * 4 + [-sine, sine] * 2, 1)
    return table.astype(np.float32).reshape(4, -1, 2 * LANES)


def deliver_kernel(*refs):
    n = 3
    plain, sums = refs[:n], refs[n : n + 7]
    outs, sem = refs[n + 7 : -1], refs[-1]
    copies = [(src, dst) for src, dst in zip(plain, outs[:n])]
    for k, dst in zip(range(7), outs[n : n + 7]):
        parts = 3 if k == 0 else 1
        part = dst.shape[1] // (2 * parts)
        for h in range(2):
            for i in range(parts):
                source, there = i * part, i * 2 * part + h * part
                copies.append((sums[k].at[h, :, source : source + part], dst.at[:, there : there + part]))
    copies = [pltpu.make_async_copy(src, dst, sem.at[i]) for i, (src, dst) in enumerate(copies)]
    for cp in copies:
        cp.start()
    half = outs[n].shape[1] // 2
    turned = jnp.transpose(
        jnp.concatenate([sums[0][0, :, half:], jnp.zeros((LANES - sums[0].shape[1], LANES), f32)], 0)
    )
    outs[n + 7][...] = turned[:8, : outs[n + 7].shape[1]]
    for cp in copies:
        cp.wait()


def deliver(out, tokens_grad, neighbours_grad, summed):
    rows = summed[0].shape[1]
    widths = [2 * v.shape[2] for v in summed]
    widths[0] -= 2 * LANES
    shapes = [out, tokens_grad, neighbours_grad] + [
        jax.ShapeDtypeStruct((v.shape[1], n), f32) for v, n in zip(summed, widths)
    ]
    vmem, anywhere = pl.BlockSpec(memory_space=pltpu.VMEM), pl.BlockSpec(memory_space=pl.ANY)
    out, tokens_grad, neighbours_grad, *grads, vectors = pl.pallas_call(
        deliver_kernel,
        out_shape=[jax.ShapeDtypeStruct(v.shape, v.dtype) for v in shapes] + [jax.ShapeDtypeStruct((8, rows), f32)],
        in_specs=[vmem] * 10,
        out_specs=[anywhere] * 10 + [vmem],
        scratch_shapes=[pltpu.SemaphoreType.DMA((21,))],
        compiler_params=pltpu.CompilerParams(vmem_limit_bytes=32 * 2**20),
        name="deliver",
    )(out, tokens_grad, neighbours_grad, *summed)
    return (
        out[None],
        tokens_grad[None],
        neighbours_grad[None],
        grads[0],
        grads[2],
        grads[3],
        grads[1],
        grads[4],
        grads[5],
        grads[6],
        *(vectors[i] for i in (0, 3, 1, 4, 2, 5)),
    )


class Refs:
    def take(self, names, refs):
        for name, ref in zip(names, refs, strict=True):
            setattr(self, name, ref)


NAMES_IN = (
    "w_qkv",
    "w_cross_kv",
    "w_out",
    "w_cross_q",
    "w_cross_out",
    "w_up",
    "w_down",
    "vectors",
    "tokens",
    "cotangent",
    "prefix",
    "neighbours",
    "index",
    "rope_table",
)
NAMES_OUT = ("out", "tokens_grad", "neighbours_grad")
GATHER = (
    (0, 768, 512, 2),
    (0, 384, 384, 2),
    (0, 0, 384, 2),
    (1, 0, 384, 2),
    (1, 384, 384, 2),
    (2, 0, 384, 2),
    (3, 0, 384, 2),
    (4, 0, 384, 2),
    (5, 0, 384, 2),
    (5, 384, 384, 2),
    (5, 768, 384, 2),
    (5, 1152, 384, 2),
    (6, 0, 128, 2),
    (6, 128, 128, 2),
    (6, 256, 128, 2),
)
REDUCE = (
    (6, 0, 256, 2),
    (6, 256, 128, 2),
    (5, 0, 512, 2),
    (5, 512, 512, 2),
    (5, 1024, 512, 2),
    (4, 0, 384, 2),
    (3, 0, 384, 2),
    (2, 0, 384, 2),
    (1, 0, 384, 2),
    (1, 384, 384, 2),
    (0, 0, 384, 2),
    (0, 384, 384, 2),
    (0, 768, 384, 2),
    (0, 1152, 128, 2),
)


def memory(nz, quarter, width, hidden, slots, rows_n, rows):
    halves = (3 * width // 2 + LANES, width, width // 2, width // 2, width // 2, hidden // 2)
    weights = [((2, nz, 4, 2 * rows, h), bf16) for h in halves]
    weights.append(((2, nz, 4, hidden // (4 * nz), width // 2), bf16))
    sums = [((2, rows, h), f32) for h in halves]
    sums.append(((2, hidden // (8 * nz), width // 2), f32))
    tok, half_tok = ((quarter, width), bf16), ((quarter, width // 2), bf16)
    half_hidden = ((quarter, hidden // 2), bf16)
    pool_half = ((slots, rows_n, width), bf16)
    kv = ((quarter, 2 * width), bf16)
    arrays = dict(
        pack=((2, rows, sum(halves)), f32),
        beside=((rows, sum(halves)), f32),
        down_sum=((1, *weights[6][0][1:]), bf16),
        down_beside=((hidden // (8 * nz), width // 2), f32),
        rope=((2, quarter, 2 * LANES), f32),
        n1=((2 * quarter, width), bf16),
        q=tok,
        kv=((4, *kv[0]), bf16),
        att=tok,
        lse=((width // LANES, 1, 2 * quarter), f32),
        first=((quarter, width), f32),
        n2=tok,
        cq=tok,
        pool=((slots, rows_n, 2 * width), bf16),
        lse_cross=((width // LANES, 8, LANES), f32),
        cm=tok,
        second=((quarter, width), f32),
        n3=tok,
        act=((quarter, hidden), bf16),
        slope=((quarter, hidden), bf16),
        vec=((8, width), f32),
        branch=tok,
        mixed_grad=tok,
        cq_grad=tok,
        self_branch=tok,
        q_grad=tok,
        one_y=tok,
        stage=((2, rows_n, width), f32),
        gkv=((4, *kv[0]), bf16),
        vec_sum=((8, width), f32),
        by_act=((quarter, hidden), bf16),
        by_cot=half_tok,
        by_n3=tok,
        by_hidden_grad=half_hidden,
        by_cm=tok,
        by_branch=half_tok,
        by_neighbours=pool_half,
        by_pool_grad=pool_half,
        by_n2=tok,
        by_cq_grad=half_tok,
        by_att=tok,
        by_self_branch=half_tok,
        by_n1=((2 * quarter, width), bf16),
        by_q_grad=half_tok,
        by_kv_grad=((2 * quarter, width), bf16),
        by_vec=((8, width), f32),
    )
    return weights, arrays, sums


def layer_kernel(nz, names, *refs):
    refs = list(refs)
    r = Refs()

    def some(n):
        taken = refs[:n]
        del refs[:n]
        return taken

    r.take(NAMES_IN, some(len(NAMES_IN)))
    r.take(NAMES_OUT, some(len(NAMES_OUT)))
    r.sums, r.w = some(7), some(7)
    r.take(names, some(len(names)))
    r.pair_sem, r.rope_sem, r.out_sem, fkv_sem, kv_sem, swap_sem, g_send, g_recv, r_send, r_recv, r.credit = refs
    p = Place(nz)
    g = Gather(p, r.w, GATHER, g_send, g_recv)
    swap = Swap(p, swap_sem)
    pairs = r.tokens.shape[1] // LANES
    down_part, turned, sent = forward(p, r, g, swap, fkv_sem, pairs)
    red = Reduce(p, r, REDUCE, r_send, r_recv)
    backward(p, r, g, swap, red, kv_sem, pairs, down_part, turned)
    for cp in sent:
        cp.wait_send()


def local_fast(
    tokens,
    prefix_len,
    neighbours,
    neighbour_index,
    w_qkv,
    w_out,
    w_cross_q,
    w_cross_kv,
    w_cross_out,
    w_up,
    w_down,
    gain_one,
    shift_one,
    gain_two,
    shift_two,
    gain_three,
    shift_three,
    cotangent,
):
    nz = lax.axis_size("dp") // 2
    quarter, width = tokens.shape[1:]
    rows, hidden = w_up.shape
    slots, rows_n = neighbours.shape[1:3]
    vectors = jnp.stack([gain_one, gain_two, gain_three, shift_one, shift_two, shift_three], 1)
    weights, arrays, sums = memory(nz, quarter, width, hidden, slots, rows_n, rows)
    vmem, smem, anywhere = (pl.BlockSpec(memory_space=m) for m in (pltpu.VMEM, pltpu.SMEM, pl.ANY))
    made = [((quarter, width), bf16), ((quarter, width), f32), ((slots, rows_n, width), f32), *sums]
    dma = pltpu.SemaphoreType.DMA
    out, tokens_grad, neighbours_grad, *summed = pl.pallas_call(
        functools.partial(layer_kernel, nz, tuple(arrays)),
        out_shape=[jax.ShapeDtypeStruct(*v) for v in made],
        in_specs=[vmem] * 10 + [smem, vmem, smem, anywhere],
        out_specs=[vmem, vmem, anywhere] + [vmem] * len(sums),
        scratch_shapes=[pltpu.VMEM(*v) for v in (*weights, *arrays.values())]
        + [
            dma((6,)),
            dma((2,)),
            dma((2,)),
            dma((2, 2)),
            dma((2,)),
            dma((2, 28)),
            dma((len(GATHER), 12)),
            dma((len(GATHER), 12)),
            dma((len(REDUCE), 8)),
            dma((len(REDUCE), 8)),
            pltpu.SemaphoreType.REGULAR((7,)),
        ],
        compiler_params=pltpu.CompilerParams(
            collective_id=0, has_side_effects=True, vmem_limit_bytes=64 * 2**20 - 2**17
        ),
    )(
        w_qkv, w_cross_kv, w_out, w_cross_q, w_cross_out, w_up, w_down, vectors,
        tokens[0], cotangent[0], prefix_len, neighbours[0],
        neighbour_index.reshape(-1), jnp.asarray(rope_table(4 * quarter)),
    )
    return deliver(out, tokens_grad, neighbours_grad, summed)


def pick_slots(pool, index):
    return jnp.stack(
        [
            jnp.concatenate([lax.dynamic_slice_in_dim(pool[s], index[s, j], 1, 0) for j in range(index.shape[1])], 0)
            for s in range(index.shape[0])
        ]
    )


def slot_places(index):
    slots = index.shape[1]
    same = index[:, :, None] == jnp.arange(slots)[None, None, :]
    return jnp.sum(jnp.where(same, jnp.arange(slots)[None, :, None], 0), 1)


def dense_dot(left_side, weight):
    return jnp.dot(left_side, weight, preferred_element_type=jnp.float32)


def input_grad(grad_out, weight):
    return lax.dot_general(
        grad_out,
        weight,
        (((grad_out.ndim - 1,), (1,)), ((), ())),
        preferred_element_type=jnp.float32,
    )


def weight_grad(left_side, grad_out):
    flat_left = left_side.reshape(-1, left_side.shape[-1])
    flat_grad = grad_out.reshape(-1, grad_out.shape[-1])
    return lax.dot_general(
        flat_left, flat_grad, (((0,), (0,)), ((), ())), preferred_element_type=jnp.float32
    )


def plain_norm_parts(array_in):
    avg_value = jnp.mean(array_in, -1, keepdims=True)
    centred = array_in - avg_value
    inv_std = lax.rsqrt(jnp.mean(centred * centred, -1, keepdims=True) + eps)
    return (centred * inv_std, inv_std)


def norm_back(grad_out, unit_part, inv_std, gain_f):
    scaled = grad_out * gain_f
    grad_in = inv_std * (
        scaled
        - jnp.mean(scaled, -1, keepdims=True)
        - unit_part * jnp.mean(scaled * unit_part, -1, keepdims=True)
    )
    return (grad_in, jnp.sum(grad_out * unit_part, (0, 1)), jnp.sum(grad_out, (0, 1)))


def rotary_tables(positions):
    half_size = HEAD // 2
    frequency = 10000.0 ** (-jnp.arange(half_size).astype(jnp.float32) / half_size)
    angles = positions.astype(jnp.float32)[:, None] * frequency[None, :]
    return (jnp.cos(angles)[:, None, :], jnp.sin(angles)[:, None, :])


def plain_rotate(array_in, cosine, sine_part):
    half_size = HEAD // 2
    first_half = array_in[..., :half_size]
    second = array_in[..., half_size:]
    return jnp.concatenate(
        [first_half * cosine - second * sine_part, second * cosine + first_half * sine_part], -1
    )


def unrotate(grad_in, cosine, sine_part):
    half_size = HEAD // 2
    first_half = grad_in[..., :half_size]
    second = grad_in[..., half_size:]
    return jnp.concatenate(
        [first_half * cosine + second * sine_part, second * cosine - first_half * sine_part], -1
    )


def grouped(array_in):
    split_heads = array_in.reshape(
        array_in.shape[0], array_in.shape[1], array_in.shape[2] // 4, 4, array_in.shape[3]
    )
    return jnp.moveaxis(split_heads, 2, 0)


def ungrouped(array_in):
    shifted_axes = jnp.moveaxis(array_in, 0, 2)
    return shifted_axes.reshape(
        shifted_axes.shape[0], shifted_axes.shape[1], -1, shifted_axes.shape[-1]
    )


def masked_scores(visible, queries, key_rows):
    scores = jnp.einsum(
        "sqhd,skhd->shqk", queries, key_rows, preferred_element_type=jnp.float32
    ) * HEAD ** (-0.5)
    return jnp.where(visible[:, None], scores, masked)


def attend_group(visible, packed):
    queries, key_rows, values = packed
    scores = masked_scores(visible, queries, key_rows)
    row_max = jnp.max(scores, -1, keepdims=True)
    exp_scores = jnp.exp(scores - row_max)
    row_total = jnp.sum(exp_scores, -1, keepdims=True)
    probabilities = (exp_scores / row_total).astype(jnp.bfloat16)
    mixed_out = jnp.einsum(
        "shqk,skhd->sqhd", probabilities, values, preferred_element_type=jnp.float32
    )
    return (mixed_out, (row_max + jnp.log(row_total))[..., 0])


def attend_back(visible, packed):
    queries, key_rows, values, grad_out, logsum = packed
    scores = masked_scores(visible, queries, key_rows)
    probabilities = jnp.exp(scores - logsum[..., None])
    grad_probs = jnp.einsum("sqhd,skhd->shqk", grad_out, values, preferred_element_type=jnp.float32)
    grad_scores = (
        probabilities * (grad_probs - jnp.sum(probabilities * grad_probs, -1, keepdims=True))
    ).astype(jnp.bfloat16)
    grad_query = jnp.einsum(
        "shqk,skhd->sqhd", grad_scores, key_rows, preferred_element_type=jnp.float32
    ) * HEAD ** (-0.5)
    grad_key = jnp.einsum(
        "shqk,sqhd->skhd", grad_scores, queries, preferred_element_type=jnp.float32
    ) * HEAD ** (-0.5)
    grad_value = jnp.einsum(
        "shqk,sqhd->skhd",
        probabilities.astype(jnp.bfloat16),
        grad_out,
        preferred_element_type=jnp.float32,
    )
    return (grad_query, grad_key, grad_value)


def local_plain(
    tokens,
    prefix_len,
    neighbours,
    neighbour_index,
    w_qkv,
    w_out,
    w_cross_q,
    w_cross_kv,
    w_cross_out,
    w_up,
    w_down,
    gain_one,
    shift_one,
    gain_two,
    shift_two,
    gain_three,
    shift_three,
    cotangent,
):
    forward_set = (
        lax.all_gather(w_qkv, ("dp", "seq"), axis=0, tiled=True),
        lax.all_gather(w_out, ("dp", "seq"), axis=0, tiled=True),
        lax.all_gather(w_cross_q, ("dp", "seq"), axis=0, tiled=True),
        lax.all_gather(w_cross_kv, ("dp", "seq"), axis=0, tiled=True),
        lax.all_gather(w_cross_out, ("dp", "seq"), axis=0, tiled=True),
        lax.all_gather(w_up, ("dp", "seq"), axis=0, tiled=True),
        lax.all_gather(w_down, ("dp", "seq"), axis=0, tiled=True),
        lax.all_gather(gain_one, ("dp", "seq"), axis=0, tiled=True),
        lax.all_gather(shift_one, ("dp", "seq"), axis=0, tiled=True),
        lax.all_gather(gain_two, ("dp", "seq"), axis=0, tiled=True),
        lax.all_gather(shift_two, ("dp", "seq"), axis=0, tiled=True),
        lax.all_gather(gain_three, ("dp", "seq"), axis=0, tiled=True),
        lax.all_gather(shift_three, ("dp", "seq"), axis=0, tiled=True),
    )
    (
        full_qkv,
        full_out,
        full_cross_q,
        full_cross_kv,
        full_cross_out,
        full_up,
        full_down,
        full_gain_one,
        full_shift_one,
        full_gain_two,
        full_shift_two,
        full_gain_three,
        full_shift_three,
    ) = forward_set
    seq_here, quarter, width = tokens.shape
    heads = width // HEAD
    hidden_width = full_up.shape[1]
    length = quarter * lax.axis_size("seq")
    seq_index = lax.axis_index("seq")
    query_pos = seq_index * quarter + jnp.arange(quarter)
    key_pos = jnp.arange(length)
    visible = (key_pos[None, None, :] <= query_pos[None, :, None]) | (
        key_pos[None, None, :] < prefix_len[:, None, None]
    )
    cosine, sine_part = rotary_tables(query_pos)
    gain_f1 = full_gain_one.astype(jnp.float32)
    gain_f2 = full_gain_two.astype(jnp.float32)
    gain_f3 = full_gain_three.astype(jnp.float32)
    resid_in = tokens.astype(jnp.float32)
    unit_one, inv_one = plain_norm_parts(resid_in)
    normed_one = (unit_one * gain_f1 + full_shift_one.astype(jnp.float32)).astype(jnp.bfloat16)
    joined = dense_dot(normed_one, full_qkv)
    query_rot = plain_rotate(
        joined[..., :width].reshape(seq_here, quarter, heads, HEAD), cosine, sine_part
    ).astype(jnp.bfloat16)
    key_local = (
        plain_rotate(
            joined[..., width : 2 * width].reshape(seq_here, quarter, heads, HEAD),
            cosine,
            sine_part,
        )
        .astype(jnp.bfloat16)
        .reshape(seq_here, quarter, width)
    )
    value_local = joined[..., 2 * width :].astype(jnp.bfloat16)
    key_all, value_all = (
        lax.all_gather(key_local, "seq", axis=1, tiled=True),
        lax.all_gather(value_local, "seq", axis=1, tiled=True),
    )
    key_heads = key_all.reshape(seq_here, length, heads, HEAD)
    value_heads = value_all.reshape(seq_here, length, heads, HEAD)
    attended, logsum = lax.map(
        functools.partial(attend_group, visible),
        (grouped(query_rot), grouped(key_heads), grouped(value_heads)),
    )
    attended = ungrouped(attended).reshape(seq_here, quarter, width).astype(jnp.bfloat16)
    first_sum = resid_in + dense_dot(attended, full_out)
    unit_two, inv_two = plain_norm_parts(first_sum)
    normed_two = (unit_two * gain_f2 + full_shift_two.astype(jnp.float32)).astype(jnp.bfloat16)
    cross_query = dense_dot(normed_two, full_cross_q).astype(jnp.bfloat16)
    pool_kv = dense_dot(neighbours, full_cross_kv).astype(jnp.bfloat16)
    slots = neighbours.shape[1]
    spans = slots // 2
    span_len = quarter // spans
    neighbour_rows = 2 * neighbours.shape[2]
    local_index = neighbour_index.reshape(seq_here, slots) - seq_index * slots
    picked = pick_slots(pool_kv, local_index)
    picked = picked.reshape(seq_here, spans, neighbour_rows, 2 * width)
    cross_keys = picked[..., :width].reshape(seq_here, spans, neighbour_rows, heads, HEAD)
    cross_values = picked[..., width:].reshape(seq_here, spans, neighbour_rows, heads, HEAD)
    cross_queries = cross_query.reshape(seq_here, spans, span_len, heads, HEAD)
    cross_scores = jnp.einsum(
        "scqhd,sckhd->schqk", cross_queries, cross_keys, preferred_element_type=jnp.float32
    ) * HEAD ** (-0.5)
    cross_probs = jax.nn.softmax(cross_scores, -1)
    cross_weights = cross_probs.astype(jnp.bfloat16)
    cross_mixed = jnp.einsum(
        "schqk,sckhd->scqhd", cross_weights, cross_values, preferred_element_type=jnp.float32
    )
    cross_mixed = cross_mixed.reshape(seq_here, quarter, width).astype(jnp.bfloat16)
    second_sum = first_sum + dense_dot(cross_mixed, full_cross_out)
    unit_three, inv_three = plain_norm_parts(second_sum)
    normed_three = (unit_three * gain_f3 + full_shift_three.astype(jnp.float32)).astype(
        jnp.bfloat16
    )
    hidden_pre = dense_dot(normed_three, full_up)
    activated = jax.nn.gelu(hidden_pre, approximate=False).astype(jnp.bfloat16)
    output = (second_sum + dense_dot(activated, full_down)).astype(jnp.bfloat16)
    grad_act = input_grad(cotangent, full_down)
    _, gelu_back = jax.vjp(functools.partial(jax.nn.gelu, approximate=False), hidden_pre)
    grad_hidden = gelu_back(grad_act)[0].astype(jnp.bfloat16)
    grad_normed_three = input_grad(grad_hidden, full_up)
    back_three, grad_gain_three, grad_shift_three = norm_back(
        grad_normed_three, unit_three, inv_three, full_gain_three.astype(jnp.float32)
    )
    grad_second = cotangent.astype(jnp.float32) + back_three
    grad_cross_branch = grad_second.astype(jnp.bfloat16)
    grad_mixed = (
        input_grad(grad_cross_branch, full_cross_out)
        .astype(jnp.bfloat16)
        .reshape(seq_here, spans, span_len, heads, HEAD)
    )
    grad_cross_probs = jnp.einsum(
        "scqhd,sckhd->schqk", grad_mixed, cross_values, preferred_element_type=jnp.float32
    )
    grad_cross_scores = (
        cross_probs
        * (grad_cross_probs - jnp.sum(cross_probs * grad_cross_probs, -1, keepdims=True))
    ).astype(jnp.bfloat16)
    grad_cross_query = (
        (
            jnp.einsum(
                "schqk,sckhd->scqhd",
                grad_cross_scores,
                cross_keys,
                preferred_element_type=jnp.float32,
            )
            * HEAD ** (-0.5)
        )
        .astype(jnp.bfloat16)
        .reshape(seq_here, quarter, width)
    )
    grad_cross_keys = jnp.einsum(
        "schqk,scqhd->sckhd", grad_cross_scores, cross_queries, preferred_element_type=jnp.float32
    ) * HEAD ** (-0.5)
    grad_cross_values = jnp.einsum(
        "schqk,scqhd->sckhd", cross_weights, grad_mixed, preferred_element_type=jnp.float32
    )
    grad_picked = jnp.concatenate(
        [
            grad_cross_keys.reshape(seq_here, spans, neighbour_rows, width),
            grad_cross_values.reshape(seq_here, spans, neighbour_rows, width),
        ],
        -1,
    )
    grad_picked = grad_picked.reshape(seq_here, slots, neighbours.shape[2], 2 * width)
    grad_pool_kv = pick_slots(grad_picked.astype(jnp.bfloat16), slot_places(local_index))
    grad_neighbours = input_grad(grad_pool_kv, full_cross_kv)
    grad_normed_two = input_grad(grad_cross_query, full_cross_q)
    back_two, grad_gain_two, grad_shift_two = norm_back(
        grad_normed_two, unit_two, inv_two, full_gain_two.astype(jnp.float32)
    )
    grad_first = grad_second + back_two
    grad_self_branch = grad_first.astype(jnp.bfloat16)
    grad_attended = (
        input_grad(grad_self_branch, full_out)
        .astype(jnp.bfloat16)
        .reshape(seq_here, quarter, heads, HEAD)
    )
    grad_query, grad_key_all, grad_value_all = lax.map(
        functools.partial(attend_back, visible),
        (
            grouped(query_rot),
            grouped(key_heads),
            grouped(value_heads),
            grouped(grad_attended),
            logsum,
        ),
    )
    grad_query = ungrouped(grad_query)
    grad_key_all = ungrouped(grad_key_all).reshape(seq_here, length, width)
    grad_value_all = ungrouped(grad_value_all).reshape(seq_here, length, width)
    grad_key, grad_value = (
        lax.psum_scatter(
            grad_key_all.astype(jnp.bfloat16), "seq", scatter_dimension=1, tiled=True
        ).astype(jnp.float32),
        lax.psum_scatter(
            grad_value_all.astype(jnp.bfloat16), "seq", scatter_dimension=1, tiled=True
        ).astype(jnp.float32),
    )
    grad_joined = jnp.concatenate(
        [
            unrotate(grad_query, cosine, sine_part).reshape(seq_here, quarter, width),
            unrotate(grad_key.reshape(seq_here, quarter, heads, HEAD), cosine, sine_part).reshape(
                seq_here, quarter, width
            ),
            grad_value,
        ],
        -1,
    ).astype(jnp.bfloat16)
    grad_normed_one = input_grad(grad_joined, full_qkv)
    back_one, grad_gain_one, grad_shift_one = norm_back(
        grad_normed_one, unit_one, inv_one, full_gain_one.astype(jnp.float32)
    )
    grad_tokens = grad_first + back_one
    norm_grads = jnp.stack(
        [
            grad_gain_one,
            grad_shift_one,
            grad_gain_two,
            grad_shift_two,
            grad_gain_three,
            grad_shift_three,
        ],
        1,
    )
    width_owned = lax.psum_scatter(
        jnp.concatenate(
            [
                weight_grad(normed_one, grad_joined),
                weight_grad(attended, grad_self_branch),
                weight_grad(normed_two, grad_cross_query),
                weight_grad(neighbours, grad_pool_kv),
                weight_grad(cross_mixed, grad_cross_branch),
                weight_grad(normed_three, grad_hidden),
                norm_grads,
            ],
            1,
        ),
        ("dp", "seq"),
        scatter_dimension=0,
        tiled=True,
    )
    down_owned = lax.psum_scatter(
        weight_grad(activated, cotangent), ("dp", "seq"), scatter_dimension=0, tiled=True
    )
    column = 8 * width + hidden_width
    return (
        output,
        grad_tokens,
        grad_neighbours,
        width_owned[:, : 3 * width],
        width_owned[:, 3 * width : 4 * width],
        width_owned[:, 4 * width : 5 * width],
        width_owned[:, 5 * width : 7 * width],
        width_owned[:, 7 * width : 8 * width],
        width_owned[:, 8 * width : column],
        down_owned,
        width_owned[:, column],
        width_owned[:, column + 1],
        width_owned[:, column + 2],
        width_owned[:, column + 3],
        width_owned[:, column + 4],
        width_owned[:, column + 5],
    )


def solution(mesh):
    sizes = dict(mesh.shape)
    fits = sizes == {"dp": 8, "seq": 4}
    return jax.shard_map(
        local_fast if fits else local_plain,
        mesh=mesh,
        in_specs=(
            P("dp", "seq", None),
            P("dp"),
            P("dp", "seq", None, None),
            P("dp", "seq", None),
            P(("dp", "seq"), None),
            P(("dp", "seq"), None),
            P(("dp", "seq"), None),
            P(("dp", "seq"), None),
            P(("dp", "seq"), None),
            P(("dp", "seq"), None),
            P(("dp", "seq"), None),
            P(("dp", "seq")),
            P(("dp", "seq")),
            P(("dp", "seq")),
            P(("dp", "seq")),
            P(("dp", "seq")),
            P(("dp", "seq")),
            P("dp", "seq", None),
        ),
        out_specs=(
            P("dp", "seq", None),
            P("dp", "seq", None),
            P("dp", "seq", None, None),
            P(("dp", "seq"), None),
            P(("dp", "seq"), None),
            P(("dp", "seq"), None),
            P(("dp", "seq"), None),
            P(("dp", "seq"), None),
            P(("dp", "seq"), None),
            P(("dp", "seq"), None),
            P(("dp", "seq")),
            P(("dp", "seq")),
            P(("dp", "seq")),
            P(("dp", "seq")),
            P(("dp", "seq")),
            P(("dp", "seq")),
        ),
        check_vma=False,
    )
```

```python
import functools
import math

import jax
import jax.numpy as jnp
import numpy as np
from jax import lax
from jax.experimental import pallas as pl
from jax.experimental.pallas import tpu as pltpu
from jax.sharding import PartitionSpec as P

HEAD = 64
eps = 1e-05
masked = -1e30
MESH = pl.DeviceIdType.MESH
bf16 = jnp.bfloat16
f32 = jnp.float32
NN = (((1,), (0,)), ((), ()))
NT = (((1,), (1,)), ((), ()))
TN = (((0,), (0,)), ((), ()))
LANES = 128
AHEAD = 3
SPREAD = 3
ACROSS, LAST = 2, 4


def dot(a, b, dims=NN):
    return lax.dot_general(a, b, dims, preferred_element_type=f32)


def norm_parts(v):
    centred = v - jnp.mean(v, -1, keepdims=True)
    inv = lax.rsqrt(jnp.mean(centred * centred, -1, keepdims=True) + eps)
    return centred * inv, inv


class Place:
    def __init__(self, nz):
        dp, s = lax.axis_index("dp"), lax.axis_index("seq")
        self.nz, self.dp, self.s = nz, dp, s
        self.z, self.x = lax.div(dp, 2), lax.rem(dp, 2)
        self.y, self.c = lax.div(s, 2), lax.rem(s, 2)
        x, y, z, c = self.x, self.y, self.z, self.c
        self.o = 1 - c
        self.own, self.at_x, self.at_y, self.at_d = (
            x * 2 + y,
            (1 - x) * 2 + y,
            x * 2 + 1 - y,
            (1 - x) * 2 + 1 - y,
        )
        self.to_z = [(lax.rem(z + j, nz) * 2 + x, s) for j in range(1, nz)]
        self.z_of = [lax.rem(z + j, nz) for j in range(1, nz)]
        self.z_from = [lax.rem(z - j + nz, nz) for j in range(1, nz)]
        self.to_x = (z * 2 + 1 - x, s)
        self.to_y = (dp, (1 - y) * 2 + c)
        self.to_c = (dp, y * 2 + 1 - c)
        self.s_y = (1 - y) * 2 + c
        self.s_c = y * 2 + 1 - c
        self.s_d = (1 - y) * 2 + 1 - c

    def meet(self):
        barrier = pltpu.get_barrier_semaphore()
        friends = [*self.to_z, self.to_x, self.to_y, self.to_c]
        for device in friends:
            pl.semaphore_signal(barrier, inc=1, device_id=device, device_id_type=MESH)
        pl.semaphore_wait(barrier, len(friends))


def remote(src, dst, send, recv, device):
    return pltpu.make_async_remote_copy(
        src_ref=src, dst_ref=dst, send_sem=send, recv_sem=recv, device_id=device, device_id_type=MESH
    )


class Gather:
    def __init__(self, place, weights, chunks, send, recv):
        self.p, self.w, self.chunks, self.ss, self.rs = place, weights, chunks, send, recv
        self.sent = [[] for _ in chunks]
        self.t, self.have = 0, set()
        self.z_first = [q for q, v in enumerate(chunks) if v[3] > 0]
        self.plane_first = [q for q, v in enumerate(chunks) if v[3] <= 0]

    def chunks_of(self, k):
        return [q for q, v in enumerate(self.chunks) if v[0] == k]

    def begin(self):
        self.along_z(self.z_first[0])

    def tick(self):
        t, order = self.t, self.z_first
        n = len(order)
        if t >= n + LAST:
            return
        if t == 0:
            for q in order[1:AHEAD]:
                self.along_z(q)
            for q in self.plane_first:
                self.plane_out(q)
        if t < n:
            self.along_xy(order[t])
        if t + AHEAD < n:
            self.along_z(order[t + AHEAD])
        if t == 1:
            for q in self.plane_first:
                self.plane_across(q)
        if t >= 2 and (t - 2) % SPREAD == 0 and (t - 2) // SPREAD < len(self.plane_first):
            self.plane_z(self.plane_first[(t - 2) // SPREAD])
        if 0 <= t - ACROSS < n:
            self.across(order[t - ACROSS])
        if 0 <= t - LAST < n:
            self.last(order[t - LAST])
        self.t += 1

    def need(self, q):
        if q in self.plane_first:
            while self.t <= SPREAD * self.plane_first.index(q) + 2:
                self.tick()
        else:
            while self.t <= self.z_first.index(q) + LAST:
                self.tick()
        if q not in self.have:
            self.have.add(q)
            if q in self.plane_first:
                self.plane_last(q)
                self.plane_ready(q)
            else:
                self.ready(q)

    def plane_out(self, q):
        p = self.p
        mine = self.part(q, p.c, p.z, p.own)
        for j, device in ((3, p.to_x), (4, p.to_y), (7, p.to_c)):
            self.send(q, j, mine, device)

    def plane_across(self, q):
        p = self.p
        from_x, from_y = self.part(q, p.c, p.z, p.at_x), self.part(q, p.c, p.z, p.at_y)
        self.wait(q, 3, from_x)
        self.send(q, 8, from_x, p.to_c)
        self.wait(q, 4, from_y)
        self.send(q, 9, from_y, p.to_c)
        if self.chunks[q][3] == 0:
            self.send(q, 5, from_y, p.to_x)
        else:
            self.send(q, 5, from_x, p.to_y)

    def plane_z(self, q):
        p, every = self.p, slice(None)
        diag = self.part(q, p.c, p.z, p.at_d)
        self.wait(q, 5, diag)
        self.send(q, 10, diag, p.to_c)
        for j, device in enumerate(p.to_z):
            self.send(q, j, self.part(q, p.c, p.z, every), device)

    def plane_last(self, q):
        p, every = self.p, slice(None)
        for j, z in enumerate(p.z_from):
            ref = self.part(q, p.c, z, every)
            self.wait(q, j, ref)
            self.send(q, 11 + j, ref, p.to_c)

    def plane_ready(self, q):
        p, every = self.p, slice(None)
        for j, xy in ((7, p.own), (8, p.at_x), (9, p.at_y), (10, p.at_d)):
            self.wait(q, j, self.part(q, p.o, p.z, xy))
        for j, z in enumerate(p.z_from):
            self.wait(q, 11 + j, self.part(q, p.o, z, every))

    def part(self, q, half, z, xy):
        k, start, width, _ = self.chunks[q]
        return self.w[k].at[half, z, xy, :, pl.ds(start, width)]

    def copy(self, q, j, ref, device):
        return remote(ref, ref, self.ss.at[q, j], self.rs.at[q, j], device)

    def send(self, q, j, ref, device):
        cp = self.copy(q, j, ref, device)
        cp.start()
        self.sent[q].append(cp)

    def wait(self, q, j, ref):
        self.copy(q, j, ref, self.p.to_c).wait_recv()

    def along_z(self, q):
        p = self.p
        for j, device in enumerate(p.to_z):
            self.send(q, j, self.part(q, p.c, p.z, p.own), device)

    def along_xy(self, q):
        p, allz = self.p, slice(None)
        for j, z in enumerate(p.z_from):
            self.wait(q, j, self.part(q, p.c, z, p.own))
        mine = self.part(q, p.c, allz, p.own)
        self.send(q, 3, mine, p.to_x)
        self.send(q, 4, mine, p.to_y)
        self.send(q, 7, mine, p.to_c)

    def across(self, q):
        p, allz, cut = self.p, slice(None), self.chunks[q][3]
        from_x, from_y = self.part(q, p.c, allz, p.at_x), self.part(q, p.c, allz, p.at_y)
        self.wait(q, 3, from_x)
        self.send(q, 5, self.part(q, p.c, pl.ds(0, cut), p.at_x), p.to_y)
        self.send(q, 8, from_x, p.to_c)
        self.wait(q, 4, from_y)
        self.send(q, 6, self.part(q, p.c, pl.ds(cut, p.nz - cut), p.at_y), p.to_x)
        self.send(q, 9, from_y, p.to_c)

    def last(self, q):
        p, cut = self.p, self.chunks[q][3]
        for j, z in ((5, pl.ds(0, cut)), (6, pl.ds(cut, p.nz - cut))):
            ref = self.part(q, p.c, z, p.at_d)
            self.wait(q, j, ref)
            self.send(q, j + 5, ref, p.to_c)

    def ready(self, q):
        p, allz, cut = self.p, slice(None), self.chunks[q][3]
        for j, z, xy in (
            (7, allz, p.own),
            (8, allz, p.at_x),
            (9, allz, p.at_y),
            (10, pl.ds(0, cut), p.at_d),
            (11, pl.ds(cut, p.nz - cut), p.at_d),
        ):
            self.wait(q, j, self.part(q, p.o, z, xy))

    def settle(self, q):
        for cp in self.sent[q]:
            cp.wait_send()
        self.sent[q] = []


def half_of(w, h, start=None, width=None):
    v = w[h] if start is None else w[h, :, :, :, pl.ds(start, width)]
    return v.reshape(-1, v.shape[-1])


def lane_masks():
    lane = lax.broadcasted_iota(jnp.int32, (1, LANES), 1)
    low = lane < HEAD
    return low, jnp.where(low, 1.0, 0.0).astype(bf16), jnp.where(low, 0.0, 1.0).astype(bf16)


def stacked(v, low, high):
    return jnp.concatenate([v * low, v * high], 0)


def swap_halves(v):
    lane = lax.broadcasted_iota(jnp.int32, v.shape, 1)
    first = lax.rem(lane, HEAD) < HEAD // 2
    return jnp.where(first, pltpu.roll(v, LANES - HEAD // 2, 1), pltpu.roll(v, HEAD // 2, 1))


def rotate(v, cosine, signed):
    return v * cosine + swap_halves(v) * signed


def forward(p, r, g, swap, kv_sem, pairs):
    n = len(g.chunks)
    c, z = p.c, p.z
    w = r.w

    vectors = r.vectors[...].astype(f32)
    count, rows = vectors.shape
    vectors = jnp.concatenate([vectors, jnp.zeros((count, LANES - rows), f32)], 1)
    vectors = jnp.concatenate([vectors, jnp.zeros((LANES - count, LANES), f32)], 0)
    vectors = jnp.transpose(vectors)[:rows]
    start = 0
    for k, ref in enumerate((r.w_qkv, r.w_cross_kv, r.w_out, r.w_cross_q, r.w_cross_out, r.w_up)):
        rows = ref[...].astype(f32)
        size = rows.shape[1] // 2
        for h in range(2):
            parts = 3 if k == 0 else 1
            part = size // parts
            for i in range(parts):
                source = i * 2 * part + h * part
                r.pack[h, :, start + i * part : start + (i + 1) * part] = rows[:, source : source + part]
            if k == 0:
                r.pack[h, :, start + size : start + size + LANES] = vectors
        start += w[k].shape[-1]
    p.meet()
    first = remote(r.pack.at[p.o], r.beside, r.pair_sem.at[0], r.pair_sem.at[1], p.to_c)
    first.start()
    down_rows, down_half = r.w_down.shape[0], w[6].shape[-1]
    down_at = pl.ds(pl.multiple_of(c * down_rows, 16), down_rows)
    down = remote(
        r.w_down.at[:, pl.ds(pl.multiple_of(p.o * down_half, LANES), down_half)],
        w[6].at[p.o, z, p.own, down_at],
        r.pair_sem.at[2],
        r.pair_sem.at[3],
        p.to_c,
    )
    down.start()
    tokens_y = remote(r.tokens, r.branch, r.pair_sem.at[4], r.pair_sem.at[5], p.to_y)
    tokens_y.start()
    ropes = [pltpu.make_async_copy(r.rope_table.at[s], r.rope.at[i], r.rope_sem.at[i]) for i, s in enumerate((p.s, p.s_y))]
    for rope in ropes:
        rope.start()
    w[6][c, z, p.own, down_at] = r.w_down[:, pl.ds(pl.multiple_of(c * down_half, LANES), down_half)]
    first.wait_recv()
    start = 0
    for k in range(6):
        width = w[k].shape[-1]
        mine, other = r.pack[c, :, start : start + width], r.beside[:, start : start + width]
        top, low = jnp.where(c == 0, mine, other), jnp.where(c == 0, other, mine)
        w[k][c, z, p.own] = jnp.concatenate([top, low], 0).astype(bf16)
        start += width
        if k == 0:
            g.begin()
    down.wait_recv()
    g.tick()
    swap.send("cot", r.cotangent.at[:, pl.ds(pl.multiple_of(p.o * down_half, LANES), down_half)], r.by_cot)
    swap.send("nb", r.neighbours, r.by_neighbours)
    for rope in ropes:
        rope.wait()
    tokens = r.tokens[...].astype(f32)
    quarter, width = tokens.shape
    unit, _ = norm_parts(tokens)
    g.tick()
    tokens_y.wait_recv()
    unit_y, _ = norm_parts(r.branch[...].astype(f32))
    g.need(0)
    part = width // 2
    r.vec[...] = jnp.transpose(half_of(w[0], 0, 3 * part, LANES).astype(f32))[:8]

    def affine(v, i):
        return (v * r.vec[i : i + 1] + r.vec[3 + i : 4 + i]).astype(bf16)

    r.n1[:quarter] = affine(unit, 0)
    r.n1[quarter:] = affine(unit_y, 0)
    swap.send("n1", r.n1, r.by_n1)
    for h in range(2):
        value = dot(r.n1[...], half_of(w[0], h, 2 * part, part)).astype(bf16)
        cols = slice(width + h * part, width + (h + 1) * part)
        r.kv[p.s, :, cols] = value[:quarter]
        r.kv[p.s_y, :, cols] = value[quarter:]

    def turned(v, i, sign=1):
        cosine, signed = r.rope[i, :, :LANES], r.rope[i, :, LANES:]
        return jnp.concatenate(
            [rotate(v[:, b : b + LANES], cosine, sign * signed) for b in range(0, v.shape[1], LANES)], 1
        )

    g.need(1)
    for h in range(2):
        key = dot(r.n1[...], half_of(w[0], h, part, part))
        cols = slice(h * part, (h + 1) * part)
        r.kv[p.s, :, cols] = turned(key[:quarter], 0).astype(bf16)
        r.kv[p.s_y, :, cols] = turned(key[quarter:], 1).astype(bf16)
    kv_sent = [
        remote(r.kv.at[s], r.kv.at[s], kv_sem.at[0, i], kv_sem.at[1, i], p.to_c) for i, s in enumerate((p.s, p.s_y))
    ]
    for cp in kv_sent:
        cp.start()
    g.need(2)
    for h in range(2):
        query = dot(r.n1[:quarter], half_of(w[0], h, 0, part))
        r.q[:, h * part : (h + 1) * part] = turned(query, 0).astype(bf16)
    g.need(3)
    g.need(4)

    def pool_rows(i, carry):
        rows = r.neighbours[pl.ds(i * 2, 2)].reshape(-1, r.neighbours.shape[2])
        for h in range(2):
            width = w[1].shape[-1]
            r.pool[pl.ds(i * 2, 2), :, h * width : (h + 1) * width] = (
                dot(rows, half_of(w[1], h)).astype(bf16).reshape(2, -1, width)
            )
        return carry

    lax.fori_loop(0, 2, pool_rows, 0)
    g.tick()
    lax.fori_loop(2, r.neighbours.shape[0] // 2, pool_rows, 0)
    for i, s in enumerate((p.s_c, p.s_d)):
        remote(r.kv.at[s], r.kv.at[s], kv_sem.at[0, i], kv_sem.at[1, i], p.to_c).wait_recv()

    low_lane, low, high = lane_masks()
    place = lax.broadcasted_iota(jnp.int32, (1, quarter), 1) + p.s * quarter
    limit = jnp.maximum(place, r.prefix[0] - 1)

    def self_pair(i, carry):
        cols = pl.ds(pl.multiple_of(i * LANES, LANES), LANES)
        vcols = pl.ds(pl.multiple_of(i * LANES + w[1].shape[-1], LANES), LANES)
        keys = r.kv[:, :, cols].reshape(-1, LANES)
        values = r.kv[:, :, vcols].reshape(-1, LANES)
        mixed = []
        for e, lanes in enumerate((low, high)):
            scores = dot(keys, r.q[:, cols] * (lanes * bf16(HEAD**-0.5)), NT)
            key_place = lax.broadcasted_iota(jnp.int32, scores.shape, 0)
            scores = jnp.where(key_place <= limit, scores, masked)
            top = jnp.max(scores, 0, keepdims=True)
            exped = jnp.exp(scores - top)
            total = jnp.sum(exped, 0, keepdims=True)
            weights = (exped * (1.0 / total)).astype(bf16)
            r.lse[i, :, e * quarter : (e + 1) * quarter] = top + jnp.log(total)
            mixed.append(dot(weights, values, TN))
        r.att[:, cols] = jnp.where(low_lane, *mixed).astype(bf16)
        return carry

    for i in range(0, pairs, 2):
        lax.fori_loop(i, i + 2, self_pair, 0)
        g.tick()
    g.need(5)

    def project(v, k):
        return jnp.concatenate([dot(v, half_of(w[k], h)) for h in range(2)], 1)

    swap.send("att", r.att, r.by_att)
    first_sum = tokens + project(r.att[...], 2)
    r.first[...] = first_sum
    r.n2[...] = affine(norm_parts(first_sum)[0], 1)
    swap.send("n2", r.n2, r.by_n2)
    g.need(6)
    r.cq[...] = project(r.n2[...], 3).astype(bf16)
    slots = r.neighbours.shape[0]
    span = quarter // (slots // 2)

    def cross_pair(i, carry):
        cols = pl.ds(pl.multiple_of(i * LANES, LANES), LANES)
        vcols = pl.ds(pl.multiple_of(i * LANES + w[1].shape[-1], LANES), LANES)
        for b in range(slots // 2):
            two = [lax.rem(r.index[b, j], slots) for j in range(2)]
            rows = slice(b * span, (b + 1) * span)
            queries = stacked(r.cq[rows, cols], low, high) * bf16(HEAD**-0.5)
            keys = jnp.concatenate([r.pool[t, :, cols] for t in two], 0)
            values = jnp.concatenate([r.pool[t, :, vcols] for t in two], 0)
            scores = dot(keys, queries, NT)
            top = jnp.max(scores, 0, keepdims=True)
            e = jnp.exp(scores - top)
            total = jnp.sum(e, 0, keepdims=True)
            weights = (e * (1.0 / total)).astype(bf16)
            r.lse_cross[i, b : b + 1] = top + jnp.log(total)
            mixed = dot(weights, values, TN)
            r.cm[rows, cols] = jnp.where(low_lane, mixed[:span], mixed[span:]).astype(bf16)
        return carry

    lax.fori_loop(0, pairs // 2, cross_pair, 0)
    g.tick()
    lax.fori_loop(pairs // 2, pairs, cross_pair, 0)
    g.need(7)
    swap.send("cm", r.cm, r.by_cm)
    second_sum = r.first[...] + project(r.cm[...], 4)
    r.second[...] = second_sum
    r.n3[...] = affine(norm_parts(second_sum)[0], 2)
    swap.send("n3", r.n3, r.by_n3)
    hidden_half = w[5].shape[-1]

    def up_tile(start, size):
        def body(h, carry):
            hidden = dot(r.n3[...], half_of(w[5], h, start, size))
            cdf = 0.5 * (1.0 + lax.erf(hidden * (0.5**0.5)))
            density = jnp.exp(-0.5 * hidden * hidden) * ((2 * math.pi) ** -0.5)
            cols = pl.ds(pl.multiple_of(h * hidden_half + start, LANES), size)
            r.act[:, cols] = (hidden * cdf).astype(bf16)
            r.slope[:, cols] = (cdf + hidden * density).astype(bf16)
            return carry

        lax.fori_loop(0, 2, body, 0)

    for q, (k, start, size, _) in enumerate(g.chunks):
        if k == 5:
            g.need(q)
            up_tile(start, size)
    swap.send("act", r.act, r.by_act)

    def down_part(q):
        _, start, size, _ = g.chunks[q]
        for h in range(2):
            cols = slice(h * down_half + start, h * down_half + start + size)
            r.out[:, cols] = (r.second[:, cols] + dot(r.act[...], half_of(w[6], h, start, size))).astype(bf16)

    return down_part, turned, (first, down, tokens_y, *kv_sent)


LAG = 4


class Reduce:
    def __init__(self, place, r, chunks, send, recv):
        self.p, self.r, self.w, self.chunks, self.ss, self.rs = place, r, r.w, chunks, send, recv
        self.sent, self.open, self.under_way, self.next = [], set(), {}, 0
        self.starts = [sum(v.shape[-1] for v in r.w[:k]) for k in range(7)]

    def free(self, k):
        p = self.p
        for device in (p.to_x, p.to_y, *p.to_z):
            pl.semaphore_signal(self.r.credit.at[k], inc=1, device_id=device, device_id_type=MESH)

    def array(self, k, half):
        if k == 6:
            return self.r.down_sum, 0 if half is self.p.c else 1
        return self.w[k], half

    def at(self, q, half, z, xy):
        k, start, width, _ = self.chunks[q]
        ref, lead = self.array(k, half)
        return ref.at[lead, z, xy, :, pl.ds(start, width)]

    def load(self, q, half, z, xy):
        k, start, width, _ = self.chunks[q]
        ref, lead = self.array(k, half)
        return ref[lead, z, xy, :, start : start + width].astype(f32)

    def save(self, q, half, z, xy, v):
        k, start, width, _ = self.chunks[q]
        ref, lead = self.array(k, half)
        ref[lead, z, xy, :, start : start + width] = v.astype(bf16)

    def copy(self, q, j, src, dst, device):
        cp = remote(src, dst, self.ss.at[q, j], self.rs.at[q, j], device)
        cp.start()
        self.sent.append(cp)

    def wait(self, q, j, ref):
        remote(ref, ref, self.ss.at[q, j], self.rs.at[q, j], self.p.to_c).wait_recv()

    def diagonal(self, q):
        p, cut = self.p, self.chunks[q][3]
        for j, z, device in ((0, pl.ds(0, cut), p.to_y), (1, pl.ds(cut, p.nz - cut), p.to_x)):
            self.copy(q, j, self.at(q, p.c, z, p.at_d), self.at(q, p.o, z, 0), device)

    def across(self, q):
        p, cut, allz = self.p, self.chunks[q][3], slice(None)
        for j, zs, to in ((0, range(cut), p.at_x), (1, range(cut, p.nz), p.at_y)):
            self.wait(q, j, self.at(q, p.o, pl.ds(zs[0], len(zs)), 0))
            for z in zs:
                self.save(q, p.c, z, to, self.load(q, p.c, z, to) + self.load(q, p.o, z, 0))
        self.copy(q, 2, self.at(q, p.c, allz, p.at_x), self.at(q, p.o, allz, 1), p.to_x)
        self.copy(q, 3, self.at(q, p.c, allz, p.at_y), self.at(q, p.o, allz, 2), p.to_y)

    def along_z(self, q):
        p, allz = self.p, slice(None)
        self.wait(q, 2, self.at(q, p.o, allz, 1))
        self.wait(q, 3, self.at(q, p.o, allz, 2))
        for z in range(p.nz):
            total = self.load(q, p.c, z, p.own) + self.load(q, p.o, z, 1) + self.load(q, p.o, z, 2)
            self.save(q, p.c, z, p.own, total)
        for j, device in enumerate(p.to_z):
            self.copy(q, 4 + j, self.at(q, p.c, p.z_of[j], p.own), self.at(q, p.o, j, 3), device)

    def steps(self, q):
        if self.chunks[q][3] > 0:
            return self.diagonal, self.across, self.along_z, self.last
        return self.z_out, self.plane_diagonal, self.plane_across, self.plane_last

    def z_out(self, q):
        p, every = self.p, slice(None)
        for j, device in enumerate(p.to_z):
            self.copy(q, 4 + j, self.at(q, p.c, p.z_of[j], every), self.at(q, p.o, j, every), device)

    def plane_diagonal(self, q):
        p, every = self.p, slice(None)
        for j in range(p.nz - 1):
            self.wait(q, 4 + j, self.at(q, p.o, j, every))
        for xy in range(4):
            total = self.load(q, p.c, p.z, xy)
            for j in range(p.nz - 1):
                total = total + self.load(q, p.o, j, xy)
            self.save(q, p.c, p.z, xy, total)
        device = p.to_x if self.chunks[q][3] == 0 else p.to_y
        self.copy(q, 0, self.at(q, p.c, p.z, p.at_d), self.at(q, p.o, p.nz - 1, 0), device)

    def plane_across(self, q):
        p, there = self.p, self.p.nz - 1
        to = p.at_y if self.chunks[q][3] == 0 else p.at_x
        self.wait(q, 0, self.at(q, p.o, there, 0))
        self.save(q, p.c, p.z, to, self.load(q, p.c, p.z, to) + self.load(q, p.o, there, 0))
        self.copy(q, 2, self.at(q, p.c, p.z, p.at_x), self.at(q, p.o, there, 1), p.to_x)
        self.copy(q, 3, self.at(q, p.c, p.z, p.at_y), self.at(q, p.o, there, 2), p.to_y)

    def plane_last(self, q):
        p, there = self.p, self.p.nz - 1
        total = self.load(q, p.c, p.z, p.own)
        for j in (1, 2):
            self.wait(q, 1 + j, self.at(q, p.o, there, j))
            total = total + self.load(q, p.o, there, j)
        self.hand_over(q, total)

    def last(self, q):
        p = self.p
        total = self.load(q, p.c, p.z, p.own)
        for j in range(p.nz - 1):
            self.wait(q, 4 + j, self.at(q, p.o, j, 3))
            total = total + self.load(q, p.o, j, 3)
        self.hand_over(q, total)

    def hand_over(self, q, total):
        p, r, (k, start, width, _) = self.p, self.r, self.chunks[q]
        cols = slice(start, start + width)
        rows = total.shape[0] // 2
        r.sums[k][p.c, :, cols] = jnp.where(p.c == 0, total[:rows], total[rows:])
        if k == 6:
            mine = r.down_beside.at[:, cols]
        else:
            mine = r.beside.at[:, self.starts[k] + start : self.starts[k] + start + width]
        mine[...] = jnp.where(p.c == 0, total[rows:], total[:rows])
        self.copy(q, 7, mine, r.sums[k].at[p.c, :, cols], p.to_c)

    def finish(self, q):
        p, (k, start, width, _) = self.p, self.chunks[q]
        self.wait(q, 7, self.r.sums[k].at[p.o, :, pl.ds(start, width)])

    def push(self, q=None, lag=LAG):
        for other in list(self.under_way):
            stage, age = self.under_way[other]
            if age + 1 < lag:
                self.under_way[other] = stage, age + 1
                continue
            self.steps(other)[stage + 1](other)
            self.under_way[other] = stage + 1, 0
            if stage == 2:
                del self.under_way[other]
        if q is not None:
            k = self.chunks[q][0]
            if k not in self.open:
                pl.semaphore_wait(self.r.credit.at[k], 1 + self.p.nz)
                self.open.add(k)
            self.steps(q)[0](q)
            self.under_way[q] = 0, 0

    def chunks_of(self, k):
        return [q for q, v in enumerate(self.chunks) if v[0] == k]

    def drain(self):
        while self.under_way:
            self.push(None, 1)
        for q in range(len(self.chunks)):
            self.finish(q)


class Swap:
    def __init__(self, place, sems):
        self.p, self.sems, self.n, self.sent, self.landed = place, sems, 0, [], {}

    def send(self, name, src, dst):
        cp = remote(src, dst, self.sems.at[0, self.n], self.sems.at[1, self.n], self.p.to_c)
        cp.start()
        self.sent.append(cp)
        self.landed[name] = cp
        self.n += 1

    def wait(self, name):
        self.landed.pop(name).wait_recv()


def norm_back_at(grad, v, gain):
    unit, inv = norm_parts(v)
    scaled = grad * gain
    back = inv * (
        scaled - jnp.mean(scaled, -1, keepdims=True) - unit * jnp.mean(scaled * unit, -1, keepdims=True)
    )
    return back, jnp.sum(grad * unit, 0, keepdims=True), jnp.sum(grad, 0, keepdims=True)


def backward(p, r, g, swap, red, kv_sem, pairs, down_part, turned):
    w, c, o = r.w, p.c, p.o
    quarter, width = r.tokens.shape
    hidden_half, pool_half = w[5].shape[-1], w[1].shape[-1]
    slots, rows_n = r.neighbours.shape[:2]
    low_lane, low, high = lane_masks()
    r.vec_sum[...] = jnp.zeros_like(r.vec_sum)

    def half(ref, h, size):
        return ref.at[:, pl.ds(pl.multiple_of(h * size, LANES), size)]

    def input_grad(ref, k, size):
        return sum(dot(ref[:, h * size : (h + 1) * size], half_of(w[k], h, 0, size), NT) for h in range(2))

    def weight_grad(k, left, left_beside, right, right_beside, size, tile=384, chunks=None, push=True):
        into, lead = red.array(k, c)
        rows = into.shape[3]
        per = tile // (4 * rows)
        for q in red.chunks_of(k) if chunks is None else chunks:
            _, start, n, _ = red.chunks[q]
            n = min(n, size - start)

            def body(i, carry, start=start, n=n):
                cols = pl.ds(pl.multiple_of(i * tile, LANES), tile)
                part = dot(left(cols), right(start, n), TN) + dot(left_beside(cols), right_beside(start, n), TN)
                into[lead, pl.ds(i * per, per), :, :, start : start + n] = part.astype(bf16).reshape(per, 4, rows, n)
                return carry

            lax.fori_loop(0, p.nz // per, body, 0)
            if push:
                red.push(q)

    def plain_grad(k, left, left_beside, right, right_beside, size, tile=384, chunks=None, push=True):
        weight_grad(
            k,
            lambda cols: left[:, cols],
            lambda cols: left_beside[:, cols],
            lambda start, n: right[:, pl.ds(pl.multiple_of(c * size + start, LANES), n)],
            lambda start, n: right_beside[:, start : start + n],
            size,
            tile,
            chunks,
            push,
        )

    def gain(i):
        return r.vec[i : i + 1]

    def keep_vec(i, gain_sum, shift_sum):
        r.vec_sum[i : i + 1] = gain_sum
        r.vec_sum[3 + i : 4 + i] = shift_sum

    for name in ("cot", "act"):
        swap.wait(name)
    red.free(6)
    plain_grad(6, r.act, r.by_act, r.cotangent, r.by_cot, w[6].shape[-1], 4 * w[6].shape[3])
    for q in g.chunks_of(6):
        g.need(q)
        down_part(q)
        g.settle(q)
        red.push()
    down_half = w[6].shape[-1]

    def act_tile(z, carry):
        rows = 4 * w[6].shape[3]
        cols = pl.ds(pl.multiple_of(z * rows, LANES), rows)
        act_grad = sum(
            dot(r.cotangent[:, h * down_half : (h + 1) * down_half], w[6][h, z].reshape(rows, down_half), NT)
            for h in range(2)
        )
        r.slope[:, cols] = (act_grad * r.slope[:, cols].astype(f32)).astype(bf16)
        return carry

    lax.fori_loop(0, p.nz, act_tile, 0)
    gh = r.slope
    swap.send("gh", half(gh, o, hidden_half), r.by_hidden_grad)
    red.push()
    grad_three = input_grad(gh, 5, hidden_half)
    red.free(5)
    red.push()
    for q in g.chunks_of(5):
        g.settle(q)
    back, dg, db = norm_back_at(grad_three, r.second[...], gain(2))
    keep_vec(2, dg, db)
    grad_second = r.cotangent[...].astype(f32) + back
    r.second[...] = grad_second
    r.branch[...] = grad_second.astype(bf16)
    swap.send("gcb", half(r.branch, o, width // 2), r.by_branch)
    for name in ("gh", "n3"):
        swap.wait(name)
    plain_grad(5, r.n3, r.by_n3, gh, r.by_hidden_grad, hidden_half)
    r.mixed_grad[...] = input_grad(r.branch, 4, width // 2).astype(bf16)
    red.free(4)
    for q in g.chunks_of(4):
        g.settle(q)

    span = quarter // (slots // 2)

    def cross_pair(i, carry):
        cols = pl.ds(pl.multiple_of(i * LANES, LANES), LANES)
        vcols = pl.ds(pl.multiple_of(i * LANES + pool_half, LANES), LANES)
        for b in range(slots // 2):
            two = [lax.rem(r.index[b, j], slots) for j in range(2)]
            rows = slice(b * span, (b + 1) * span)
            queries = stacked(r.cq[rows, cols], low, high) * bf16(HEAD**-0.5)
            grads = stacked(r.mixed_grad[rows, cols], low, high)
            keys = jnp.concatenate([r.pool[t, :, cols] for t in two], 0)
            values = jnp.concatenate([r.pool[t, :, vcols] for t in two], 0)
            probs = jnp.exp(dot(keys, queries, NT) - r.lse_cross[i, b : b + 1])
            grad_probs = dot(values, grads, NT)
            score_grad = (probs * (grad_probs - jnp.sum(probs * grad_probs, 0, keepdims=True))).astype(bf16)
            r.gkv[b, :, cols] = dot(score_grad, queries).astype(bf16)
            r.gkv[b, :, vcols] = dot(probs.astype(bf16), grads).astype(bf16)
            gq = dot(score_grad, keys, TN) * HEAD**-0.5
            r.cq_grad[rows, cols] = jnp.where(low_lane, gq[:span], gq[span:]).astype(bf16)
        return carry

    for i in range(0, pairs, 2):
        lax.fori_loop(i, i + 2, cross_pair, 0)
        red.push()
    swap.send("gcq", half(r.cq_grad, o, width // 2), r.by_cq_grad)
    grad_two = input_grad(r.cq_grad, 3, width // 2)
    red.free(3)
    for q in g.chunks_of(3):
        g.settle(q)
    back, dg, db = norm_back_at(grad_two, r.first[...], gain(1))
    keep_vec(1, dg, db)
    grad_first = r.second[...] + back
    r.first[...] = grad_first
    r.self_branch[...] = grad_first.astype(bf16)
    swap.send("gsb", half(r.self_branch, o, width // 2), r.by_self_branch)
    r.mixed_grad[...] = input_grad(r.self_branch, 2, width // 2).astype(bf16)
    red.free(2)
    for q in g.chunks_of(2):
        g.settle(q)
    swap.wait("gcb")
    swap.wait("cm")
    plain_grad(4, r.cm, r.by_cm, r.branch, r.by_branch, width // 2)
    for s in range(slots):
        j = 0
        for k in range(slots):
            j = jnp.where(lax.rem(r.index[k // 2, k % 2], slots) == s, k, j)
        b, odd = lax.div(j, 2), lax.rem(j, 2)
        r.pool[s] = jnp.where(odd == 0, r.gkv[b, :rows_n], r.gkv[b, rows_n:])
    swap.send("gp", r.pool.at[:, :, pl.ds(pl.multiple_of(o * pool_half, LANES), pool_half)], r.by_pool_grad)

    cosine, signed = r.rope[0, :, :LANES], r.rope[0, :, LANES:]
    place = lax.broadcasted_iota(jnp.int32, (1, quarter), 1) + p.s * quarter
    limit = jnp.maximum(place, r.prefix[0] - 1)
    group, groups = width, 2
    each = pairs // groups

    def self_pair(i, carry):
        cols = pl.ds(pl.multiple_of(i * LANES, LANES), LANES)
        vcols = pl.ds(pl.multiple_of(i * LANES + pool_half, LANES), LANES)
        start = lax.div(i, each) * group + lax.rem(i, each) * LANES
        keys = r.kv[:, :, cols].reshape(-1, LANES)
        values = r.kv[:, :, vcols].reshape(-1, LANES)
        key_grad = value_grad = 0.0
        query_grads = []
        for e, lanes in enumerate((low, high)):
            queries = r.q[:, cols] * (lanes * bf16(HEAD**-0.5))
            grads = r.mixed_grad[:, cols] * lanes
            scores = dot(keys, queries, NT)
            key_place = lax.broadcasted_iota(jnp.int32, scores.shape, 0)
            logsum = r.lse[i, :, e * quarter : (e + 1) * quarter]
            probs = jnp.exp(jnp.where(key_place <= limit, scores, masked) - logsum)
            grad_probs = dot(values, grads, NT)
            score_grad = (probs * (grad_probs - jnp.sum(probs * grad_probs, 0, keepdims=True))).astype(bf16)
            key_grad = key_grad + dot(score_grad, queries)
            value_grad = value_grad + dot(probs.astype(bf16), grads)
            query_grads.append(dot(score_grad, keys, TN))
        for offset, part in ((0, key_grad), (group // 2, value_grad)):
            there = pl.ds(pl.multiple_of(start + offset, LANES), LANES)
            r.gkv[:, :, there] = part.astype(bf16).reshape(4, quarter, LANES)
        query_grad = jnp.where(low_lane, *query_grads) * HEAD**-0.5
        r.q[:, cols] = rotate(query_grad, cosine, -signed).astype(bf16)
        return carry

    for i in range(groups):
        for j in range(each):
            lax.fori_loop(i * each + j, i * each + j + 1, self_pair, 0)
            red.push()
        cols = pl.ds(i * group, group)
        swap.send(f"far{i}", r.gkv.at[p.s_d, :, cols], r.by_act.at[:, cols])
        swap.send(f"near{i}", r.gkv.at[p.s_c, :, cols], r.by_act.at[:, pl.ds((groups + i) * group, group)])
    swap.send("gq", half(r.q, o, width // 2), r.by_q_grad)
    swap.wait("gcq")
    swap.wait("n2")
    plain_grad(3, r.n2, r.by_n2, r.cq_grad, r.by_cq_grad, width // 2)
    for i in range(groups):
        cols = slice(i * group, (i + 1) * group)
        for j, (name, s, other) in enumerate((("near", p.s, groups + i), ("far", p.s_y, i))):
            swap.wait(f"{name}{i}")
            total = r.gkv[s, :, cols].astype(f32) + r.by_act[:, other * group : (other + 1) * group].astype(f32)
            total = jnp.concatenate([turned(total[:, : group // 2], j, -1), total[:, group // 2 :]], 1)
            r.gkv[s, :, cols] = total.astype(bf16)
    half_kv = pl.ds(pl.multiple_of(o * group, LANES), group)
    for j, (name, s) in enumerate((("gkv", p.s), ("gkvy", p.s_y))):
        swap.send(name, r.gkv.at[s, :, half_kv], r.by_hidden_grad.at[:, pl.ds(j * group, group)])
    red.push()
    part = width // 2

    def kv_grads(cols):
        return jnp.concatenate([r.gkv[s, :, cols] for s in (p.s, p.s_y)], 0)

    grad_one = sum(dot(kv_grads(slice(h * group, (h + 1) * group)), half_of(w[0], h, part, group), NT) for h in range(2))
    r.mixed_grad[...] = grad_one[quarter:].astype(bf16)
    to_y = remote(r.mixed_grad, r.one_y, kv_sem.at[0], kv_sem.at[1], p.to_y)
    to_y.start()
    r.second[...] = grad_one[:quarter] + sum(
        dot(r.q[:, h * part : (h + 1) * part], half_of(w[0], h, 0, part), NT) for h in range(2)
    )
    red.free(0)
    for q in g.chunks_of(0):
        g.settle(q)
    for name in ("gq", "n1", "gkv", "gkvy"):
        swap.wait(name)
    first_chunk, *kv_chunks, vec_chunk = red.chunks_of(0)
    plain_grad(0, r.n1.at[:quarter], r.by_n1.at[:quarter], r.q, r.by_q_grad, part, chunks=[first_chunk])
    weight_grad(
        0,
        lambda cols: r.n1[:, cols],
        lambda cols: r.by_n1[:, cols],
        lambda start, n: kv_grads(pl.ds(pl.multiple_of(c * group + start - part, LANES), n)),
        lambda start, n: jnp.concatenate(
            [r.by_hidden_grad[:, j * group + start - part : j * group + start - part + n] for j in range(2)], 0
        ),
        3 * part,
        chunks=kv_chunks,
    )
    swap.wait("gsb")
    swap.wait("att")
    plain_grad(2, r.att, r.by_att, r.self_branch, r.by_self_branch, width // 2)

    out = [None, None]
    for s in range(slots):
        rows = r.pool[s]
        slot_grad = sum(
            dot(rows[:, h * pool_half : (h + 1) * pool_half], half_of(w[1], h), NT) for h in range(2)
        )
        if out[s % 2] is not None:
            out[s % 2].wait()
        stage = r.tokens_grad.at[(s % 2) * rows_n : (s % 2 + 1) * rows_n]
        stage[...] = slot_grad
        out[s % 2] = pltpu.make_async_copy(stage, r.neighbours_grad.at[s], r.out_sem.at[s % 2])
        out[s % 2].start()
        if s == slots // 2:
            red.push()
    red.free(1)
    for q in g.chunks_of(1):
        g.settle(q)
    swap.wait("gp")
    swap.wait("nb")
    size = slots * rows_n
    weight_grad(
        1,
        lambda cols: r.neighbours[:, :, cols].reshape(size, -1),
        lambda cols: r.by_neighbours[:, :, cols].reshape(size, -1),
        lambda start, n: r.pool[:, :, pl.ds(pl.multiple_of(c * pool_half + start, LANES), n)].reshape(size, -1),
        lambda start, n: r.by_pool_grad[:, :, start : start + n].reshape(size, -1),
        pool_half,
    )
    to_y.wait_recv()
    grad_one = r.second[...] + r.one_y[...].astype(f32)
    back, dg, db = norm_back_at(grad_one, r.tokens[...].astype(f32), gain(0))
    keep_vec(0, dg, db)
    for cp in out:
        cp.wait()
    r.tokens_grad[...] = r.first[...] + back
    swap.send("vec", r.vec_sum, r.by_vec)
    swap.wait("vec")
    vec = jnp.concatenate([r.vec_sum[...] + r.by_vec[...], jnp.zeros((LANES - 8, width), f32)], 0)
    w[0][c, :, :, :, 3 * part :] = jnp.transpose(vec).astype(bf16).reshape(p.nz, 4, -1, LANES)
    red.push(vec_chunk)
    red.drain()
    for cp in (*red.sent, *swap.sent, to_y):
        cp.wait_send()


def rope_table(length):
    half = HEAD // 2
    freq = (10000.0 ** (-np.arange(half, dtype=np.float32) / half)).astype(np.float32)
    angles = np.arange(length, dtype=np.float32)[:, None] * freq[None, :]
    cosine, sine = np.cos(angles), np.sin(angles)
    table = np.concatenate([cosine] * 4 + [-sine, sine] * 2, 1)
    return table.astype(np.float32).reshape(4, -1, 2 * LANES)


def deliver_kernel(*refs):
    n = 10
    sources, outs, held = refs[:n], refs[n : 2 * n + 1], refs[2 * n + 1 : 3 * n + 1]
    arrive, leave = refs[3 * n + 1 :]
    taken = [pltpu.make_async_copy(sources[i], held[i], arrive.at[i]) for i in range(n)]
    for cp in taken:
        cp.start()
    left = []

    def put(src, dst):
        left.append(pltpu.make_async_copy(src, dst, leave.at[len(left)]))
        left[-1].start()

    for i in range(n):
        taken[i].wait()
        if i < 3:
            put(held[i], outs[i])
            continue
        parts = 3 if i == 3 else 1
        part = outs[i].shape[1] // (2 * parts)
        for h in range(2):
            for j in range(parts):
                put(held[i].at[h, :, j * part : (j + 1) * part], outs[i].at[:, (2 * j + h) * part : (2 * j + h + 1) * part])
        if i == 3:
            rows = held[i].shape[1]
            vectors = jnp.concatenate([held[i][0, :, parts * part :], jnp.zeros((LANES - rows, LANES), f32)], 0)
            outs[n][...] = jnp.transpose(vectors)[:8, :rows]
    for cp in left:
        cp.wait()


def deliver(out, tokens_grad, neighbours_grad, summed):
    rows = summed[0].shape[1]
    widths = [2 * v.shape[2] for v in summed]
    widths[0] -= 2 * LANES
    shapes = [out, tokens_grad, neighbours_grad] + [
        jax.ShapeDtypeStruct((v.shape[1], n), f32) for v, n in zip(summed, widths)
    ]
    vmem, hbm = pl.BlockSpec(memory_space=pltpu.VMEM), pl.BlockSpec(memory_space=pltpu.HBM)
    sources = (out, tokens_grad, neighbours_grad, *summed)
    out, tokens_grad, neighbours_grad, *grads, vectors = pl.pallas_call(
        deliver_kernel,
        out_shape=[jax.ShapeDtypeStruct(v.shape, v.dtype) for v in shapes] + [jax.ShapeDtypeStruct((8, rows), f32)],
        in_specs=[hbm] * 10,
        out_specs=[hbm] * 10 + [vmem],
        scratch_shapes=[pltpu.VMEM(v.shape, v.dtype) for v in sources]
        + [pltpu.SemaphoreType.DMA((10,)), pltpu.SemaphoreType.DMA((21,))],
        compiler_params=pltpu.CompilerParams(vmem_limit_bytes=64 * 2**20 - 2**17),
        name="deliver",
    )(*sources)
    return (
        out[None],
        tokens_grad[None],
        neighbours_grad[None],
        grads[0],
        grads[2],
        grads[3],
        grads[1],
        grads[4],
        grads[5],
        grads[6],
        *(vectors[i] for i in (0, 3, 1, 4, 2, 5)),
    )


class Refs:
    def take(self, names, refs):
        for name, ref in zip(names, refs, strict=True):
            setattr(self, name, ref)


NAMES_IN = (
    "w_qkv",
    "w_cross_kv",
    "w_out",
    "w_cross_q",
    "w_cross_out",
    "w_up",
    "w_down",
    "vectors",
    "tokens",
    "cotangent",
    "prefix",
    "neighbours",
    "index",
    "rope_table",
)
NAMES_OUT = ("out", "tokens_grad", "neighbours_grad")
GATHER = (
    (0, 768, 512, 2),
    (0, 384, 384, 2),
    (0, 0, 384, 2),
    (1, 0, 384, 2),
    (1, 384, 384, 2),
    (2, 0, 384, 2),
    (3, 0, 384, 2),
    (4, 0, 384, 2),
    (5, 0, 384, 2),
    (5, 384, 384, 2),
    (5, 768, 384, 2),
    (5, 1152, 384, 2),
    (6, 0, 128, 2),
    (6, 128, 128, 2),
    (6, 256, 128, 2),
)
REDUCE = (
    (6, 0, 256, 2),
    (6, 256, 128, 2),
    (5, 0, 512, 2),
    (5, 512, 512, 2),
    (5, 1024, 512, 2),
    (4, 0, 384, 2),
    (3, 0, 384, 2),
    (2, 0, 384, 2),
    (1, 0, 384, 2),
    (1, 384, 384, 2),
    (0, 0, 384, 2),
    (0, 384, 384, 2),
    (0, 768, 384, 2),
    (0, 1152, 128, 2),
)


def memory(nz, quarter, width, hidden, slots, rows_n, rows):
    halves = (3 * width // 2 + LANES, width, width // 2, width // 2, width // 2, hidden // 2)
    weights = [((2, nz, 4, 2 * rows, h), bf16) for h in halves]
    weights.append(((2, nz, 4, hidden // (4 * nz), width // 2), bf16))
    sums = [((2, rows, h), f32) for h in halves]
    sums.append(((2, hidden // (8 * nz), width // 2), f32))
    tok, half_tok = ((quarter, width), bf16), ((quarter, width // 2), bf16)
    half_hidden = ((quarter, hidden // 2), bf16)
    pool_half = ((slots, rows_n, width), bf16)
    kv = ((quarter, 2 * width), bf16)
    arrays = dict(
        pack=((2, rows, sum(halves)), f32),
        beside=((rows, sum(halves)), f32),
        down_sum=weights[6],
        down_beside=((hidden // (8 * nz), width // 2), f32),
        rope=((2, quarter, 2 * LANES), f32),
        n1=((2 * quarter, width), bf16),
        q=tok,
        kv=((4, *kv[0]), bf16),
        att=tok,
        lse=((width // LANES, 1, 2 * quarter), f32),
        first=((quarter, width), f32),
        n2=tok,
        cq=tok,
        pool=((slots, rows_n, 2 * width), bf16),
        lse_cross=((width // LANES, 8, LANES), f32),
        cm=tok,
        second=((quarter, width), f32),
        n3=tok,
        act=((quarter, hidden), bf16),
        slope=((quarter, hidden), bf16),
        vec=((8, width), f32),
        branch=tok,
        mixed_grad=tok,
        cq_grad=tok,
        self_branch=tok,
        one_y=tok,
        gkv=((4, *kv[0]), bf16),
        vec_sum=((8, width), f32),
        by_act=((quarter, hidden), bf16),
        by_cot=half_tok,
        by_n3=tok,
        by_hidden_grad=half_hidden,
        by_cm=tok,
        by_branch=half_tok,
        by_neighbours=pool_half,
        by_pool_grad=pool_half,
        by_n2=tok,
        by_cq_grad=half_tok,
        by_att=tok,
        by_self_branch=half_tok,
        by_n1=((2 * quarter, width), bf16),
        by_q_grad=half_tok,
        by_vec=((8, width), f32),
    )
    return weights, arrays, sums


def layer_kernel(nz, names, *refs):
    refs = list(refs)
    r = Refs()

    def some(n):
        taken = refs[:n]
        del refs[:n]
        return taken

    r.take(NAMES_IN, some(len(NAMES_IN)))
    r.take(NAMES_OUT, some(len(NAMES_OUT)))
    r.sums, r.w = some(7), some(7)
    r.take(names, some(len(names)))
    r.pair_sem, r.rope_sem, r.out_sem, fkv_sem, kv_sem, swap_sem, g_send, g_recv, r_send, r_recv, r.credit = refs
    p = Place(nz)
    g = Gather(p, r.w, GATHER, g_send, g_recv)
    swap = Swap(p, swap_sem)
    pairs = r.tokens.shape[1] // LANES
    down_part, turned, sent = forward(p, r, g, swap, fkv_sem, pairs)
    red = Reduce(p, r, REDUCE, r_send, r_recv)
    backward(p, r, g, swap, red, kv_sem, pairs, down_part, turned)
    for cp in sent:
        cp.wait_send()


def local_fast(
    tokens,
    prefix_len,
    neighbours,
    neighbour_index,
    w_qkv,
    w_out,
    w_cross_q,
    w_cross_kv,
    w_cross_out,
    w_up,
    w_down,
    gain_one,
    shift_one,
    gain_two,
    shift_two,
    gain_three,
    shift_three,
    cotangent,
):
    nz = lax.axis_size("dp") // 2
    quarter, width = tokens.shape[1:]
    rows, hidden = w_up.shape
    slots, rows_n = neighbours.shape[1:3]
    vectors = jnp.stack([gain_one, gain_two, gain_three, shift_one, shift_two, shift_three])
    weights, arrays, sums = memory(nz, quarter, width, hidden, slots, rows_n, rows)
    vmem, smem, anywhere = (pl.BlockSpec(memory_space=m) for m in (pltpu.VMEM, pltpu.SMEM, pl.ANY))
    made = [((quarter, width), bf16), ((quarter, width), f32), ((slots, rows_n, width), f32), *sums]
    dma = pltpu.SemaphoreType.DMA
    out, tokens_grad, neighbours_grad, *summed = pl.pallas_call(
        functools.partial(layer_kernel, nz, tuple(arrays)),
        out_shape=[jax.ShapeDtypeStruct(*v) for v in made],
        in_specs=[vmem] * 10 + [smem, vmem, smem, anywhere],
        out_specs=[vmem, vmem, anywhere] + [vmem] * len(sums),
        scratch_shapes=[pltpu.VMEM(*v) for v in (*weights, *arrays.values())]
        + [
            dma((6,)),
            dma((2,)),
            dma((2,)),
            dma((2, 2)),
            dma((2,)),
            dma((2, 28)),
            dma((len(GATHER), 14)),
            dma((len(GATHER), 14)),
            dma((len(REDUCE), 8)),
            dma((len(REDUCE), 8)),
            pltpu.SemaphoreType.REGULAR((7,)),
        ],
        compiler_params=pltpu.CompilerParams(
            collective_id=0, has_side_effects=True, vmem_limit_bytes=64 * 2**20 - 2**17
        ),
    )(
        w_qkv, w_cross_kv, w_out, w_cross_q, w_cross_out, w_up, w_down, vectors,
        tokens[0], cotangent[0], prefix_len, neighbours[0],
        neighbour_index[0], jnp.asarray(rope_table(4 * quarter)),
    )
    return deliver(out, tokens_grad, neighbours_grad, summed)


def pick_slots(pool, index):
    return jnp.stack(
        [
            jnp.concatenate([lax.dynamic_slice_in_dim(pool[s], index[s, j], 1, 0) for j in range(index.shape[1])], 0)
            for s in range(index.shape[0])
        ]
    )


def slot_places(index):
    slots = index.shape[1]
    same = index[:, :, None] == jnp.arange(slots)[None, None, :]
    return jnp.sum(jnp.where(same, jnp.arange(slots)[None, :, None], 0), 1)


def dense_dot(left_side, weight):
    return jnp.dot(left_side, weight, preferred_element_type=jnp.float32)


def input_grad(grad_out, weight):
    return lax.dot_general(
        grad_out,
        weight,
        (((grad_out.ndim - 1,), (1,)), ((), ())),
        preferred_element_type=jnp.float32,
    )


def weight_grad(left_side, grad_out):
    flat_left = left_side.reshape(-1, left_side.shape[-1])
    flat_grad = grad_out.reshape(-1, grad_out.shape[-1])
    return lax.dot_general(
        flat_left, flat_grad, (((0,), (0,)), ((), ())), preferred_element_type=jnp.float32
    )


def plain_norm_parts(array_in):
    avg_value = jnp.mean(array_in, -1, keepdims=True)
    centred = array_in - avg_value
    inv_std = lax.rsqrt(jnp.mean(centred * centred, -1, keepdims=True) + eps)
    return (centred * inv_std, inv_std)


def norm_back(grad_out, unit_part, inv_std, gain_f):
    scaled = grad_out * gain_f
    grad_in = inv_std * (
        scaled
        - jnp.mean(scaled, -1, keepdims=True)
        - unit_part * jnp.mean(scaled * unit_part, -1, keepdims=True)
    )
    return (grad_in, jnp.sum(grad_out * unit_part, (0, 1)), jnp.sum(grad_out, (0, 1)))


def rotary_tables(positions):
    half_size = HEAD // 2
    frequency = 10000.0 ** (-jnp.arange(half_size).astype(jnp.float32) / half_size)
    angles = positions.astype(jnp.float32)[:, None] * frequency[None, :]
    return (jnp.cos(angles)[:, None, :], jnp.sin(angles)[:, None, :])


def plain_rotate(array_in, cosine, sine_part):
    half_size = HEAD // 2
    first_half = array_in[..., :half_size]
    second = array_in[..., half_size:]
    return jnp.concatenate(
        [first_half * cosine - second * sine_part, second * cosine + first_half * sine_part], -1
    )


def unrotate(grad_in, cosine, sine_part):
    half_size = HEAD // 2
    first_half = grad_in[..., :half_size]
    second = grad_in[..., half_size:]
    return jnp.concatenate(
        [first_half * cosine + second * sine_part, second * cosine - first_half * sine_part], -1
    )


def grouped(array_in):
    split_heads = array_in.reshape(
        array_in.shape[0], array_in.shape[1], array_in.shape[2] // 4, 4, array_in.shape[3]
    )
    return jnp.moveaxis(split_heads, 2, 0)


def ungrouped(array_in):
    shifted_axes = jnp.moveaxis(array_in, 0, 2)
    return shifted_axes.reshape(
        shifted_axes.shape[0], shifted_axes.shape[1], -1, shifted_axes.shape[-1]
    )


def masked_scores(visible, queries, key_rows):
    scores = jnp.einsum(
        "sqhd,skhd->shqk", queries, key_rows, preferred_element_type=jnp.float32
    ) * HEAD ** (-0.5)
    return jnp.where(visible[:, None], scores, masked)


def attend_group(visible, packed):
    queries, key_rows, values = packed
    scores = masked_scores(visible, queries, key_rows)
    row_max = jnp.max(scores, -1, keepdims=True)
    exp_scores = jnp.exp(scores - row_max)
    row_total = jnp.sum(exp_scores, -1, keepdims=True)
    probabilities = (exp_scores / row_total).astype(jnp.bfloat16)
    mixed_out = jnp.einsum(
        "shqk,skhd->sqhd", probabilities, values, preferred_element_type=jnp.float32
    )
    return (mixed_out, (row_max + jnp.log(row_total))[..., 0])


def attend_back(visible, packed):
    queries, key_rows, values, grad_out, logsum = packed
    scores = masked_scores(visible, queries, key_rows)
    probabilities = jnp.exp(scores - logsum[..., None])
    grad_probs = jnp.einsum("sqhd,skhd->shqk", grad_out, values, preferred_element_type=jnp.float32)
    grad_scores = (
        probabilities * (grad_probs - jnp.sum(probabilities * grad_probs, -1, keepdims=True))
    ).astype(jnp.bfloat16)
    grad_query = jnp.einsum(
        "shqk,skhd->sqhd", grad_scores, key_rows, preferred_element_type=jnp.float32
    ) * HEAD ** (-0.5)
    grad_key = jnp.einsum(
        "shqk,sqhd->skhd", grad_scores, queries, preferred_element_type=jnp.float32
    ) * HEAD ** (-0.5)
    grad_value = jnp.einsum(
        "shqk,sqhd->skhd",
        probabilities.astype(jnp.bfloat16),
        grad_out,
        preferred_element_type=jnp.float32,
    )
    return (grad_query, grad_key, grad_value)


def local_plain(
    tokens,
    prefix_len,
    neighbours,
    neighbour_index,
    w_qkv,
    w_out,
    w_cross_q,
    w_cross_kv,
    w_cross_out,
    w_up,
    w_down,
    gain_one,
    shift_one,
    gain_two,
    shift_two,
    gain_three,
    shift_three,
    cotangent,
):
    forward_set = (
        lax.all_gather(w_qkv, ("dp", "seq"), axis=0, tiled=True),
        lax.all_gather(w_out, ("dp", "seq"), axis=0, tiled=True),
        lax.all_gather(w_cross_q, ("dp", "seq"), axis=0, tiled=True),
        lax.all_gather(w_cross_kv, ("dp", "seq"), axis=0, tiled=True),
        lax.all_gather(w_cross_out, ("dp", "seq"), axis=0, tiled=True),
        lax.all_gather(w_up, ("dp", "seq"), axis=0, tiled=True),
        lax.all_gather(w_down, ("dp", "seq"), axis=0, tiled=True),
        lax.all_gather(gain_one, ("dp", "seq"), axis=0, tiled=True),
        lax.all_gather(shift_one, ("dp", "seq"), axis=0, tiled=True),
        lax.all_gather(gain_two, ("dp", "seq"), axis=0, tiled=True),
        lax.all_gather(shift_two, ("dp", "seq"), axis=0, tiled=True),
        lax.all_gather(gain_three, ("dp", "seq"), axis=0, tiled=True),
        lax.all_gather(shift_three, ("dp", "seq"), axis=0, tiled=True),
    )
    (
        full_qkv,
        full_out,
        full_cross_q,
        full_cross_kv,
        full_cross_out,
        full_up,
        full_down,
        full_gain_one,
        full_shift_one,
        full_gain_two,
        full_shift_two,
        full_gain_three,
        full_shift_three,
    ) = forward_set
    seq_here, quarter, width = tokens.shape
    heads = width // HEAD
    hidden_width = full_up.shape[1]
    length = quarter * lax.axis_size("seq")
    seq_index = lax.axis_index("seq")
    query_pos = seq_index * quarter + jnp.arange(quarter)
    key_pos = jnp.arange(length)
    visible = (key_pos[None, None, :] <= query_pos[None, :, None]) | (
        key_pos[None, None, :] < prefix_len[:, None, None]
    )
    cosine, sine_part = rotary_tables(query_pos)
    gain_f1 = full_gain_one.astype(jnp.float32)
    gain_f2 = full_gain_two.astype(jnp.float32)
    gain_f3 = full_gain_three.astype(jnp.float32)
    resid_in = tokens.astype(jnp.float32)
    unit_one, inv_one = plain_norm_parts(resid_in)
    normed_one = (unit_one * gain_f1 + full_shift_one.astype(jnp.float32)).astype(jnp.bfloat16)
    joined = dense_dot(normed_one, full_qkv)
    query_rot = plain_rotate(
        joined[..., :width].reshape(seq_here, quarter, heads, HEAD), cosine, sine_part
    ).astype(jnp.bfloat16)
    key_local = (
        plain_rotate(
            joined[..., width : 2 * width].reshape(seq_here, quarter, heads, HEAD),
            cosine,
            sine_part,
        )
        .astype(jnp.bfloat16)
        .reshape(seq_here, quarter, width)
    )
    value_local = joined[..., 2 * width :].astype(jnp.bfloat16)
    key_all, value_all = (
        lax.all_gather(key_local, "seq", axis=1, tiled=True),
        lax.all_gather(value_local, "seq", axis=1, tiled=True),
    )
    key_heads = key_all.reshape(seq_here, length, heads, HEAD)
    value_heads = value_all.reshape(seq_here, length, heads, HEAD)
    attended, logsum = lax.map(
        functools.partial(attend_group, visible),
        (grouped(query_rot), grouped(key_heads), grouped(value_heads)),
    )
    attended = ungrouped(attended).reshape(seq_here, quarter, width).astype(jnp.bfloat16)
    first_sum = resid_in + dense_dot(attended, full_out)
    unit_two, inv_two = plain_norm_parts(first_sum)
    normed_two = (unit_two * gain_f2 + full_shift_two.astype(jnp.float32)).astype(jnp.bfloat16)
    cross_query = dense_dot(normed_two, full_cross_q).astype(jnp.bfloat16)
    pool_kv = dense_dot(neighbours, full_cross_kv).astype(jnp.bfloat16)
    slots = neighbours.shape[1]
    spans = slots // 2
    span_len = quarter // spans
    neighbour_rows = 2 * neighbours.shape[2]
    local_index = neighbour_index.reshape(seq_here, slots) - seq_index * slots
    picked = pick_slots(pool_kv, local_index)
    picked = picked.reshape(seq_here, spans, neighbour_rows, 2 * width)
    cross_keys = picked[..., :width].reshape(seq_here, spans, neighbour_rows, heads, HEAD)
    cross_values = picked[..., width:].reshape(seq_here, spans, neighbour_rows, heads, HEAD)
    cross_queries = cross_query.reshape(seq_here, spans, span_len, heads, HEAD)
    cross_scores = jnp.einsum(
        "scqhd,sckhd->schqk", cross_queries, cross_keys, preferred_element_type=jnp.float32
    ) * HEAD ** (-0.5)
    cross_probs = jax.nn.softmax(cross_scores, -1)
    cross_weights = cross_probs.astype(jnp.bfloat16)
    cross_mixed = jnp.einsum(
        "schqk,sckhd->scqhd", cross_weights, cross_values, preferred_element_type=jnp.float32
    )
    cross_mixed = cross_mixed.reshape(seq_here, quarter, width).astype(jnp.bfloat16)
    second_sum = first_sum + dense_dot(cross_mixed, full_cross_out)
    unit_three, inv_three = plain_norm_parts(second_sum)
    normed_three = (unit_three * gain_f3 + full_shift_three.astype(jnp.float32)).astype(
        jnp.bfloat16
    )
    hidden_pre = dense_dot(normed_three, full_up)
    activated = jax.nn.gelu(hidden_pre, approximate=False).astype(jnp.bfloat16)
    output = (second_sum + dense_dot(activated, full_down)).astype(jnp.bfloat16)
    grad_act = input_grad(cotangent, full_down)
    _, gelu_back = jax.vjp(functools.partial(jax.nn.gelu, approximate=False), hidden_pre)
    grad_hidden = gelu_back(grad_act)[0].astype(jnp.bfloat16)
    grad_normed_three = input_grad(grad_hidden, full_up)
    back_three, grad_gain_three, grad_shift_three = norm_back(
        grad_normed_three, unit_three, inv_three, full_gain_three.astype(jnp.float32)
    )
    grad_second = cotangent.astype(jnp.float32) + back_three
    grad_cross_branch = grad_second.astype(jnp.bfloat16)
    grad_mixed = (
        input_grad(grad_cross_branch, full_cross_out)
        .astype(jnp.bfloat16)
        .reshape(seq_here, spans, span_len, heads, HEAD)
    )
    grad_cross_probs = jnp.einsum(
        "scqhd,sckhd->schqk", grad_mixed, cross_values, preferred_element_type=jnp.float32
    )
    grad_cross_scores = (
        cross_probs
        * (grad_cross_probs - jnp.sum(cross_probs * grad_cross_probs, -1, keepdims=True))
    ).astype(jnp.bfloat16)
    grad_cross_query = (
        (
            jnp.einsum(
                "schqk,sckhd->scqhd",
                grad_cross_scores,
                cross_keys,
                preferred_element_type=jnp.float32,
            )
            * HEAD ** (-0.5)
        )
        .astype(jnp.bfloat16)
        .reshape(seq_here, quarter, width)
    )
    grad_cross_keys = jnp.einsum(
        "schqk,scqhd->sckhd", grad_cross_scores, cross_queries, preferred_element_type=jnp.float32
    ) * HEAD ** (-0.5)
    grad_cross_values = jnp.einsum(
        "schqk,scqhd->sckhd", cross_weights, grad_mixed, preferred_element_type=jnp.float32
    )
    grad_picked = jnp.concatenate(
        [
            grad_cross_keys.reshape(seq_here, spans, neighbour_rows, width),
            grad_cross_values.reshape(seq_here, spans, neighbour_rows, width),
        ],
        -1,
    )
    grad_picked = grad_picked.reshape(seq_here, slots, neighbours.shape[2], 2 * width)
    grad_pool_kv = pick_slots(grad_picked.astype(jnp.bfloat16), slot_places(local_index))
    grad_neighbours = input_grad(grad_pool_kv, full_cross_kv)
    grad_normed_two = input_grad(grad_cross_query, full_cross_q)
    back_two, grad_gain_two, grad_shift_two = norm_back(
        grad_normed_two, unit_two, inv_two, full_gain_two.astype(jnp.float32)
    )
    grad_first = grad_second + back_two
    grad_self_branch = grad_first.astype(jnp.bfloat16)
    grad_attended = (
        input_grad(grad_self_branch, full_out)
        .astype(jnp.bfloat16)
        .reshape(seq_here, quarter, heads, HEAD)
    )
    grad_query, grad_key_all, grad_value_all = lax.map(
        functools.partial(attend_back, visible),
        (
            grouped(query_rot),
            grouped(key_heads),
            grouped(value_heads),
            grouped(grad_attended),
            logsum,
        ),
    )
    grad_query = ungrouped(grad_query)
    grad_key_all = ungrouped(grad_key_all).reshape(seq_here, length, width)
    grad_value_all = ungrouped(grad_value_all).reshape(seq_here, length, width)
    grad_key, grad_value = (
        lax.psum_scatter(
            grad_key_all.astype(jnp.bfloat16), "seq", scatter_dimension=1, tiled=True
        ).astype(jnp.float32),
        lax.psum_scatter(
            grad_value_all.astype(jnp.bfloat16), "seq", scatter_dimension=1, tiled=True
        ).astype(jnp.float32),
    )
    grad_joined = jnp.concatenate(
        [
            unrotate(grad_query, cosine, sine_part).reshape(seq_here, quarter, width),
            unrotate(grad_key.reshape(seq_here, quarter, heads, HEAD), cosine, sine_part).reshape(
                seq_here, quarter, width
            ),
            grad_value,
        ],
        -1,
    ).astype(jnp.bfloat16)
    grad_normed_one = input_grad(grad_joined, full_qkv)
    back_one, grad_gain_one, grad_shift_one = norm_back(
        grad_normed_one, unit_one, inv_one, full_gain_one.astype(jnp.float32)
    )
    grad_tokens = grad_first + back_one
    norm_grads = jnp.stack(
        [
            grad_gain_one,
            grad_shift_one,
            grad_gain_two,
            grad_shift_two,
            grad_gain_three,
            grad_shift_three,
        ],
        1,
    )
    width_owned = lax.psum_scatter(
        jnp.concatenate(
            [
                weight_grad(normed_one, grad_joined),
                weight_grad(attended, grad_self_branch),
                weight_grad(normed_two, grad_cross_query),
                weight_grad(neighbours, grad_pool_kv),
                weight_grad(cross_mixed, grad_cross_branch),
                weight_grad(normed_three, grad_hidden),
                norm_grads,
            ],
            1,
        ),
        ("dp", "seq"),
        scatter_dimension=0,
        tiled=True,
    )
    down_owned = lax.psum_scatter(
        weight_grad(activated, cotangent), ("dp", "seq"), scatter_dimension=0, tiled=True
    )
    column = 8 * width + hidden_width
    return (
        output,
        grad_tokens,
        grad_neighbours,
        width_owned[:, : 3 * width],
        width_owned[:, 3 * width : 4 * width],
        width_owned[:, 4 * width : 5 * width],
        width_owned[:, 5 * width : 7 * width],
        width_owned[:, 7 * width : 8 * width],
        width_owned[:, 8 * width : column],
        down_owned,
        width_owned[:, column],
        width_owned[:, column + 1],
        width_owned[:, column + 2],
        width_owned[:, column + 3],
        width_owned[:, column + 4],
        width_owned[:, column + 5],
    )


def solution(mesh):
    sizes = dict(mesh.shape)
    fits = sizes == {"dp": 8, "seq": 4}
    return jax.shard_map(
        local_fast if fits else local_plain,
        mesh=mesh,
        in_specs=(
            P("dp", "seq", None),
            P("dp"),
            P("dp", "seq", None, None),
            P("dp", "seq", None),
            P(("dp", "seq"), None),
            P(("dp", "seq"), None),
            P(("dp", "seq"), None),
            P(("dp", "seq"), None),
            P(("dp", "seq"), None),
            P(("dp", "seq"), None),
            P(("dp", "seq"), None),
            P(("dp", "seq")),
            P(("dp", "seq")),
            P(("dp", "seq")),
            P(("dp", "seq")),
            P(("dp", "seq")),
            P(("dp", "seq")),
            P("dp", "seq", None),
        ),
        out_specs=(
            P("dp", "seq", None),
            P("dp", "seq", None),
            P("dp", "seq", None, None),
            P(("dp", "seq"), None),
            P(("dp", "seq"), None),
            P(("dp", "seq"), None),
            P(("dp", "seq"), None),
            P(("dp", "seq"), None),
            P(("dp", "seq"), None),
            P(("dp", "seq"), None),
            P(("dp", "seq")),
            P(("dp", "seq")),
            P(("dp", "seq")),
            P(("dp", "seq")),
            P(("dp", "seq")),
            P(("dp", "seq")),
        ),
        check_vma=False,
    )
```

```python
import functools
import math

import jax
import jax.numpy as jnp
import numpy as np
from jax import lax
from jax.experimental import pallas as pl
from jax.experimental.pallas import tpu as pltpu
from jax.sharding import PartitionSpec as P

HEAD = 64
eps = 1e-05
masked = -1e30
MESH = pl.DeviceIdType.MESH
bf16 = jnp.bfloat16
f32 = jnp.float32
NN = (((1,), (0,)), ((), ()))
NT = (((1,), (1,)), ((), ()))
TN = (((0,), (0,)), ((), ()))
LANES = 128
AHEAD = 3
SPREAD = 3
ACROSS, LAST = 2, 4


def dot(a, b, dims=NN):
    return lax.dot_general(a, b, dims, preferred_element_type=f32)


def norm_parts(v):
    centred = v - jnp.mean(v, -1, keepdims=True)
    inv = lax.rsqrt(jnp.mean(centred * centred, -1, keepdims=True) + eps)
    return centred * inv, inv


class Place:
    def __init__(self, nz):
        dp, s = lax.axis_index("dp"), lax.axis_index("seq")
        self.nz, self.dp, self.s = nz, dp, s
        self.z, self.x = lax.div(dp, 2), lax.rem(dp, 2)
        self.y, self.c = lax.div(s, 2), lax.rem(s, 2)
        x, y, z, c = self.x, self.y, self.z, self.c
        self.o = 1 - c
        self.own, self.at_x, self.at_y, self.at_d = (
            x * 2 + y,
            (1 - x) * 2 + y,
            x * 2 + 1 - y,
            (1 - x) * 2 + 1 - y,
        )
        self.to_z = [(lax.rem(z + j, nz) * 2 + x, s) for j in range(1, nz)]
        self.z_of = [lax.rem(z + j, nz) for j in range(1, nz)]
        self.z_from = [lax.rem(z - j + nz, nz) for j in range(1, nz)]
        self.to_x = (z * 2 + 1 - x, s)
        self.to_y = (dp, (1 - y) * 2 + c)
        self.to_c = (dp, y * 2 + 1 - c)
        self.s_y = (1 - y) * 2 + c
        self.s_c = y * 2 + 1 - c
        self.s_d = (1 - y) * 2 + 1 - c

    def meet(self):
        barrier = pltpu.get_barrier_semaphore()
        friends = [*self.to_z, self.to_x, self.to_y, self.to_c]
        for device in friends:
            pl.semaphore_signal(barrier, inc=1, device_id=device, device_id_type=MESH)
        pl.semaphore_wait(barrier, len(friends))


def remote(src, dst, send, recv, device):
    return pltpu.make_async_remote_copy(
        src_ref=src, dst_ref=dst, send_sem=send, recv_sem=recv, device_id=device, device_id_type=MESH
    )


class Gather:
    def __init__(self, place, weights, chunks, send, recv):
        self.p, self.w, self.chunks, self.ss, self.rs = place, weights, chunks, send, recv
        self.sent = [[] for _ in chunks]
        self.t, self.have = 0, set()
        self.z_first = [q for q, v in enumerate(chunks) if v[3] > 0]
        self.plane_first = [q for q, v in enumerate(chunks) if v[3] <= 0]

    def chunks_of(self, k):
        return [q for q, v in enumerate(self.chunks) if v[0] == k]

    def begin(self):
        self.along_z(self.z_first[0])

    def tick(self):
        t, order = self.t, self.z_first
        n = len(order)
        if t >= n + LAST:
            return
        if t == 0:
            for q in order[1:AHEAD]:
                self.along_z(q)
            for q in self.plane_first:
                self.plane_out(q)
        if t < n:
            self.along_xy(order[t])
        if t + AHEAD < n:
            self.along_z(order[t + AHEAD])
        if t == 1:
            for q in self.plane_first:
                self.plane_across(q)
        if t >= 2 and (t - 2) % SPREAD == 0 and (t - 2) // SPREAD < len(self.plane_first):
            self.plane_z(self.plane_first[(t - 2) // SPREAD])
        if 0 <= t - ACROSS < n:
            self.across(order[t - ACROSS])
        if 0 <= t - LAST < n:
            self.last(order[t - LAST])
        self.t += 1

    def need(self, q):
        if q in self.plane_first:
            while self.t <= SPREAD * self.plane_first.index(q) + 2:
                self.tick()
        else:
            while self.t <= self.z_first.index(q) + LAST:
                self.tick()
        if q not in self.have:
            self.have.add(q)
            if q in self.plane_first:
                self.plane_last(q)
                self.plane_ready(q)
            else:
                self.ready(q)

    def plane_out(self, q):
        p = self.p
        mine = self.part(q, p.c, p.z, p.own)
        for j, device in ((3, p.to_x), (4, p.to_y), (7, p.to_c)):
            self.send(q, j, mine, device)

    def plane_across(self, q):
        p = self.p
        from_x, from_y = self.part(q, p.c, p.z, p.at_x), self.part(q, p.c, p.z, p.at_y)
        self.wait(q, 3, from_x)
        self.send(q, 8, from_x, p.to_c)
        self.wait(q, 4, from_y)
        self.send(q, 9, from_y, p.to_c)
        if self.chunks[q][3] == 0:
            self.send(q, 5, from_y, p.to_x)
        else:
            self.send(q, 5, from_x, p.to_y)

    def plane_z(self, q):
        p, every = self.p, slice(None)
        diag = self.part(q, p.c, p.z, p.at_d)
        self.wait(q, 5, diag)
        self.send(q, 10, diag, p.to_c)
        for j, device in enumerate(p.to_z):
            self.send(q, j, self.part(q, p.c, p.z, every), device)

    def plane_last(self, q):
        p, every = self.p, slice(None)
        for j, z in enumerate(p.z_from):
            ref = self.part(q, p.c, z, every)
            self.wait(q, j, ref)
            self.send(q, 11 + j, ref, p.to_c)

    def plane_ready(self, q):
        p, every = self.p, slice(None)
        for j, xy in ((7, p.own), (8, p.at_x), (9, p.at_y), (10, p.at_d)):
            self.wait(q, j, self.part(q, p.o, p.z, xy))
        for j, z in enumerate(p.z_from):
            self.wait(q, 11 + j, self.part(q, p.o, z, every))

    def part(self, q, half, z, xy):
        k, start, width, _ = self.chunks[q]
        return self.w[k].at[half, z, xy, :, pl.ds(start, width)]

    def copy(self, q, j, ref, device):
        return remote(ref, ref, self.ss.at[q, j], self.rs.at[q, j], device)

    def send(self, q, j, ref, device):
        cp = self.copy(q, j, ref, device)
        cp.start()
        self.sent[q].append(cp)

    def wait(self, q, j, ref):
        self.copy(q, j, ref, self.p.to_c).wait_recv()

    def along_z(self, q):
        p = self.p
        for j, device in enumerate(p.to_z):
            self.send(q, j, self.part(q, p.c, p.z, p.own), device)

    def along_xy(self, q):
        p, allz = self.p, slice(None)
        for j, z in enumerate(p.z_from):
            self.wait(q, j, self.part(q, p.c, z, p.own))
        mine = self.part(q, p.c, allz, p.own)
        self.send(q, 3, mine, p.to_x)
        self.send(q, 4, mine, p.to_y)
        self.send(q, 7, mine, p.to_c)

    def across(self, q):
        p, allz, cut = self.p, slice(None), self.chunks[q][3]
        from_x, from_y = self.part(q, p.c, allz, p.at_x), self.part(q, p.c, allz, p.at_y)
        self.wait(q, 3, from_x)
        self.send(q, 5, self.part(q, p.c, pl.ds(0, cut), p.at_x), p.to_y)
        self.send(q, 8, from_x, p.to_c)
        self.wait(q, 4, from_y)
        self.send(q, 6, self.part(q, p.c, pl.ds(cut, p.nz - cut), p.at_y), p.to_x)
        self.send(q, 9, from_y, p.to_c)

    def last(self, q):
        p, cut = self.p, self.chunks[q][3]
        for j, z in ((5, pl.ds(0, cut)), (6, pl.ds(cut, p.nz - cut))):
            ref = self.part(q, p.c, z, p.at_d)
            self.wait(q, j, ref)
            self.send(q, j + 5, ref, p.to_c)

    def ready(self, q):
        p, allz, cut = self.p, slice(None), self.chunks[q][3]
        for j, z, xy in (
            (7, allz, p.own),
            (8, allz, p.at_x),
            (9, allz, p.at_y),
            (10, pl.ds(0, cut), p.at_d),
            (11, pl.ds(cut, p.nz - cut), p.at_d),
        ):
            self.wait(q, j, self.part(q, p.o, z, xy))

    def settle(self, q):
        for cp in self.sent[q]:
            cp.wait_send()
        self.sent[q] = []


def half_of(w, h, start=None, width=None):
    v = w[h] if start is None else w[h, :, :, :, pl.ds(start, width)]
    return v.reshape(-1, v.shape[-1])


def lane_masks():
    lane = lax.broadcasted_iota(jnp.int32, (1, LANES), 1)
    low = lane < HEAD
    return low, jnp.where(low, 1.0, 0.0).astype(bf16), jnp.where(low, 0.0, 1.0).astype(bf16)


def stacked(v, low, high):
    return jnp.concatenate([v * low, v * high], 0)


def swap_halves(v):
    lane = lax.broadcasted_iota(jnp.int32, v.shape, 1)
    first = lax.rem(lane, HEAD) < HEAD // 2
    return jnp.where(first, pltpu.roll(v, LANES - HEAD // 2, 1), pltpu.roll(v, HEAD // 2, 1))


def rotate(v, cosine, signed):
    return v * cosine + swap_halves(v) * signed


def forward(p, r, g, swap, kv_sem, pairs):
    n = len(g.chunks)
    c, z = p.c, p.z
    w = r.w

    vectors = r.vectors[...].astype(f32)
    count, rows = vectors.shape
    vectors = jnp.concatenate([vectors, jnp.zeros((count, LANES - rows), f32)], 1)
    vectors = jnp.concatenate([vectors, jnp.zeros((LANES - count, LANES), f32)], 0)
    vectors = jnp.transpose(vectors)[:rows]
    start = 0
    for k, ref in enumerate((r.w_qkv, r.w_cross_kv, r.w_out, r.w_cross_q, r.w_cross_out, r.w_up)):
        rows = ref[...].astype(f32)
        size = rows.shape[1] // 2
        for h in range(2):
            parts = 3 if k == 0 else 1
            part = size // parts
            for i in range(parts):
                source = i * 2 * part + h * part
                r.pack[h, :, start + i * part : start + (i + 1) * part] = rows[:, source : source + part]
            if k == 0:
                r.pack[h, :, start + size : start + size + LANES] = vectors
        start += w[k].shape[-1]
    p.meet()
    first = remote(r.pack.at[p.o], r.beside, r.pair_sem.at[0], r.pair_sem.at[1], p.to_c)
    first.start()
    down_rows, down_half = r.w_down.shape[0], w[6].shape[-1]
    down_at = pl.ds(pl.multiple_of(c * down_rows, 16), down_rows)
    down = remote(
        r.w_down.at[:, pl.ds(pl.multiple_of(p.o * down_half, LANES), down_half)],
        w[6].at[p.o, z, p.own, down_at],
        r.pair_sem.at[2],
        r.pair_sem.at[3],
        p.to_c,
    )
    down.start()
    tokens_y = remote(r.tokens, r.branch, r.pair_sem.at[4], r.pair_sem.at[5], p.to_y)
    tokens_y.start()
    ropes = [pltpu.make_async_copy(r.rope_table.at[s], r.rope.at[i], r.rope_sem.at[i]) for i, s in enumerate((p.s, p.s_y))]
    for rope in ropes:
        rope.start()
    w[6][c, z, p.own, down_at] = r.w_down[:, pl.ds(pl.multiple_of(c * down_half, LANES), down_half)]
    first.wait_recv()
    start = 0
    for k in range(6):
        width = w[k].shape[-1]
        mine, other = r.pack[c, :, start : start + width], r.beside[:, start : start + width]
        top, low = jnp.where(c == 0, mine, other), jnp.where(c == 0, other, mine)
        w[k][c, z, p.own] = jnp.concatenate([top, low], 0).astype(bf16)
        start += width
        if k == 0:
            g.begin()
    down.wait_recv()
    g.tick()
    swap.send("cot", r.cotangent.at[:, pl.ds(pl.multiple_of(p.o * down_half, LANES), down_half)], r.by_cot)
    swap.send("nb", r.neighbours, r.by_neighbours)
    for rope in ropes:
        rope.wait()
    tokens = r.tokens[...].astype(f32)
    quarter, width = tokens.shape
    unit, _ = norm_parts(tokens)
    g.tick()
    tokens_y.wait_recv()
    unit_y, _ = norm_parts(r.branch[...].astype(f32))
    g.need(0)
    part = width // 2
    r.vec[...] = jnp.transpose(half_of(w[0], 0, 3 * part, LANES).astype(f32))[:8]

    def affine(v, i):
        return (v * r.vec[i : i + 1] + r.vec[3 + i : 4 + i]).astype(bf16)

    r.n1[:quarter] = affine(unit, 0)
    r.n1[quarter:] = affine(unit_y, 0)
    swap.send("n1", r.n1, r.by_n1)
    for h in range(2):
        value = dot(r.n1[...], half_of(w[0], h, 2 * part, part)).astype(bf16)
        cols = slice(width + h * part, width + (h + 1) * part)
        r.kv[p.s, :, cols] = value[:quarter]
        r.kv[p.s_y, :, cols] = value[quarter:]

    def turned(v, i, sign=1):
        cosine, signed = r.rope[i, :, :LANES], r.rope[i, :, LANES:]
        return jnp.concatenate(
            [rotate(v[:, b : b + LANES], cosine, sign * signed) for b in range(0, v.shape[1], LANES)], 1
        )

    g.need(1)
    for h in range(2):
        key = dot(r.n1[...], half_of(w[0], h, part, part))
        cols = slice(h * part, (h + 1) * part)
        r.kv[p.s, :, cols] = turned(key[:quarter], 0).astype(bf16)
        r.kv[p.s_y, :, cols] = turned(key[quarter:], 1).astype(bf16)
    kv_sent = [
        remote(r.kv.at[s], r.kv.at[s], kv_sem.at[0, i], kv_sem.at[1, i], p.to_c) for i, s in enumerate((p.s, p.s_y))
    ]
    for cp in kv_sent:
        cp.start()
    g.need(2)
    for h in range(2):
        query = dot(r.n1[:quarter], half_of(w[0], h, 0, part))
        r.q[:, h * part : (h + 1) * part] = turned(query, 0).astype(bf16)
    g.need(3)
    g.need(4)

    def pool_rows(i, carry):
        rows = r.neighbours[pl.ds(i * 2, 2)].reshape(-1, r.neighbours.shape[2])
        for h in range(2):
            width = w[1].shape[-1]
            r.pool[pl.ds(i * 2, 2), :, h * width : (h + 1) * width] = (
                dot(rows, half_of(w[1], h)).astype(bf16).reshape(2, -1, width)
            )
        return carry

    lax.fori_loop(0, 2, pool_rows, 0)
    g.tick()
    lax.fori_loop(2, r.neighbours.shape[0] // 2, pool_rows, 0)
    for i, s in enumerate((p.s_c, p.s_d)):
        remote(r.kv.at[s], r.kv.at[s], kv_sem.at[0, i], kv_sem.at[1, i], p.to_c).wait_recv()

    low_lane, low, high = lane_masks()
    place = lax.broadcasted_iota(jnp.int32, (1, quarter), 1) + p.s * quarter
    limit = jnp.maximum(place, r.prefix[0] - 1)

    def self_pair(i, carry):
        cols = pl.ds(pl.multiple_of(i * LANES, LANES), LANES)
        vcols = pl.ds(pl.multiple_of(i * LANES + w[1].shape[-1], LANES), LANES)
        keys = r.kv[:, :, cols].reshape(-1, LANES)
        values = r.kv[:, :, vcols].reshape(-1, LANES)
        mixed = []
        for e, lanes in enumerate((low, high)):
            scores = dot(keys, r.q[:, cols] * (lanes * bf16(HEAD**-0.5)), NT)
            key_place = lax.broadcasted_iota(jnp.int32, scores.shape, 0)
            scores = jnp.where(key_place <= limit, scores, masked)
            top = jnp.max(scores, 0, keepdims=True)
            exped = jnp.exp(scores - top)
            total = jnp.sum(exped, 0, keepdims=True)
            weights = (exped * (1.0 / total)).astype(bf16)
            r.lse[i, :, e * quarter : (e + 1) * quarter] = top + jnp.log(total)
            mixed.append(dot(weights, values, TN))
        r.att[:, cols] = jnp.where(low_lane, *mixed).astype(bf16)
        return carry

    for i in range(0, pairs, 2):
        lax.fori_loop(i, i + 2, self_pair, 0)
        g.tick()
    g.need(5)

    def project(v, k):
        return jnp.concatenate([dot(v, half_of(w[k], h)) for h in range(2)], 1)

    swap.send("att", r.att, r.by_att)
    first_sum = tokens + project(r.att[...], 2)
    r.first[...] = first_sum
    r.n2[...] = affine(norm_parts(first_sum)[0], 1)
    swap.send("n2", r.n2, r.by_n2)
    g.need(6)
    r.cq[...] = project(r.n2[...], 3).astype(bf16)
    slots = r.neighbours.shape[0]
    span = quarter // (slots // 2)

    def cross_pair(i, carry):
        cols = pl.ds(pl.multiple_of(i * LANES, LANES), LANES)
        vcols = pl.ds(pl.multiple_of(i * LANES + w[1].shape[-1], LANES), LANES)
        for b in range(slots // 2):
            two = [lax.rem(r.index[b, j], slots) for j in range(2)]
            rows = slice(b * span, (b + 1) * span)
            queries = stacked(r.cq[rows, cols], low, high) * bf16(HEAD**-0.5)
            keys = jnp.concatenate([r.pool[t, :, cols] for t in two], 0)
            values = jnp.concatenate([r.pool[t, :, vcols] for t in two], 0)
            scores = dot(keys, queries, NT)
            top = jnp.max(scores, 0, keepdims=True)
            e = jnp.exp(scores - top)
            total = jnp.sum(e, 0, keepdims=True)
            weights = (e * (1.0 / total)).astype(bf16)
            r.lse_cross[i, b : b + 1] = top + jnp.log(total)
            mixed = dot(weights, values, TN)
            r.cm[rows, cols] = jnp.where(low_lane, mixed[:span], mixed[span:]).astype(bf16)
        return carry

    lax.fori_loop(0, pairs // 2, cross_pair, 0)
    g.tick()
    lax.fori_loop(pairs // 2, pairs, cross_pair, 0)
    g.need(7)
    swap.send("cm", r.cm, r.by_cm)
    second_sum = r.first[...] + project(r.cm[...], 4)
    r.second[...] = second_sum
    r.n3[...] = affine(norm_parts(second_sum)[0], 2)
    swap.send("n3", r.n3, r.by_n3)
    hidden_half = w[5].shape[-1]

    def up_tile(start, size):
        def body(h, carry):
            hidden = dot(r.n3[...], half_of(w[5], h, start, size))
            cdf = 0.5 * (1.0 + lax.erf(hidden * (0.5**0.5)))
            density = jnp.exp(-0.5 * hidden * hidden) * ((2 * math.pi) ** -0.5)
            cols = pl.ds(pl.multiple_of(h * hidden_half + start, LANES), size)
            r.act[:, cols] = (hidden * cdf).astype(bf16)
            r.slope[:, cols] = (cdf + hidden * density).astype(bf16)
            return carry

        lax.fori_loop(0, 2, body, 0)

    for q, (k, start, size, _) in enumerate(g.chunks):
        if k == 5:
            g.need(q)
            up_tile(start, size)
    swap.send("act", r.act, r.by_act)

    def down_part(q):
        _, start, size, _ = g.chunks[q]
        for h in range(2):
            cols = slice(h * down_half + start, h * down_half + start + size)
            r.out[:, cols] = (r.second[:, cols] + dot(r.act[...], half_of(w[6], h, start, size))).astype(bf16)

    return down_part, turned, (first, down, tokens_y, *kv_sent)


LAGS = (6, 5, 3)


class Reduce:
    def __init__(self, place, r, chunks, send, recv):
        self.p, self.r, self.w, self.chunks, self.ss, self.rs = place, r, r.w, chunks, send, recv
        self.sent, self.open, self.under_way, self.phase = [], set(), {}, 0
        self.starts = [sum(v.shape[-1] for v in r.w[:k]) for k in range(7)]

    def free(self, k):
        p = self.p
        for device in (p.to_x, p.to_y, *p.to_z):
            pl.semaphore_signal(self.r.credit.at[k], inc=1, device_id=device, device_id_type=MESH)

    def array(self, k, half):
        if k == 6:
            return self.r.down_sum, 0 if half is self.p.c else 1
        return self.w[k], half

    def at(self, q, half, z, xy):
        k, start, width, _ = self.chunks[q]
        ref, lead = self.array(k, half)
        return ref.at[lead, z, xy, :, pl.ds(start, width)]

    def load(self, q, half, z, xy):
        k, start, width, _ = self.chunks[q]
        ref, lead = self.array(k, half)
        return ref[lead, z, xy, :, start : start + width].astype(f32)

    def save(self, q, half, z, xy, v):
        k, start, width, _ = self.chunks[q]
        ref, lead = self.array(k, half)
        ref[lead, z, xy, :, start : start + width] = v.astype(bf16)

    def copy(self, q, j, src, dst, device):
        cp = remote(src, dst, self.ss.at[q, j], self.rs.at[q, j], device)
        cp.start()
        self.sent.append(cp)

    def wait(self, q, j, ref):
        remote(ref, ref, self.ss.at[q, j], self.rs.at[q, j], self.p.to_c).wait_recv()

    def diagonal(self, q):
        p, cut = self.p, self.chunks[q][3]
        for j, z, device in ((0, pl.ds(0, cut), p.to_y), (1, pl.ds(cut, p.nz - cut), p.to_x)):
            self.copy(q, j, self.at(q, p.c, z, p.at_d), self.at(q, p.o, z, 0), device)

    def across(self, q):
        p, cut, allz = self.p, self.chunks[q][3], slice(None)
        for j, zs, to in ((0, range(cut), p.at_x), (1, range(cut, p.nz), p.at_y)):
            self.wait(q, j, self.at(q, p.o, pl.ds(zs[0], len(zs)), 0))
            for z in zs:
                self.save(q, p.c, z, to, self.load(q, p.c, z, to) + self.load(q, p.o, z, 0))
        self.copy(q, 2, self.at(q, p.c, allz, p.at_x), self.at(q, p.o, allz, 1), p.to_x)
        self.copy(q, 3, self.at(q, p.c, allz, p.at_y), self.at(q, p.o, allz, 2), p.to_y)

    def along_z(self, q):
        p, allz = self.p, slice(None)
        self.wait(q, 2, self.at(q, p.o, allz, 1))
        self.wait(q, 3, self.at(q, p.o, allz, 2))
        for z in range(p.nz):
            total = self.load(q, p.c, z, p.own) + self.load(q, p.o, z, 1) + self.load(q, p.o, z, 2)
            self.save(q, p.c, z, p.own, total)
        for j, device in enumerate(p.to_z):
            self.copy(q, 4 + j, self.at(q, p.c, p.z_of[j], p.own), self.at(q, p.o, j, 3), device)

    def steps(self, q):
        if self.chunks[q][3] > 0:
            return self.diagonal, self.across, self.along_z, self.last
        return self.z_out, self.plane_diagonal, self.plane_across, self.plane_last

    def z_out(self, q):
        p, every = self.p, slice(None)
        for j, device in enumerate(p.to_z):
            self.copy(q, 4 + j, self.at(q, p.c, p.z_of[j], every), self.at(q, p.o, j, every), device)

    def plane_diagonal(self, q):
        p, every = self.p, slice(None)
        for j in range(p.nz - 1):
            self.wait(q, 4 + j, self.at(q, p.o, j, every))
        for xy in range(4):
            total = self.load(q, p.c, p.z, xy)
            for j in range(p.nz - 1):
                total = total + self.load(q, p.o, j, xy)
            self.save(q, p.c, p.z, xy, total)
        device = p.to_x if self.chunks[q][3] == 0 else p.to_y
        self.copy(q, 0, self.at(q, p.c, p.z, p.at_d), self.at(q, p.o, p.nz - 1, 0), device)

    def plane_across(self, q):
        p, there = self.p, self.p.nz - 1
        to = p.at_y if self.chunks[q][3] == 0 else p.at_x
        self.wait(q, 0, self.at(q, p.o, there, 0))
        self.save(q, p.c, p.z, to, self.load(q, p.c, p.z, to) + self.load(q, p.o, there, 0))
        self.copy(q, 2, self.at(q, p.c, p.z, p.at_x), self.at(q, p.o, there, 1), p.to_x)
        self.copy(q, 3, self.at(q, p.c, p.z, p.at_y), self.at(q, p.o, there, 2), p.to_y)

    def plane_last(self, q):
        p, there = self.p, self.p.nz - 1
        total = self.load(q, p.c, p.z, p.own)
        for j in (1, 2):
            self.wait(q, 1 + j, self.at(q, p.o, there, j))
            total = total + self.load(q, p.o, there, j)
        self.hand_over(q, total)

    def last(self, q):
        p = self.p
        total = self.load(q, p.c, p.z, p.own)
        for j in range(p.nz - 1):
            self.wait(q, 4 + j, self.at(q, p.o, j, 3))
            total = total + self.load(q, p.o, j, 3)
        self.hand_over(q, total)

    def hand_over(self, q, total):
        p, r, (k, start, width, _) = self.p, self.r, self.chunks[q]
        cols = slice(start, start + width)
        rows = total.shape[0] // 2
        r.sums[k][p.c, :, cols] = jnp.where(p.c == 0, total[:rows], total[rows:])
        if k == 6:
            mine = r.down_beside.at[:, cols]
        else:
            mine = r.beside.at[:, self.starts[k] + start : self.starts[k] + start + width]
        mine[...] = jnp.where(p.c == 0, total[rows:], total[:rows])
        self.copy(q, 7, mine, r.sums[k].at[p.c, :, cols], p.to_c)

    def finish(self, q):
        p, (k, start, width, _) = self.p, self.chunks[q]
        self.wait(q, 7, self.r.sums[k].at[p.o, :, pl.ds(start, width)])

    def push(self, q=None, lag=None):
        lag = lag or LAGS[self.phase]
        for other in list(self.under_way):
            stage, age = self.under_way[other]
            if age + 1 < lag:
                self.under_way[other] = stage, age + 1
                continue
            self.steps(other)[stage + 1](other)
            self.under_way[other] = stage + 1, 0
            if stage == 2:
                del self.under_way[other]
        if q is not None:
            k = self.chunks[q][0]
            if k not in self.open:
                pl.semaphore_wait(self.r.credit.at[k], 1 + self.p.nz)
                self.open.add(k)
            self.steps(q)[0](q)
            self.under_way[q] = 0, 0

    def chunks_of(self, k):
        return [q for q, v in enumerate(self.chunks) if v[0] == k]

    def drain(self):
        while self.under_way:
            self.push(None, 1)
        for q in range(len(self.chunks)):
            self.finish(q)


class Swap:
    def __init__(self, place, sems):
        self.p, self.sems, self.n, self.sent, self.landed = place, sems, 0, [], {}

    def send(self, name, src, dst):
        cp = remote(src, dst, self.sems.at[0, self.n], self.sems.at[1, self.n], self.p.to_c)
        cp.start()
        self.sent.append(cp)
        self.landed[name] = cp
        self.n += 1

    def wait(self, name):
        self.landed.pop(name).wait_recv()


def norm_back_at(grad, v, gain):
    unit, inv = norm_parts(v)
    scaled = grad * gain
    back = inv * (
        scaled - jnp.mean(scaled, -1, keepdims=True) - unit * jnp.mean(scaled * unit, -1, keepdims=True)
    )
    return back, jnp.sum(grad * unit, 0, keepdims=True), jnp.sum(grad, 0, keepdims=True)


def backward(p, r, g, swap, red, kv_sem, pairs, down_part, turned):
    w, c, o = r.w, p.c, p.o
    quarter, width = r.tokens.shape
    hidden_half, pool_half = w[5].shape[-1], w[1].shape[-1]
    slots, rows_n = r.neighbours.shape[:2]
    low_lane, low, high = lane_masks()
    r.vec_sum[...] = jnp.zeros_like(r.vec_sum)

    def half(ref, h, size):
        return ref.at[:, pl.ds(pl.multiple_of(h * size, LANES), size)]

    def input_grad(ref, k, size):
        return sum(dot(ref[:, h * size : (h + 1) * size], half_of(w[k], h, 0, size), NT) for h in range(2))

    def weight_grad(k, left, left_beside, right, right_beside, size, tile=384, chunks=None, push=True):
        into, lead = red.array(k, c)
        rows = into.shape[3]
        per = tile // (4 * rows)
        for q in red.chunks_of(k) if chunks is None else chunks:
            _, start, n, _ = red.chunks[q]
            n = min(n, size - start)

            def body(i, carry, start=start, n=n):
                cols = pl.ds(pl.multiple_of(i * tile, LANES), tile)
                part = dot(left(cols), right(start, n), TN) + dot(left_beside(cols), right_beside(start, n), TN)
                into[lead, pl.ds(i * per, per), :, :, start : start + n] = part.astype(bf16).reshape(per, 4, rows, n)
                return carry

            lax.fori_loop(0, p.nz // per, body, 0)
            if push:
                red.push(q)

    def plain_grad(k, left, left_beside, right, right_beside, size, tile=384, chunks=None, push=True):
        weight_grad(
            k,
            lambda cols: left[:, cols],
            lambda cols: left_beside[:, cols],
            lambda start, n: right[:, pl.ds(pl.multiple_of(c * size + start, LANES), n)],
            lambda start, n: right_beside[:, start : start + n],
            size,
            tile,
            chunks,
            push,
        )

    def gain(i):
        return r.vec[i : i + 1]

    def keep_vec(i, gain_sum, shift_sum):
        r.vec_sum[i : i + 1] = gain_sum
        r.vec_sum[3 + i : 4 + i] = shift_sum

    for name in ("cot", "act"):
        swap.wait(name)
    red.free(6)
    plain_grad(6, r.act, r.by_act, r.cotangent, r.by_cot, w[6].shape[-1], 4 * w[6].shape[3])
    for q in g.chunks_of(6):
        g.need(q)
        down_part(q)
        g.settle(q)
        red.push()
    down_half = w[6].shape[-1]

    def act_tile(z, carry):
        rows = 4 * w[6].shape[3]
        cols = pl.ds(pl.multiple_of(z * rows, LANES), rows)
        act_grad = sum(
            dot(r.cotangent[:, h * down_half : (h + 1) * down_half], w[6][h, z].reshape(rows, down_half), NT)
            for h in range(2)
        )
        r.slope[:, cols] = (act_grad * r.slope[:, cols].astype(f32)).astype(bf16)
        return carry

    lax.fori_loop(0, p.nz, act_tile, 0)
    gh = r.slope
    swap.send("gh", half(gh, o, hidden_half), r.by_hidden_grad)
    red.push()
    grad_three = input_grad(gh, 5, hidden_half)
    red.free(5)
    red.push()
    for q in g.chunks_of(5):
        g.settle(q)
    back, dg, db = norm_back_at(grad_three, r.second[...], gain(2))
    keep_vec(2, dg, db)
    grad_second = r.cotangent[...].astype(f32) + back
    r.second[...] = grad_second
    r.branch[...] = grad_second.astype(bf16)
    swap.send("gcb", half(r.branch, o, width // 2), r.by_branch)
    for name in ("gh", "n3"):
        swap.wait(name)
    plain_grad(5, r.n3, r.by_n3, gh, r.by_hidden_grad, hidden_half)
    r.mixed_grad[...] = input_grad(r.branch, 4, width // 2).astype(bf16)
    red.free(4)
    for q in g.chunks_of(4):
        g.settle(q)

    span = quarter // (slots // 2)

    def cross_pair(i, carry):
        cols = pl.ds(pl.multiple_of(i * LANES, LANES), LANES)
        vcols = pl.ds(pl.multiple_of(i * LANES + pool_half, LANES), LANES)
        for b in range(slots // 2):
            two = [lax.rem(r.index[b, j], slots) for j in range(2)]
            rows = slice(b * span, (b + 1) * span)
            queries = stacked(r.cq[rows, cols], low, high) * bf16(HEAD**-0.5)
            grads = stacked(r.mixed_grad[rows, cols], low, high)
            keys = jnp.concatenate([r.pool[t, :, cols] for t in two], 0)
            values = jnp.concatenate([r.pool[t, :, vcols] for t in two], 0)
            probs = jnp.exp(dot(keys, queries, NT) - r.lse_cross[i, b : b + 1])
            grad_probs = dot(values, grads, NT)
            score_grad = (probs * (grad_probs - jnp.sum(probs * grad_probs, 0, keepdims=True))).astype(bf16)
            r.gkv[b, :, cols] = dot(score_grad, queries).astype(bf16)
            r.gkv[b, :, vcols] = dot(probs.astype(bf16), grads).astype(bf16)
            gq = dot(score_grad, keys, TN) * HEAD**-0.5
            r.cq_grad[rows, cols] = jnp.where(low_lane, gq[:span], gq[span:]).astype(bf16)
        return carry

    for i in range(0, pairs, 2):
        lax.fori_loop(i, i + 2, cross_pair, 0)
        red.push()
    swap.send("gcq", half(r.cq_grad, o, width // 2), r.by_cq_grad)
    grad_two = input_grad(r.cq_grad, 3, width // 2)
    red.free(3)
    for q in g.chunks_of(3):
        g.settle(q)
    back, dg, db = norm_back_at(grad_two, r.first[...], gain(1))
    keep_vec(1, dg, db)
    grad_first = r.second[...] + back
    r.first[...] = grad_first
    r.self_branch[...] = grad_first.astype(bf16)
    swap.send("gsb", half(r.self_branch, o, width // 2), r.by_self_branch)
    r.mixed_grad[...] = input_grad(r.self_branch, 2, width // 2).astype(bf16)
    red.free(2)
    for q in g.chunks_of(2):
        g.settle(q)
    swap.wait("gcb")
    swap.wait("cm")
    plain_grad(4, r.cm, r.by_cm, r.branch, r.by_branch, width // 2)
    for s in range(slots):
        j = 0
        for k in range(slots):
            j = jnp.where(lax.rem(r.index[k // 2, k % 2], slots) == s, k, j)
        b, odd = lax.div(j, 2), lax.rem(j, 2)
        r.pool[s] = jnp.where(odd == 0, r.gkv[b, :rows_n], r.gkv[b, rows_n:])
    swap.send("gp", r.pool.at[:, :, pl.ds(pl.multiple_of(o * pool_half, LANES), pool_half)], r.by_pool_grad)

    cosine, signed = r.rope[0, :, :LANES], r.rope[0, :, LANES:]
    place = lax.broadcasted_iota(jnp.int32, (1, quarter), 1) + p.s * quarter
    limit = jnp.maximum(place, r.prefix[0] - 1)
    group, groups = width, 2
    each = pairs // groups

    def self_pair(i, carry):
        cols = pl.ds(pl.multiple_of(i * LANES, LANES), LANES)
        vcols = pl.ds(pl.multiple_of(i * LANES + pool_half, LANES), LANES)
        start = lax.div(i, each) * group + lax.rem(i, each) * LANES
        keys = r.kv[:, :, cols].reshape(-1, LANES)
        values = r.kv[:, :, vcols].reshape(-1, LANES)
        key_grad = value_grad = 0.0
        query_grads = []
        for e, lanes in enumerate((low, high)):
            queries = r.q[:, cols] * (lanes * bf16(HEAD**-0.5))
            grads = r.mixed_grad[:, cols] * lanes
            scores = dot(keys, queries, NT)
            key_place = lax.broadcasted_iota(jnp.int32, scores.shape, 0)
            logsum = r.lse[i, :, e * quarter : (e + 1) * quarter]
            probs = jnp.exp(jnp.where(key_place <= limit, scores, masked) - logsum)
            grad_probs = dot(values, grads, NT)
            score_grad = (probs * (grad_probs - jnp.sum(probs * grad_probs, 0, keepdims=True))).astype(bf16)
            key_grad = key_grad + dot(score_grad, queries)
            value_grad = value_grad + dot(probs.astype(bf16), grads)
            query_grads.append(dot(score_grad, keys, TN))
        for offset, part in ((0, key_grad), (group // 2, value_grad)):
            there = pl.ds(pl.multiple_of(start + offset, LANES), LANES)
            r.gkv[:, :, there] = part.astype(bf16).reshape(4, quarter, LANES)
        query_grad = jnp.where(low_lane, *query_grads) * HEAD**-0.5
        r.q[:, cols] = rotate(query_grad, cosine, -signed).astype(bf16)
        return carry

    for i in range(groups):
        for j in range(each):
            lax.fori_loop(i * each + j, i * each + j + 1, self_pair, 0)
            red.push()
        cols = pl.ds(i * group, group)
        swap.send(f"far{i}", r.gkv.at[p.s_d, :, cols], r.by_act.at[:, cols])
        swap.send(f"near{i}", r.gkv.at[p.s_c, :, cols], r.by_act.at[:, pl.ds((groups + i) * group, group)])
    red.phase = 1
    swap.send("gq", half(r.q, o, width // 2), r.by_q_grad)
    swap.wait("gcq")
    swap.wait("n2")
    plain_grad(3, r.n2, r.by_n2, r.cq_grad, r.by_cq_grad, width // 2)
    for i in range(groups):
        cols = slice(i * group, (i + 1) * group)
        for j, (name, s, other) in enumerate((("near", p.s, groups + i), ("far", p.s_y, i))):
            swap.wait(f"{name}{i}")
            total = r.gkv[s, :, cols].astype(f32) + r.by_act[:, other * group : (other + 1) * group].astype(f32)
            total = jnp.concatenate([turned(total[:, : group // 2], j, -1), total[:, group // 2 :]], 1)
            r.gkv[s, :, cols] = total.astype(bf16)
    half_kv = pl.ds(pl.multiple_of(o * group, LANES), group)
    for j, (name, s) in enumerate((("gkv", p.s), ("gkvy", p.s_y))):
        swap.send(name, r.gkv.at[s, :, half_kv], r.by_hidden_grad.at[:, pl.ds(j * group, group)])
    red.push()
    part = width // 2

    def kv_grads(cols):
        return jnp.concatenate([r.gkv[s, :, cols] for s in (p.s, p.s_y)], 0)

    grad_one = sum(dot(kv_grads(slice(h * group, (h + 1) * group)), half_of(w[0], h, part, group), NT) for h in range(2))
    r.mixed_grad[...] = grad_one[quarter:].astype(bf16)
    to_y = remote(r.mixed_grad, r.one_y, kv_sem.at[0], kv_sem.at[1], p.to_y)
    to_y.start()
    r.second[...] = grad_one[:quarter] + sum(
        dot(r.q[:, h * part : (h + 1) * part], half_of(w[0], h, 0, part), NT) for h in range(2)
    )
    red.free(0)
    for q in g.chunks_of(0):
        g.settle(q)
    for name in ("gq", "n1", "gkv", "gkvy"):
        swap.wait(name)
    first_chunk, *kv_chunks, vec_chunk = red.chunks_of(0)
    plain_grad(0, r.n1.at[:quarter], r.by_n1.at[:quarter], r.q, r.by_q_grad, part, chunks=[first_chunk])
    weight_grad(
        0,
        lambda cols: r.n1[:, cols],
        lambda cols: r.by_n1[:, cols],
        lambda start, n: kv_grads(pl.ds(pl.multiple_of(c * group + start - part, LANES), n)),
        lambda start, n: jnp.concatenate(
            [r.by_hidden_grad[:, j * group + start - part : j * group + start - part + n] for j in range(2)], 0
        ),
        3 * part,
        chunks=kv_chunks,
    )
    swap.wait("gsb")
    swap.wait("att")
    plain_grad(2, r.att, r.by_att, r.self_branch, r.by_self_branch, width // 2)

    out = [None, None]
    for s in range(slots):
        rows = r.pool[s]
        slot_grad = sum(
            dot(rows[:, h * pool_half : (h + 1) * pool_half], half_of(w[1], h), NT) for h in range(2)
        )
        if out[s % 2] is not None:
            out[s % 2].wait()
        stage = r.tokens_grad.at[(s % 2) * rows_n : (s % 2 + 1) * rows_n]
        stage[...] = slot_grad
        out[s % 2] = pltpu.make_async_copy(stage, r.neighbours_grad.at[s], r.out_sem.at[s % 2])
        out[s % 2].start()
        if s == slots // 2:
            red.push()
    red.phase = 2
    red.free(1)
    for q in g.chunks_of(1):
        g.settle(q)
    swap.wait("gp")
    swap.wait("nb")
    size = slots * rows_n
    weight_grad(
        1,
        lambda cols: r.neighbours[:, :, cols].reshape(size, -1),
        lambda cols: r.by_neighbours[:, :, cols].reshape(size, -1),
        lambda start, n: r.pool[:, :, pl.ds(pl.multiple_of(c * pool_half + start, LANES), n)].reshape(size, -1),
        lambda start, n: r.by_pool_grad[:, :, start : start + n].reshape(size, -1),
        pool_half,
    )
    to_y.wait_recv()
    grad_one = r.second[...] + r.one_y[...].astype(f32)
    back, dg, db = norm_back_at(grad_one, r.tokens[...].astype(f32), gain(0))
    keep_vec(0, dg, db)
    for cp in out:
        cp.wait()
    r.tokens_grad[...] = r.first[...] + back
    swap.send("vec", r.vec_sum, r.by_vec)
    swap.wait("vec")
    vec = jnp.concatenate([r.vec_sum[...] + r.by_vec[...], jnp.zeros((LANES - 8, width), f32)], 0)
    w[0][c, :, :, :, 3 * part :] = jnp.transpose(vec).astype(bf16).reshape(p.nz, 4, -1, LANES)
    red.push(vec_chunk)
    red.drain()
    for cp in (*red.sent, *swap.sent, to_y):
        cp.wait_send()


def rope_table(length):
    half = HEAD // 2
    freq = (10000.0 ** (-np.arange(half, dtype=np.float32) / half)).astype(np.float32)
    angles = np.arange(length, dtype=np.float32)[:, None] * freq[None, :]
    cosine, sine = np.cos(angles), np.sin(angles)
    table = np.concatenate([cosine] * 4 + [-sine, sine] * 2, 1)
    return table.astype(np.float32).reshape(4, -1, 2 * LANES)


def deliver_kernel(*refs):
    n = 10
    sources, outs, held = refs[:n], refs[n : 2 * n + 1], refs[2 * n + 1 : 3 * n + 1]
    arrive, leave = refs[3 * n + 1 :]
    taken = [pltpu.make_async_copy(sources[i], held[i], arrive.at[i]) for i in range(n)]
    for cp in taken:
        cp.start()
    left = []

    def put(src, dst):
        left.append(pltpu.make_async_copy(src, dst, leave.at[len(left)]))
        left[-1].start()

    for i in range(n):
        taken[i].wait()
        if i < 3:
            put(held[i], outs[i])
            continue
        parts = 3 if i == 3 else 1
        part = outs[i].shape[1] // (2 * parts)
        for h in range(2):
            for j in range(parts):
                put(held[i].at[h, :, j * part : (j + 1) * part], outs[i].at[:, (2 * j + h) * part : (2 * j + h + 1) * part])
        if i == 3:
            rows = held[i].shape[1]
            vectors = jnp.concatenate([held[i][0, :, parts * part :], jnp.zeros((LANES - rows, LANES), f32)], 0)
            outs[n][...] = jnp.transpose(vectors)[:8, :rows]
    for cp in left:
        cp.wait()


def deliver(out, tokens_grad, neighbours_grad, summed):
    rows = summed[0].shape[1]
    widths = [2 * v.shape[2] for v in summed]
    widths[0] -= 2 * LANES
    shapes = [out, tokens_grad, neighbours_grad] + [
        jax.ShapeDtypeStruct((v.shape[1], n), f32) for v, n in zip(summed, widths)
    ]
    vmem, hbm = pl.BlockSpec(memory_space=pltpu.VMEM), pl.BlockSpec(memory_space=pltpu.HBM)
    sources = (out, tokens_grad, neighbours_grad, *summed)
    out, tokens_grad, neighbours_grad, *grads, vectors = pl.pallas_call(
        deliver_kernel,
        out_shape=[jax.ShapeDtypeStruct(v.shape, v.dtype) for v in shapes] + [jax.ShapeDtypeStruct((8, rows), f32)],
        in_specs=[hbm] * 10,
        out_specs=[hbm] * 10 + [vmem],
        scratch_shapes=[pltpu.VMEM(v.shape, v.dtype) for v in sources]
        + [pltpu.SemaphoreType.DMA((10,)), pltpu.SemaphoreType.DMA((21,))],
        compiler_params=pltpu.CompilerParams(vmem_limit_bytes=64 * 2**20 - 2**17),
        name="deliver",
    )(*sources)
    return (
        out[None],
        tokens_grad[None],
        neighbours_grad[None],
        grads[0],
        grads[2],
        grads[3],
        grads[1],
        grads[4],
        grads[5],
        grads[6],
        *(vectors[i] for i in (0, 3, 1, 4, 2, 5)),
    )


class Refs:
    def take(self, names, refs):
        for name, ref in zip(names, refs, strict=True):
            setattr(self, name, ref)


NAMES_IN = (
    "w_qkv",
    "w_cross_kv",
    "w_out",
    "w_cross_q",
    "w_cross_out",
    "w_up",
    "w_down",
    "vectors",
    "tokens",
    "cotangent",
    "prefix",
    "neighbours",
    "index",
    "rope_table",
)
NAMES_OUT = ("out", "tokens_grad", "neighbours_grad")
GATHER = (
    (0, 768, 512, 2),
    (0, 384, 384, 2),
    (0, 0, 384, 2),
    (1, 0, 384, 2),
    (1, 384, 384, 2),
    (2, 0, 384, 2),
    (3, 0, 384, 2),
    (4, 0, 384, 2),
    (5, 0, 384, 2),
    (5, 384, 384, 2),
    (5, 768, 384, 2),
    (5, 1152, 384, 2),
    (6, 0, 128, 2),
    (6, 128, 128, 2),
    (6, 256, 128, 2),
)
REDUCE = (
    (6, 0, 128, 2),
    (6, 128, 128, 2),
    (6, 256, 128, 2),
    (5, 0, 384, 2),
    (5, 384, 384, 2),
    (5, 768, 384, 2),
    (5, 1152, 384, 2),
    (4, 0, 384, 2),
    (3, 0, 384, 2),
    (2, 0, 384, 2),
    (1, 0, 384, 2),
    (1, 384, 384, 2),
    (0, 0, 384, 2),
    (0, 384, 384, 2),
    (0, 768, 384, 2),
    (0, 1152, 128, 2),
)


def memory(nz, quarter, width, hidden, slots, rows_n, rows):
    halves = (3 * width // 2 + LANES, width, width // 2, width // 2, width // 2, hidden // 2)
    weights = [((2, nz, 4, 2 * rows, h), bf16) for h in halves]
    weights.append(((2, nz, 4, hidden // (4 * nz), width // 2), bf16))
    sums = [((2, rows, h), f32) for h in halves]
    sums.append(((2, hidden // (8 * nz), width // 2), f32))
    tok, half_tok = ((quarter, width), bf16), ((quarter, width // 2), bf16)
    half_hidden = ((quarter, hidden // 2), bf16)
    pool_half = ((slots, rows_n, width), bf16)
    kv = ((quarter, 2 * width), bf16)
    arrays = dict(
        pack=((2, rows, sum(halves)), f32),
        beside=((rows, sum(halves)), f32),
        down_sum=weights[6],
        down_beside=((hidden // (8 * nz), width // 2), f32),
        rope=((2, quarter, 2 * LANES), f32),
        n1=((2 * quarter, width), bf16),
        q=tok,
        kv=((4, *kv[0]), bf16),
        att=tok,
        lse=((width // LANES, 1, 2 * quarter), f32),
        first=((quarter, width), f32),
        n2=tok,
        cq=tok,
        pool=((slots, rows_n, 2 * width), bf16),
        lse_cross=((width // LANES, 8, LANES), f32),
        cm=tok,
        second=((quarter, width), f32),
        n3=tok,
        act=((quarter, hidden), bf16),
        slope=((quarter, hidden), bf16),
        vec=((8, width), f32),
        branch=tok,
        mixed_grad=tok,
        cq_grad=tok,
        self_branch=tok,
        one_y=tok,
        gkv=((4, *kv[0]), bf16),
        vec_sum=((8, width), f32),
        by_act=((quarter, hidden), bf16),
        by_cot=half_tok,
        by_n3=tok,
        by_hidden_grad=half_hidden,
        by_cm=tok,
        by_branch=half_tok,
        by_neighbours=pool_half,
        by_pool_grad=pool_half,
        by_n2=tok,
        by_cq_grad=half_tok,
        by_att=tok,
        by_self_branch=half_tok,
        by_n1=((2 * quarter, width), bf16),
        by_q_grad=half_tok,
        by_vec=((8, width), f32),
    )
    return weights, arrays, sums


def layer_kernel(nz, names, *refs):
    refs = list(refs)
    r = Refs()

    def some(n):
        taken = refs[:n]
        del refs[:n]
        return taken

    r.take(NAMES_IN, some(len(NAMES_IN)))
    r.take(NAMES_OUT, some(len(NAMES_OUT)))
    r.sums, r.w = some(7), some(7)
    r.take(names, some(len(names)))
    r.pair_sem, r.rope_sem, r.out_sem, fkv_sem, kv_sem, swap_sem, g_send, g_recv, r_send, r_recv, r.credit = refs
    p = Place(nz)
    g = Gather(p, r.w, GATHER, g_send, g_recv)
    swap = Swap(p, swap_sem)
    pairs = r.tokens.shape[1] // LANES
    down_part, turned, sent = forward(p, r, g, swap, fkv_sem, pairs)
    red = Reduce(p, r, REDUCE, r_send, r_recv)
    backward(p, r, g, swap, red, kv_sem, pairs, down_part, turned)
    for cp in sent:
        cp.wait_send()


def local_fast(
    tokens,
    prefix_len,
    neighbours,
    neighbour_index,
    w_qkv,
    w_out,
    w_cross_q,
    w_cross_kv,
    w_cross_out,
    w_up,
    w_down,
    gain_one,
    shift_one,
    gain_two,
    shift_two,
    gain_three,
    shift_three,
    cotangent,
):
    nz = lax.axis_size("dp") // 2
    quarter, width = tokens.shape[1:]
    rows, hidden = w_up.shape
    slots, rows_n = neighbours.shape[1:3]
    vectors = jnp.stack([gain_one, gain_two, gain_three, shift_one, shift_two, shift_three])
    weights, arrays, sums = memory(nz, quarter, width, hidden, slots, rows_n, rows)
    vmem, smem, anywhere = (pl.BlockSpec(memory_space=m) for m in (pltpu.VMEM, pltpu.SMEM, pl.ANY))
    made = [((quarter, width), bf16), ((quarter, width), f32), ((slots, rows_n, width), f32), *sums]
    dma = pltpu.SemaphoreType.DMA
    out, tokens_grad, neighbours_grad, *summed = pl.pallas_call(
        functools.partial(layer_kernel, nz, tuple(arrays)),
        out_shape=[jax.ShapeDtypeStruct(*v) for v in made],
        in_specs=[vmem] * 10 + [smem, vmem, smem, anywhere],
        out_specs=[vmem, vmem, anywhere] + [vmem] * len(sums),
        scratch_shapes=[pltpu.VMEM(*v) for v in (*weights, *arrays.values())]
        + [
            dma((6,)),
            dma((2,)),
            dma((2,)),
            dma((2, 2)),
            dma((2,)),
            dma((2, 28)),
            dma((len(GATHER), 14)),
            dma((len(GATHER), 14)),
            dma((len(REDUCE), 8)),
            dma((len(REDUCE), 8)),
            pltpu.SemaphoreType.REGULAR((7,)),
        ],
        compiler_params=pltpu.CompilerParams(
            collective_id=0, has_side_effects=True, vmem_limit_bytes=64 * 2**20 - 2**17
        ),
    )(
        w_qkv, w_cross_kv, w_out, w_cross_q, w_cross_out, w_up, w_down, vectors,
        tokens[0], cotangent[0], prefix_len, neighbours[0],
        neighbour_index[0], jnp.asarray(rope_table(4 * quarter)),
    )
    return deliver(out, tokens_grad, neighbours_grad, summed)


def pick_slots(pool, index):
    return jnp.stack(
        [
            jnp.concatenate([lax.dynamic_slice_in_dim(pool[s], index[s, j], 1, 0) for j in range(index.shape[1])], 0)
            for s in range(index.shape[0])
        ]
    )


def slot_places(index):
    slots = index.shape[1]
    same = index[:, :, None] == jnp.arange(slots)[None, None, :]
    return jnp.sum(jnp.where(same, jnp.arange(slots)[None, :, None], 0), 1)


def dense_dot(left_side, weight):
    return jnp.dot(left_side, weight, preferred_element_type=jnp.float32)


def input_grad(grad_out, weight):
    return lax.dot_general(
        grad_out,
        weight,
        (((grad_out.ndim - 1,), (1,)), ((), ())),
        preferred_element_type=jnp.float32,
    )


def weight_grad(left_side, grad_out):
    flat_left = left_side.reshape(-1, left_side.shape[-1])
    flat_grad = grad_out.reshape(-1, grad_out.shape[-1])
    return lax.dot_general(
        flat_left, flat_grad, (((0,), (0,)), ((), ())), preferred_element_type=jnp.float32
    )


def plain_norm_parts(array_in):
    avg_value = jnp.mean(array_in, -1, keepdims=True)
    centred = array_in - avg_value
    inv_std = lax.rsqrt(jnp.mean(centred * centred, -1, keepdims=True) + eps)
    return (centred * inv_std, inv_std)


def norm_back(grad_out, unit_part, inv_std, gain_f):
    scaled = grad_out * gain_f
    grad_in = inv_std * (
        scaled
        - jnp.mean(scaled, -1, keepdims=True)
        - unit_part * jnp.mean(scaled * unit_part, -1, keepdims=True)
    )
    return (grad_in, jnp.sum(grad_out * unit_part, (0, 1)), jnp.sum(grad_out, (0, 1)))


def rotary_tables(positions):
    half_size = HEAD // 2
    frequency = 10000.0 ** (-jnp.arange(half_size).astype(jnp.float32) / half_size)
    angles = positions.astype(jnp.float32)[:, None] * frequency[None, :]
    return (jnp.cos(angles)[:, None, :], jnp.sin(angles)[:, None, :])


def plain_rotate(array_in, cosine, sine_part):
    half_size = HEAD // 2
    first_half = array_in[..., :half_size]
    second = array_in[..., half_size:]
    return jnp.concatenate(
        [first_half * cosine - second * sine_part, second * cosine + first_half * sine_part], -1
    )


def unrotate(grad_in, cosine, sine_part):
    half_size = HEAD // 2
    first_half = grad_in[..., :half_size]
    second = grad_in[..., half_size:]
    return jnp.concatenate(
        [first_half * cosine + second * sine_part, second * cosine - first_half * sine_part], -1
    )


def grouped(array_in):
    split_heads = array_in.reshape(
        array_in.shape[0], array_in.shape[1], array_in.shape[2] // 4, 4, array_in.shape[3]
    )
    return jnp.moveaxis(split_heads, 2, 0)


def ungrouped(array_in):
    shifted_axes = jnp.moveaxis(array_in, 0, 2)
    return shifted_axes.reshape(
        shifted_axes.shape[0], shifted_axes.shape[1], -1, shifted_axes.shape[-1]
    )


def masked_scores(visible, queries, key_rows):
    scores = jnp.einsum(
        "sqhd,skhd->shqk", queries, key_rows, preferred_element_type=jnp.float32
    ) * HEAD ** (-0.5)
    return jnp.where(visible[:, None], scores, masked)


def attend_group(visible, packed):
    queries, key_rows, values = packed
    scores = masked_scores(visible, queries, key_rows)
    row_max = jnp.max(scores, -1, keepdims=True)
    exp_scores = jnp.exp(scores - row_max)
    row_total = jnp.sum(exp_scores, -1, keepdims=True)
    probabilities = (exp_scores / row_total).astype(jnp.bfloat16)
    mixed_out = jnp.einsum(
        "shqk,skhd->sqhd", probabilities, values, preferred_element_type=jnp.float32
    )
    return (mixed_out, (row_max + jnp.log(row_total))[..., 0])


def attend_back(visible, packed):
    queries, key_rows, values, grad_out, logsum = packed
    scores = masked_scores(visible, queries, key_rows)
    probabilities = jnp.exp(scores - logsum[..., None])
    grad_probs = jnp.einsum("sqhd,skhd->shqk", grad_out, values, preferred_element_type=jnp.float32)
    grad_scores = (
        probabilities * (grad_probs - jnp.sum(probabilities * grad_probs, -1, keepdims=True))
    ).astype(jnp.bfloat16)
    grad_query = jnp.einsum(
        "shqk,skhd->sqhd", grad_scores, key_rows, preferred_element_type=jnp.float32
    ) * HEAD ** (-0.5)
    grad_key = jnp.einsum(
        "shqk,sqhd->skhd", grad_scores, queries, preferred_element_type=jnp.float32
    ) * HEAD ** (-0.5)
    grad_value = jnp.einsum(
        "shqk,sqhd->skhd",
        probabilities.astype(jnp.bfloat16),
        grad_out,
        preferred_element_type=jnp.float32,
    )
    return (grad_query, grad_key, grad_value)


def local_plain(
    tokens,
    prefix_len,
    neighbours,
    neighbour_index,
    w_qkv,
    w_out,
    w_cross_q,
    w_cross_kv,
    w_cross_out,
    w_up,
    w_down,
    gain_one,
    shift_one,
    gain_two,
    shift_two,
    gain_three,
    shift_three,
    cotangent,
):
    forward_set = (
        lax.all_gather(w_qkv, ("dp", "seq"), axis=0, tiled=True),
        lax.all_gather(w_out, ("dp", "seq"), axis=0, tiled=True),
        lax.all_gather(w_cross_q, ("dp", "seq"), axis=0, tiled=True),
        lax.all_gather(w_cross_kv, ("dp", "seq"), axis=0, tiled=True),
        lax.all_gather(w_cross_out, ("dp", "seq"), axis=0, tiled=True),
        lax.all_gather(w_up, ("dp", "seq"), axis=0, tiled=True),
        lax.all_gather(w_down, ("dp", "seq"), axis=0, tiled=True),
        lax.all_gather(gain_one, ("dp", "seq"), axis=0, tiled=True),
        lax.all_gather(shift_one, ("dp", "seq"), axis=0, tiled=True),
        lax.all_gather(gain_two, ("dp", "seq"), axis=0, tiled=True),
        lax.all_gather(shift_two, ("dp", "seq"), axis=0, tiled=True),
        lax.all_gather(gain_three, ("dp", "seq"), axis=0, tiled=True),
        lax.all_gather(shift_three, ("dp", "seq"), axis=0, tiled=True),
    )
    (
        full_qkv,
        full_out,
        full_cross_q,
        full_cross_kv,
        full_cross_out,
        full_up,
        full_down,
        full_gain_one,
        full_shift_one,
        full_gain_two,
        full_shift_two,
        full_gain_three,
        full_shift_three,
    ) = forward_set
    seq_here, quarter, width = tokens.shape
    heads = width // HEAD
    hidden_width = full_up.shape[1]
    length = quarter * lax.axis_size("seq")
    seq_index = lax.axis_index("seq")
    query_pos = seq_index * quarter + jnp.arange(quarter)
    key_pos = jnp.arange(length)
    visible = (key_pos[None, None, :] <= query_pos[None, :, None]) | (
        key_pos[None, None, :] < prefix_len[:, None, None]
    )
    cosine, sine_part = rotary_tables(query_pos)
    gain_f1 = full_gain_one.astype(jnp.float32)
    gain_f2 = full_gain_two.astype(jnp.float32)
    gain_f3 = full_gain_three.astype(jnp.float32)
    resid_in = tokens.astype(jnp.float32)
    unit_one, inv_one = plain_norm_parts(resid_in)
    normed_one = (unit_one * gain_f1 + full_shift_one.astype(jnp.float32)).astype(jnp.bfloat16)
    joined = dense_dot(normed_one, full_qkv)
    query_rot = plain_rotate(
        joined[..., :width].reshape(seq_here, quarter, heads, HEAD), cosine, sine_part
    ).astype(jnp.bfloat16)
    key_local = (
        plain_rotate(
            joined[..., width : 2 * width].reshape(seq_here, quarter, heads, HEAD),
            cosine,
            sine_part,
        )
        .astype(jnp.bfloat16)
        .reshape(seq_here, quarter, width)
    )
    value_local = joined[..., 2 * width :].astype(jnp.bfloat16)
    key_all, value_all = (
        lax.all_gather(key_local, "seq", axis=1, tiled=True),
        lax.all_gather(value_local, "seq", axis=1, tiled=True),
    )
    key_heads = key_all.reshape(seq_here, length, heads, HEAD)
    value_heads = value_all.reshape(seq_here, length, heads, HEAD)
    attended, logsum = lax.map(
        functools.partial(attend_group, visible),
        (grouped(query_rot), grouped(key_heads), grouped(value_heads)),
    )
    attended = ungrouped(attended).reshape(seq_here, quarter, width).astype(jnp.bfloat16)
    first_sum = resid_in + dense_dot(attended, full_out)
    unit_two, inv_two = plain_norm_parts(first_sum)
    normed_two = (unit_two * gain_f2 + full_shift_two.astype(jnp.float32)).astype(jnp.bfloat16)
    cross_query = dense_dot(normed_two, full_cross_q).astype(jnp.bfloat16)
    pool_kv = dense_dot(neighbours, full_cross_kv).astype(jnp.bfloat16)
    slots = neighbours.shape[1]
    spans = slots // 2
    span_len = quarter // spans
    neighbour_rows = 2 * neighbours.shape[2]
    local_index = neighbour_index.reshape(seq_here, slots) - seq_index * slots
    picked = pick_slots(pool_kv, local_index)
    picked = picked.reshape(seq_here, spans, neighbour_rows, 2 * width)
    cross_keys = picked[..., :width].reshape(seq_here, spans, neighbour_rows, heads, HEAD)
    cross_values = picked[..., width:].reshape(seq_here, spans, neighbour_rows, heads, HEAD)
    cross_queries = cross_query.reshape(seq_here, spans, span_len, heads, HEAD)
    cross_scores = jnp.einsum(
        "scqhd,sckhd->schqk", cross_queries, cross_keys, preferred_element_type=jnp.float32
    ) * HEAD ** (-0.5)
    cross_probs = jax.nn.softmax(cross_scores, -1)
    cross_weights = cross_probs.astype(jnp.bfloat16)
    cross_mixed = jnp.einsum(
        "schqk,sckhd->scqhd", cross_weights, cross_values, preferred_element_type=jnp.float32
    )
    cross_mixed = cross_mixed.reshape(seq_here, quarter, width).astype(jnp.bfloat16)
    second_sum = first_sum + dense_dot(cross_mixed, full_cross_out)
    unit_three, inv_three = plain_norm_parts(second_sum)
    normed_three = (unit_three * gain_f3 + full_shift_three.astype(jnp.float32)).astype(
        jnp.bfloat16
    )
    hidden_pre = dense_dot(normed_three, full_up)
    activated = jax.nn.gelu(hidden_pre, approximate=False).astype(jnp.bfloat16)
    output = (second_sum + dense_dot(activated, full_down)).astype(jnp.bfloat16)
    grad_act = input_grad(cotangent, full_down)
    _, gelu_back = jax.vjp(functools.partial(jax.nn.gelu, approximate=False), hidden_pre)
    grad_hidden = gelu_back(grad_act)[0].astype(jnp.bfloat16)
    grad_normed_three = input_grad(grad_hidden, full_up)
    back_three, grad_gain_three, grad_shift_three = norm_back(
        grad_normed_three, unit_three, inv_three, full_gain_three.astype(jnp.float32)
    )
    grad_second = cotangent.astype(jnp.float32) + back_three
    grad_cross_branch = grad_second.astype(jnp.bfloat16)
    grad_mixed = (
        input_grad(grad_cross_branch, full_cross_out)
        .astype(jnp.bfloat16)
        .reshape(seq_here, spans, span_len, heads, HEAD)
    )
    grad_cross_probs = jnp.einsum(
        "scqhd,sckhd->schqk", grad_mixed, cross_values, preferred_element_type=jnp.float32
    )
    grad_cross_scores = (
        cross_probs
        * (grad_cross_probs - jnp.sum(cross_probs * grad_cross_probs, -1, keepdims=True))
    ).astype(jnp.bfloat16)
    grad_cross_query = (
        (
            jnp.einsum(
                "schqk,sckhd->scqhd",
                grad_cross_scores,
                cross_keys,
                preferred_element_type=jnp.float32,
            )
            * HEAD ** (-0.5)
        )
        .astype(jnp.bfloat16)
        .reshape(seq_here, quarter, width)
    )
    grad_cross_keys = jnp.einsum(
        "schqk,scqhd->sckhd", grad_cross_scores, cross_queries, preferred_element_type=jnp.float32
    ) * HEAD ** (-0.5)
    grad_cross_values = jnp.einsum(
        "schqk,scqhd->sckhd", cross_weights, grad_mixed, preferred_element_type=jnp.float32
    )
    grad_picked = jnp.concatenate(
        [
            grad_cross_keys.reshape(seq_here, spans, neighbour_rows, width),
            grad_cross_values.reshape(seq_here, spans, neighbour_rows, width),
        ],
        -1,
    )
    grad_picked = grad_picked.reshape(seq_here, slots, neighbours.shape[2], 2 * width)
    grad_pool_kv = pick_slots(grad_picked.astype(jnp.bfloat16), slot_places(local_index))
    grad_neighbours = input_grad(grad_pool_kv, full_cross_kv)
    grad_normed_two = input_grad(grad_cross_query, full_cross_q)
    back_two, grad_gain_two, grad_shift_two = norm_back(
        grad_normed_two, unit_two, inv_two, full_gain_two.astype(jnp.float32)
    )
    grad_first = grad_second + back_two
    grad_self_branch = grad_first.astype(jnp.bfloat16)
    grad_attended = (
        input_grad(grad_self_branch, full_out)
        .astype(jnp.bfloat16)
        .reshape(seq_here, quarter, heads, HEAD)
    )
    grad_query, grad_key_all, grad_value_all = lax.map(
        functools.partial(attend_back, visible),
        (
            grouped(query_rot),
            grouped(key_heads),
            grouped(value_heads),
            grouped(grad_attended),
            logsum,
        ),
    )
    grad_query = ungrouped(grad_query)
    grad_key_all = ungrouped(grad_key_all).reshape(seq_here, length, width)
    grad_value_all = ungrouped(grad_value_all).reshape(seq_here, length, width)
    grad_key, grad_value = (
        lax.psum_scatter(
            grad_key_all.astype(jnp.bfloat16), "seq", scatter_dimension=1, tiled=True
        ).astype(jnp.float32),
        lax.psum_scatter(
            grad_value_all.astype(jnp.bfloat16), "seq", scatter_dimension=1, tiled=True
        ).astype(jnp.float32),
    )
    grad_joined = jnp.concatenate(
        [
            unrotate(grad_query, cosine, sine_part).reshape(seq_here, quarter, width),
            unrotate(grad_key.reshape(seq_here, quarter, heads, HEAD), cosine, sine_part).reshape(
                seq_here, quarter, width
            ),
            grad_value,
        ],
        -1,
    ).astype(jnp.bfloat16)
    grad_normed_one = input_grad(grad_joined, full_qkv)
    back_one, grad_gain_one, grad_shift_one = norm_back(
        grad_normed_one, unit_one, inv_one, full_gain_one.astype(jnp.float32)
    )
    grad_tokens = grad_first + back_one
    norm_grads = jnp.stack(
        [
            grad_gain_one,
            grad_shift_one,
            grad_gain_two,
            grad_shift_two,
            grad_gain_three,
            grad_shift_three,
        ],
        1,
    )
    width_owned = lax.psum_scatter(
        jnp.concatenate(
            [
                weight_grad(normed_one, grad_joined),
                weight_grad(attended, grad_self_branch),
                weight_grad(normed_two, grad_cross_query),
                weight_grad(neighbours, grad_pool_kv),
                weight_grad(cross_mixed, grad_cross_branch),
                weight_grad(normed_three, grad_hidden),
                norm_grads,
            ],
            1,
        ),
        ("dp", "seq"),
        scatter_dimension=0,
        tiled=True,
    )
    down_owned = lax.psum_scatter(
        weight_grad(activated, cotangent), ("dp", "seq"), scatter_dimension=0, tiled=True
    )
    column = 8 * width + hidden_width
    return (
        output,
        grad_tokens,
        grad_neighbours,
        width_owned[:, : 3 * width],
        width_owned[:, 3 * width : 4 * width],
        width_owned[:, 4 * width : 5 * width],
        width_owned[:, 5 * width : 7 * width],
        width_owned[:, 7 * width : 8 * width],
        width_owned[:, 8 * width : column],
        down_owned,
        width_owned[:, column],
        width_owned[:, column + 1],
        width_owned[:, column + 2],
        width_owned[:, column + 3],
        width_owned[:, column + 4],
        width_owned[:, column + 5],
    )


def solution(mesh):
    sizes = dict(mesh.shape)
    fits = sizes == {"dp": 8, "seq": 4}
    return jax.shard_map(
        local_fast if fits else local_plain,
        mesh=mesh,
        in_specs=(
            P("dp", "seq", None),
            P("dp"),
            P("dp", "seq", None, None),
            P("dp", "seq", None),
            P(("dp", "seq"), None),
            P(("dp", "seq"), None),
            P(("dp", "seq"), None),
            P(("dp", "seq"), None),
            P(("dp", "seq"), None),
            P(("dp", "seq"), None),
            P(("dp", "seq"), None),
            P(("dp", "seq")),
            P(("dp", "seq")),
            P(("dp", "seq")),
            P(("dp", "seq")),
            P(("dp", "seq")),
            P(("dp", "seq")),
            P("dp", "seq", None),
        ),
        out_specs=(
            P("dp", "seq", None),
            P("dp", "seq", None),
            P("dp", "seq", None, None),
            P(("dp", "seq"), None),
            P(("dp", "seq"), None),
            P(("dp", "seq"), None),
            P(("dp", "seq"), None),
            P(("dp", "seq"), None),
            P(("dp", "seq"), None),
            P(("dp", "seq"), None),
            P(("dp", "seq")),
            P(("dp", "seq")),
            P(("dp", "seq")),
            P(("dp", "seq")),
            P(("dp", "seq")),
            P(("dp", "seq")),
        ),
        check_vma=False,
    )
```

```python
import functools
import math

import jax
import jax.numpy as jnp
import numpy as np
from jax import lax
from jax.experimental import pallas as pl
from jax.experimental.pallas import tpu as pltpu
from jax.sharding import PartitionSpec as P

HEAD = 64
eps = 1e-05
masked = -1e30
MESH = pl.DeviceIdType.MESH
bf16 = jnp.bfloat16
f32 = jnp.float32
NN = (((1,), (0,)), ((), ()))
NT = (((1,), (1,)), ((), ()))
TN = (((0,), (0,)), ((), ()))
LANES = 128
AHEAD = 3
SPREAD = 3
ACROSS, LAST = 2, 4


def dot(a, b, dims=NN):
    return lax.dot_general(a, b, dims, preferred_element_type=f32)


def norm_parts(v):
    centred = v - jnp.mean(v, -1, keepdims=True)
    inv = lax.rsqrt(jnp.mean(centred * centred, -1, keepdims=True) + eps)
    return centred * inv, inv


class Place:
    def __init__(self, nz):
        dp, s = lax.axis_index("dp"), lax.axis_index("seq")
        self.nz, self.dp, self.s = nz, dp, s
        self.z, self.x = lax.div(dp, 2), lax.rem(dp, 2)
        self.y, self.c = lax.div(s, 2), lax.rem(s, 2)
        x, y, z, c = self.x, self.y, self.z, self.c
        self.o = 1 - c
        self.own, self.at_x, self.at_y, self.at_d = (
            x * 2 + y,
            (1 - x) * 2 + y,
            x * 2 + 1 - y,
            (1 - x) * 2 + 1 - y,
        )
        self.to_z = [(lax.rem(z + j, nz) * 2 + x, s) for j in range(1, nz)]
        self.z_of = [lax.rem(z + j, nz) for j in range(1, nz)]
        self.z_from = [lax.rem(z - j + nz, nz) for j in range(1, nz)]
        self.to_x = (z * 2 + 1 - x, s)
        self.to_y = (dp, (1 - y) * 2 + c)
        self.to_c = (dp, y * 2 + 1 - c)
        self.s_y = (1 - y) * 2 + c
        self.s_c = y * 2 + 1 - c
        self.s_d = (1 - y) * 2 + 1 - c

    def meet(self):
        barrier = pltpu.get_barrier_semaphore()
        friends = [*self.to_z, self.to_x, self.to_y, self.to_c]
        for device in friends:
            pl.semaphore_signal(barrier, inc=1, device_id=device, device_id_type=MESH)
        pl.semaphore_wait(barrier, len(friends))


def remote(src, dst, send, recv, device):
    return pltpu.make_async_remote_copy(
        src_ref=src, dst_ref=dst, send_sem=send, recv_sem=recv, device_id=device, device_id_type=MESH
    )


class Gather:
    def __init__(self, place, weights, chunks, send, recv):
        self.p, self.w, self.chunks, self.ss, self.rs = place, weights, chunks, send, recv
        self.sent = [[] for _ in chunks]
        self.t, self.have = 0, set()
        self.z_first = [q for q, v in enumerate(chunks) if v[3] > 0]
        self.plane_first = [q for q, v in enumerate(chunks) if v[3] <= 0]

    def chunks_of(self, k):
        return [q for q, v in enumerate(self.chunks) if v[0] == k]

    def begin(self):
        self.along_z(self.z_first[0])

    def tick(self):
        t, order = self.t, self.z_first
        n = len(order)
        if t >= n + LAST:
            return
        if t == 0:
            for q in order[1:AHEAD]:
                self.along_z(q)
            for q in self.plane_first:
                self.plane_out(q)
        if t < n:
            self.along_xy(order[t])
        if t + AHEAD < n:
            self.along_z(order[t + AHEAD])
        if t == 1:
            for q in self.plane_first:
                self.plane_across(q)
        if t >= 2 and (t - 2) % SPREAD == 0 and (t - 2) // SPREAD < len(self.plane_first):
            self.plane_z(self.plane_first[(t - 2) // SPREAD])
        if 0 <= t - ACROSS < n:
            self.across(order[t - ACROSS])
        if 0 <= t - LAST < n:
            self.last(order[t - LAST])
        self.t += 1

    def need(self, q):
        if q in self.plane_first:
            while self.t <= SPREAD * self.plane_first.index(q) + 2:
                self.tick()
        else:
            while self.t <= self.z_first.index(q) + LAST:
                self.tick()
        if q not in self.have:
            self.have.add(q)
            if q in self.plane_first:
                self.plane_last(q)
                self.plane_ready(q)
            else:
                self.ready(q)

    def plane_out(self, q):
        p = self.p
        mine = self.part(q, p.c, p.z, p.own)
        for j, device in ((3, p.to_x), (4, p.to_y), (7, p.to_c)):
            self.send(q, j, mine, device)

    def plane_across(self, q):
        p = self.p
        from_x, from_y = self.part(q, p.c, p.z, p.at_x), self.part(q, p.c, p.z, p.at_y)
        self.wait(q, 3, from_x)
        self.send(q, 8, from_x, p.to_c)
        self.wait(q, 4, from_y)
        self.send(q, 9, from_y, p.to_c)
        if self.chunks[q][3] == 0:
            self.send(q, 5, from_y, p.to_x)
        else:
            self.send(q, 5, from_x, p.to_y)

    def plane_z(self, q):
        p, every = self.p, slice(None)
        diag = self.part(q, p.c, p.z, p.at_d)
        self.wait(q, 5, diag)
        self.send(q, 10, diag, p.to_c)
        for j, device in enumerate(p.to_z):
            self.send(q, j, self.part(q, p.c, p.z, every), device)

    def plane_last(self, q):
        p, every = self.p, slice(None)
        for j, z in enumerate(p.z_from):
            ref = self.part(q, p.c, z, every)
            self.wait(q, j, ref)
            self.send(q, 11 + j, ref, p.to_c)

    def plane_ready(self, q):
        p, every = self.p, slice(None)
        for j, xy in ((7, p.own), (8, p.at_x), (9, p.at_y), (10, p.at_d)):
            self.wait(q, j, self.part(q, p.o, p.z, xy))
        for j, z in enumerate(p.z_from):
            self.wait(q, 11 + j, self.part(q, p.o, z, every))

    def part(self, q, half, z, xy):
        k, start, width, _ = self.chunks[q]
        return self.w[k].at[half, z, xy, :, pl.ds(start, width)]

    def copy(self, q, j, ref, device):
        return remote(ref, ref, self.ss.at[q, j], self.rs.at[q, j], device)

    def send(self, q, j, ref, device):
        cp = self.copy(q, j, ref, device)
        cp.start()
        self.sent[q].append(cp)

    def wait(self, q, j, ref):
        self.copy(q, j, ref, self.p.to_c).wait_recv()

    def along_z(self, q):
        p = self.p
        for j, device in enumerate(p.to_z):
            self.send(q, j, self.part(q, p.c, p.z, p.own), device)

    def along_xy(self, q):
        p, allz = self.p, slice(None)
        for j, z in enumerate(p.z_from):
            self.wait(q, j, self.part(q, p.c, z, p.own))
        mine = self.part(q, p.c, allz, p.own)
        self.send(q, 3, mine, p.to_x)
        self.send(q, 4, mine, p.to_y)
        self.send(q, 7, mine, p.to_c)

    def across(self, q):
        p, allz, cut = self.p, slice(None), self.chunks[q][3]
        from_x, from_y = self.part(q, p.c, allz, p.at_x), self.part(q, p.c, allz, p.at_y)
        self.wait(q, 3, from_x)
        self.send(q, 5, self.part(q, p.c, pl.ds(0, cut), p.at_x), p.to_y)
        self.send(q, 8, from_x, p.to_c)
        self.wait(q, 4, from_y)
        self.send(q, 6, self.part(q, p.c, pl.ds(cut, p.nz - cut), p.at_y), p.to_x)
        self.send(q, 9, from_y, p.to_c)

    def last(self, q):
        p, cut = self.p, self.chunks[q][3]
        for j, z in ((5, pl.ds(0, cut)), (6, pl.ds(cut, p.nz - cut))):
            ref = self.part(q, p.c, z, p.at_d)
            self.wait(q, j, ref)
            self.send(q, j + 5, ref, p.to_c)

    def ready(self, q):
        p, allz, cut = self.p, slice(None), self.chunks[q][3]
        for j, z, xy in (
            (7, allz, p.own),
            (8, allz, p.at_x),
            (9, allz, p.at_y),
            (10, pl.ds(0, cut), p.at_d),
            (11, pl.ds(cut, p.nz - cut), p.at_d),
        ):
            self.wait(q, j, self.part(q, p.o, z, xy))

    def settle(self, q):
        for cp in self.sent[q]:
            cp.wait_send()
        self.sent[q] = []


def half_of(w, h, start=None, width=None):
    v = w[h] if start is None else w[h, :, :, :, pl.ds(start, width)]
    return v.reshape(-1, v.shape[-1])


def lane_masks():
    lane = lax.broadcasted_iota(jnp.int32, (1, LANES), 1)
    low = lane < HEAD
    return low, jnp.where(low, 1.0, 0.0).astype(bf16), jnp.where(low, 0.0, 1.0).astype(bf16)


def stacked(v, low, high):
    return jnp.concatenate([v * low, v * high], 0)


def swap_halves(v):
    lane = lax.broadcasted_iota(jnp.int32, v.shape, 1)
    first = lax.rem(lane, HEAD) < HEAD // 2
    return jnp.where(first, pltpu.roll(v, LANES - HEAD // 2, 1), pltpu.roll(v, HEAD // 2, 1))


def rotate(v, cosine, signed):
    return v * cosine + swap_halves(v) * signed


def forward(p, r, g, swap, kv_sem, pairs):
    n = len(g.chunks)
    c, z = p.c, p.z
    w = r.w

    vectors = r.vectors[...].astype(f32)
    count, rows = vectors.shape
    vectors = jnp.concatenate([vectors, jnp.zeros((count, LANES - rows), f32)], 1)
    vectors = jnp.concatenate([vectors, jnp.zeros((LANES - count, LANES), f32)], 0)
    vectors = jnp.transpose(vectors)[:rows]
    start = 0
    for k, ref in enumerate((r.w_qkv, r.w_cross_kv, r.w_out, r.w_cross_q, r.w_cross_out, r.w_up)):
        rows = ref[...].astype(f32)
        size = rows.shape[1] // 2
        for h in range(2):
            parts = 3 if k == 0 else 1
            part = size // parts
            for i in range(parts):
                source = i * 2 * part + h * part
                r.pack[h, :, start + i * part : start + (i + 1) * part] = rows[:, source : source + part]
            if k == 0:
                r.pack[h, :, start + size : start + size + LANES] = vectors
        start += w[k].shape[-1]
    p.meet()
    first = remote(r.pack.at[p.o], r.beside, r.pair_sem.at[0], r.pair_sem.at[1], p.to_c)
    first.start()
    down_rows, down_half = r.w_down.shape[0], w[6].shape[-1]
    down_at = pl.ds(pl.multiple_of(c * down_rows, 16), down_rows)
    down = remote(
        r.w_down.at[:, pl.ds(pl.multiple_of(p.o * down_half, LANES), down_half)],
        w[6].at[p.o, z, p.own, down_at],
        r.pair_sem.at[2],
        r.pair_sem.at[3],
        p.to_c,
    )
    down.start()
    tokens_y = remote(r.tokens, r.branch, r.pair_sem.at[4], r.pair_sem.at[5], p.to_y)
    tokens_y.start()
    ropes = [pltpu.make_async_copy(r.rope_table.at[s], r.rope.at[i], r.rope_sem.at[i]) for i, s in enumerate((p.s, p.s_y))]
    for rope in ropes:
        rope.start()
    w[6][c, z, p.own, down_at] = r.w_down[:, pl.ds(pl.multiple_of(c * down_half, LANES), down_half)]
    first.wait_recv()
    start = 0
    for k in range(6):
        width = w[k].shape[-1]
        mine, other = r.pack[c, :, start : start + width], r.beside[:, start : start + width]
        top, low = jnp.where(c == 0, mine, other), jnp.where(c == 0, other, mine)
        w[k][c, z, p.own] = jnp.concatenate([top, low], 0).astype(bf16)
        start += width
        if k == 0:
            g.begin()
    down.wait_recv()
    g.tick()
    swap.send("cot", r.cotangent.at[:, pl.ds(pl.multiple_of(p.o * down_half, LANES), down_half)], r.by_cot)
    swap.send("nb", r.neighbours, r.by_neighbours)
    for rope in ropes:
        rope.wait()
    tokens = r.tokens[...].astype(f32)
    quarter, width = tokens.shape
    unit, _ = norm_parts(tokens)
    g.tick()
    tokens_y.wait_recv()
    unit_y, _ = norm_parts(r.branch[...].astype(f32))
    g.need(0)
    part = width // 2
    r.vec[...] = jnp.transpose(half_of(w[0], 0, 3 * part, LANES).astype(f32))[:8]

    def affine(v, i):
        return (v * r.vec[i : i + 1] + r.vec[3 + i : 4 + i]).astype(bf16)

    r.n1[:quarter] = affine(unit, 0)
    r.n1[quarter:] = affine(unit_y, 0)
    swap.send("n1", r.n1, r.by_n1)
    for h in range(2):
        value = dot(r.n1[...], half_of(w[0], h, 2 * part, part)).astype(bf16)
        cols = slice(width + h * part, width + (h + 1) * part)
        r.kv[p.s, :, cols] = value[:quarter]
        r.kv[p.s_y, :, cols] = value[quarter:]

    def turned(v, i, sign=1):
        cosine, signed = r.rope[i, :, :LANES], r.rope[i, :, LANES:]
        return jnp.concatenate(
            [rotate(v[:, b : b + LANES], cosine, sign * signed) for b in range(0, v.shape[1], LANES)], 1
        )

    g.need(1)
    for h in range(2):
        key = dot(r.n1[...], half_of(w[0], h, part, part))
        cols = slice(h * part, (h + 1) * part)
        r.kv[p.s, :, cols] = turned(key[:quarter], 0).astype(bf16)
        r.kv[p.s_y, :, cols] = turned(key[quarter:], 1).astype(bf16)
    kv_sent = [
        remote(r.kv.at[s], r.kv.at[s], kv_sem.at[0, i], kv_sem.at[1, i], p.to_c) for i, s in enumerate((p.s, p.s_y))
    ]
    for cp in kv_sent:
        cp.start()
    g.need(2)
    for h in range(2):
        query = dot(r.n1[:quarter], half_of(w[0], h, 0, part))
        r.q[:, h * part : (h + 1) * part] = turned(query, 0).astype(bf16)
    g.need(3)
    g.need(4)

    def pool_rows(i, carry):
        rows = r.neighbours[pl.ds(i * 2, 2)].reshape(-1, r.neighbours.shape[2])
        for h in range(2):
            width = w[1].shape[-1]
            r.pool[pl.ds(i * 2, 2), :, h * width : (h + 1) * width] = (
                dot(rows, half_of(w[1], h)).astype(bf16).reshape(2, -1, width)
            )
        return carry

    lax.fori_loop(0, 2, pool_rows, 0)
    g.tick()
    lax.fori_loop(2, r.neighbours.shape[0] // 2, pool_rows, 0)
    for i, s in enumerate((p.s_c, p.s_d)):
        remote(r.kv.at[s], r.kv.at[s], kv_sem.at[0, i], kv_sem.at[1, i], p.to_c).wait_recv()

    low_lane, low, high = lane_masks()
    place = lax.broadcasted_iota(jnp.int32, (1, quarter), 1) + p.s * quarter
    limit = jnp.maximum(place, r.prefix[0] - 1)

    def self_pair(i, carry):
        cols = pl.ds(pl.multiple_of(i * LANES, LANES), LANES)
        vcols = pl.ds(pl.multiple_of(i * LANES + w[1].shape[-1], LANES), LANES)
        keys = r.kv[:, :, cols].reshape(-1, LANES)
        values = r.kv[:, :, vcols].reshape(-1, LANES)
        mixed = []
        for e, lanes in enumerate((low, high)):
            scores = dot(keys, r.q[:, cols] * (lanes * bf16(HEAD**-0.5)), NT)
            key_place = lax.broadcasted_iota(jnp.int32, scores.shape, 0)
            scores = jnp.where(key_place <= limit, scores, masked)
            top = jnp.max(scores, 0, keepdims=True)
            exped = jnp.exp(scores - top)
            total = jnp.sum(exped, 0, keepdims=True)
            weights = (exped * (1.0 / total)).astype(bf16)
            r.lse[i, :, e * quarter : (e + 1) * quarter] = top + jnp.log(total)
            mixed.append(dot(weights, values, TN))
        r.att[:, cols] = jnp.where(low_lane, *mixed).astype(bf16)
        return carry

    for i in range(0, pairs, 2):
        lax.fori_loop(i, i + 2, self_pair, 0)
        g.tick()
    g.need(5)

    def project(v, k):
        return jnp.concatenate([dot(v, half_of(w[k], h)) for h in range(2)], 1)

    swap.send("att", r.att, r.by_att)
    first_sum = tokens + project(r.att[...], 2)
    r.first[...] = first_sum
    r.n2[...] = affine(norm_parts(first_sum)[0], 1)
    swap.send("n2", r.n2, r.by_n2)
    g.need(6)
    r.cq[...] = project(r.n2[...], 3).astype(bf16)
    slots = r.neighbours.shape[0]
    span = quarter // (slots // 2)

    def cross_pair(i, carry):
        cols = pl.ds(pl.multiple_of(i * LANES, LANES), LANES)
        vcols = pl.ds(pl.multiple_of(i * LANES + w[1].shape[-1], LANES), LANES)
        for b in range(slots // 2):
            two = [lax.rem(r.index[b, j], slots) for j in range(2)]
            rows = slice(b * span, (b + 1) * span)
            queries = stacked(r.cq[rows, cols], low, high) * bf16(HEAD**-0.5)
            keys = jnp.concatenate([r.pool[t, :, cols] for t in two], 0)
            values = jnp.concatenate([r.pool[t, :, vcols] for t in two], 0)
            scores = dot(keys, queries, NT)
            top = jnp.max(scores, 0, keepdims=True)
            e = jnp.exp(scores - top)
            total = jnp.sum(e, 0, keepdims=True)
            weights = (e * (1.0 / total)).astype(bf16)
            r.lse_cross[i, b : b + 1] = top + jnp.log(total)
            mixed = dot(weights, values, TN)
            r.cm[rows, cols] = jnp.where(low_lane, mixed[:span], mixed[span:]).astype(bf16)
        return carry

    lax.fori_loop(0, pairs // 2, cross_pair, 0)
    g.tick()
    lax.fori_loop(pairs // 2, pairs, cross_pair, 0)
    g.need(7)
    swap.send("cm", r.cm, r.by_cm)
    second_sum = r.first[...] + project(r.cm[...], 4)
    r.second[...] = second_sum
    r.n3[...] = affine(norm_parts(second_sum)[0], 2)
    swap.send("n3", r.n3, r.by_n3)
    hidden_half = w[5].shape[-1]

    def up_tile(start, size):
        def body(h, carry):
            hidden = dot(r.n3[...], half_of(w[5], h, start, size))
            cdf = 0.5 * (1.0 + lax.erf(hidden * (0.5**0.5)))
            density = jnp.exp(-0.5 * hidden * hidden) * ((2 * math.pi) ** -0.5)
            cols = pl.ds(pl.multiple_of(h * hidden_half + start, LANES), size)
            r.act[:, cols] = (hidden * cdf).astype(bf16)
            r.slope[:, cols] = (cdf + hidden * density).astype(bf16)
            return carry

        lax.fori_loop(0, 2, body, 0)

    for q, (k, start, size, _) in enumerate(g.chunks):
        if k == 5:
            g.need(q)
            up_tile(start, size)
    swap.send("act", r.act, r.by_act)

    def down_part(q):
        _, start, size, _ = g.chunks[q]
        for h in range(2):
            cols = slice(h * down_half + start, h * down_half + start + size)
            r.out[:, cols] = (r.second[:, cols] + dot(r.act[...], half_of(w[6], h, start, size))).astype(bf16)

    return down_part, turned, (first, down, tokens_y, *kv_sent)


LAGS = (6, 5, 3)
JOINT = True


class Reduce:
    def __init__(self, place, r, chunks, send, recv):
        self.p, self.r, self.w, self.chunks, self.ss, self.rs = place, r, r.w, chunks, send, recv
        self.sent, self.open, self.under_way, self.phase = [], set(), {}, 0
        self.starts = [sum(v.shape[-1] for v in r.w[:k]) for k in range(7)]

    def free(self, k):
        p = self.p
        for device in (p.to_x, p.to_y, *p.to_z):
            pl.semaphore_signal(self.r.credit.at[k], inc=1, device_id=device, device_id_type=MESH)

    def array(self, k, half):
        if k == 6:
            return self.r.down_sum, 0 if half is self.p.c else 1
        return self.w[k], half

    def at(self, q, half, z, xy):
        k, start, width, _ = self.chunks[q]
        ref, lead = self.array(k, half)
        return ref.at[lead, z, xy, :, pl.ds(start, width)]

    def load(self, q, half, z, xy):
        k, start, width, _ = self.chunks[q]
        ref, lead = self.array(k, half)
        return ref[lead, z, xy, :, start : start + width].astype(f32)

    def save(self, q, half, z, xy, v):
        k, start, width, _ = self.chunks[q]
        ref, lead = self.array(k, half)
        ref[lead, z, xy, :, start : start + width] = v.astype(bf16)

    def copy(self, q, j, src, dst, device):
        cp = remote(src, dst, self.ss.at[q, j], self.rs.at[q, j], device)
        cp.start()
        self.sent.append(cp)

    def wait(self, q, j, ref):
        remote(ref, ref, self.ss.at[q, j], self.rs.at[q, j], self.p.to_c).wait_recv()

    def diagonal(self, q):
        p, cut = self.p, self.chunks[q][3]
        for j, z, device in ((0, pl.ds(0, cut), p.to_y), (1, pl.ds(cut, p.nz - cut), p.to_x)):
            self.copy(q, j, self.at(q, p.c, z, p.at_d), self.at(q, p.o, z, 0), device)

    def across(self, q):
        p, cut, allz = self.p, self.chunks[q][3], slice(None)
        for j, zs, to in ((0, range(cut), p.at_x), (1, range(cut, p.nz), p.at_y)):
            self.wait(q, j, self.at(q, p.o, pl.ds(zs[0], len(zs)), 0))
            for z in zs:
                self.save(q, p.c, z, to, self.load(q, p.c, z, to) + self.load(q, p.o, z, 0))
        self.copy(q, 2, self.at(q, p.c, allz, p.at_x), self.at(q, p.o, allz, 1), p.to_x)
        self.copy(q, 3, self.at(q, p.c, allz, p.at_y), self.at(q, p.o, allz, 2), p.to_y)

    def along_z(self, q):
        p, allz = self.p, slice(None)
        self.wait(q, 2, self.at(q, p.o, allz, 1))
        self.wait(q, 3, self.at(q, p.o, allz, 2))
        for z in range(p.nz):
            total = self.load(q, p.c, z, p.own) + self.load(q, p.o, z, 1) + self.load(q, p.o, z, 2)
            self.save(q, p.c, z, p.own, total)
        for j, device in enumerate(p.to_z):
            self.copy(q, 4 + j, self.at(q, p.c, p.z_of[j], p.own), self.at(q, p.o, j, 3), device)

    def steps(self, q):
        if self.chunks[q][3] > 0:
            return self.diagonal, self.across, self.along_z, self.last
        return self.z_out, self.plane_diagonal, self.plane_across, self.plane_last

    def z_out(self, q):
        p, every = self.p, slice(None)
        for j, device in enumerate(p.to_z):
            self.copy(q, 4 + j, self.at(q, p.c, p.z_of[j], every), self.at(q, p.o, j, every), device)

    def plane_diagonal(self, q):
        p, every = self.p, slice(None)
        for j in range(p.nz - 1):
            self.wait(q, 4 + j, self.at(q, p.o, j, every))
        for xy in range(4):
            total = self.load(q, p.c, p.z, xy)
            for j in range(p.nz - 1):
                total = total + self.load(q, p.o, j, xy)
            self.save(q, p.c, p.z, xy, total)
        device = p.to_x if self.chunks[q][3] == 0 else p.to_y
        self.copy(q, 0, self.at(q, p.c, p.z, p.at_d), self.at(q, p.o, p.nz - 1, 0), device)

    def plane_across(self, q):
        p, there = self.p, self.p.nz - 1
        to = p.at_y if self.chunks[q][3] == 0 else p.at_x
        self.wait(q, 0, self.at(q, p.o, there, 0))
        self.save(q, p.c, p.z, to, self.load(q, p.c, p.z, to) + self.load(q, p.o, there, 0))
        self.copy(q, 2, self.at(q, p.c, p.z, p.at_x), self.at(q, p.o, there, 1), p.to_x)
        self.copy(q, 3, self.at(q, p.c, p.z, p.at_y), self.at(q, p.o, there, 2), p.to_y)

    def plane_last(self, q):
        p, there = self.p, self.p.nz - 1
        total = self.load(q, p.c, p.z, p.own)
        for j in (1, 2):
            self.wait(q, 1 + j, self.at(q, p.o, there, j))
            total = total + self.load(q, p.o, there, j)
        self.hand_over(q, total)

    def last(self, q):
        p = self.p
        total = self.load(q, p.c, p.z, p.own)
        for j in range(p.nz - 1):
            self.wait(q, 4 + j, self.at(q, p.o, j, 3))
            total = total + self.load(q, p.o, j, 3)
        self.hand_over(q, total)

    def hand_over(self, q, total):
        p, r, (k, start, width, _) = self.p, self.r, self.chunks[q]
        cols = slice(start, start + width)
        rows = total.shape[0] // 2
        r.sums[k][p.c, :, cols] = jnp.where(p.c == 0, total[:rows], total[rows:])
        if k == 6:
            mine = r.down_beside.at[:, cols]
        else:
            mine = r.beside.at[:, self.starts[k] + start : self.starts[k] + start + width]
        mine[...] = jnp.where(p.c == 0, total[rows:], total[:rows])
        self.copy(q, 7, mine, r.sums[k].at[p.c, :, cols], p.to_c)

    def finish(self, q):
        p, (k, start, width, _) = self.p, self.chunks[q]
        self.wait(q, 7, self.r.sums[k].at[p.o, :, pl.ds(start, width)])

    def push(self, q=None, lag=None):
        lag = lag or LAGS[self.phase]
        for other in list(self.under_way):
            stage, age = self.under_way[other]
            if age + 1 < lag:
                self.under_way[other] = stage, age + 1
                continue
            self.steps(other)[stage + 1](other)
            self.under_way[other] = stage + 1, 0
            if stage == 2:
                del self.under_way[other]
        if q is not None:
            k = self.chunks[q][0]
            if k not in self.open:
                pl.semaphore_wait(self.r.credit.at[k], 1 + self.p.nz)
                self.open.add(k)
            self.steps(q)[0](q)
            self.under_way[q] = 0, 0

    def chunks_of(self, k):
        return [q for q, v in enumerate(self.chunks) if v[0] == k]

    def drain(self):
        while self.under_way:
            self.push(None, 1)
        for q in range(len(self.chunks)):
            self.finish(q)


class Swap:
    def __init__(self, place, sems):
        self.p, self.sems, self.n, self.sent, self.landed = place, sems, 0, [], {}

    def send(self, name, src, dst):
        cp = remote(src, dst, self.sems.at[0, self.n], self.sems.at[1, self.n], self.p.to_c)
        cp.start()
        self.sent.append(cp)
        self.landed[name] = cp
        self.n += 1

    def wait(self, name):
        self.landed.pop(name).wait_recv()


def norm_back_at(grad, v, gain):
    unit, inv = norm_parts(v)
    scaled = grad * gain
    back = inv * (
        scaled - jnp.mean(scaled, -1, keepdims=True) - unit * jnp.mean(scaled * unit, -1, keepdims=True)
    )
    return back, jnp.sum(grad * unit, 0, keepdims=True), jnp.sum(grad, 0, keepdims=True)


def backward(p, r, g, swap, red, kv_sem, pairs, down_part, turned):
    w, c, o = r.w, p.c, p.o
    quarter, width = r.tokens.shape
    hidden_half, pool_half = w[5].shape[-1], w[1].shape[-1]
    slots, rows_n = r.neighbours.shape[:2]
    low_lane, low, high = lane_masks()
    r.vec_sum[...] = jnp.zeros_like(r.vec_sum)

    def half(ref, h, size):
        return ref.at[:, pl.ds(pl.multiple_of(h * size, LANES), size)]

    def input_grad(ref, k, size):
        return sum(dot(ref[:, h * size : (h + 1) * size], half_of(w[k], h, 0, size), NT) for h in range(2))

    def weight_grad(k, left, left_beside, right, right_beside, size, tile=384, chunks=None, push=True):
        into, lead = red.array(k, c)
        rows = into.shape[3]
        per = tile // (4 * rows)
        columns = [(q, red.chunks[q][1]) for q in (red.chunks_of(k) if chunks is None else chunks)]
        columns = [(q, start, min(red.chunks[q][2], size - start)) for q, start in columns]
        for together in [columns] if JOINT else [[v] for v in columns]:

            def body(i, carry, together=together):
                cols = pl.ds(pl.multiple_of(i * tile, LANES), tile)
                turned_left, turned_beside = jnp.transpose(left(cols)), jnp.transpose(left_beside(cols))
                for _, start, n in together:
                    part = dot(turned_left, right(start, n)) + dot(turned_beside, right_beside(start, n))
                    into[lead, pl.ds(i * per, per), :, :, start : start + n] = part.astype(bf16).reshape(per, 4, rows, n)
                return carry

            lax.fori_loop(0, p.nz // per, body, 0)
            if push:
                for q, _, _ in together:
                    red.push(q)

    def plain_grad(k, left, left_beside, right, right_beside, size, tile=384, chunks=None, push=True):
        weight_grad(
            k,
            lambda cols: left[:, cols],
            lambda cols: left_beside[:, cols],
            lambda start, n: right[:, pl.ds(pl.multiple_of(c * size + start, LANES), n)],
            lambda start, n: right_beside[:, start : start + n],
            size,
            tile,
            chunks,
            push,
        )

    def gain(i):
        return r.vec[i : i + 1]

    def keep_vec(i, gain_sum, shift_sum):
        r.vec_sum[i : i + 1] = gain_sum
        r.vec_sum[3 + i : 4 + i] = shift_sum

    for name in ("cot", "act"):
        swap.wait(name)
    red.free(6)
    plain_grad(6, r.act, r.by_act, r.cotangent, r.by_cot, w[6].shape[-1], 4 * w[6].shape[3])
    for q in g.chunks_of(6):
        g.need(q)
        down_part(q)
        g.settle(q)
        red.push()
    down_half = w[6].shape[-1]

    def act_tile(z, carry):
        rows = 4 * w[6].shape[3]
        cols = pl.ds(pl.multiple_of(z * rows, LANES), rows)
        act_grad = sum(
            dot(r.cotangent[:, h * down_half : (h + 1) * down_half], w[6][h, z].reshape(rows, down_half), NT)
            for h in range(2)
        )
        r.slope[:, cols] = (act_grad * r.slope[:, cols].astype(f32)).astype(bf16)
        return carry

    lax.fori_loop(0, p.nz, act_tile, 0)
    gh = r.slope
    swap.send("gh", half(gh, o, hidden_half), r.by_hidden_grad)
    red.push()
    grad_three = input_grad(gh, 5, hidden_half)
    red.free(5)
    red.push()
    for q in g.chunks_of(5):
        g.settle(q)
    back, dg, db = norm_back_at(grad_three, r.second[...], gain(2))
    keep_vec(2, dg, db)
    grad_second = r.cotangent[...].astype(f32) + back
    r.second[...] = grad_second
    r.branch[...] = grad_second.astype(bf16)
    swap.send("gcb", half(r.branch, o, width // 2), r.by_branch)
    for name in ("gh", "n3"):
        swap.wait(name)
    plain_grad(5, r.n3, r.by_n3, gh, r.by_hidden_grad, hidden_half)
    r.mixed_grad[...] = input_grad(r.branch, 4, width // 2).astype(bf16)
    red.free(4)
    for q in g.chunks_of(4):
        g.settle(q)

    span = quarter // (slots // 2)

    def cross_pair(i, carry):
        cols = pl.ds(pl.multiple_of(i * LANES, LANES), LANES)
        vcols = pl.ds(pl.multiple_of(i * LANES + pool_half, LANES), LANES)
        for b in range(slots // 2):
            two = [lax.rem(r.index[b, j], slots) for j in range(2)]
            rows = slice(b * span, (b + 1) * span)
            queries = stacked(r.cq[rows, cols], low, high) * bf16(HEAD**-0.5)
            grads = stacked(r.mixed_grad[rows, cols], low, high)
            keys = jnp.concatenate([r.pool[t, :, cols] for t in two], 0)
            values = jnp.concatenate([r.pool[t, :, vcols] for t in two], 0)
            probs = jnp.exp(dot(keys, queries, NT) - r.lse_cross[i, b : b + 1])
            grad_probs = dot(values, grads, NT)
            score_grad = (probs * (grad_probs - jnp.sum(probs * grad_probs, 0, keepdims=True))).astype(bf16)
            r.gkv[b, :, cols] = dot(score_grad, queries).astype(bf16)
            r.gkv[b, :, vcols] = dot(probs.astype(bf16), grads).astype(bf16)
            gq = dot(score_grad, keys, TN) * HEAD**-0.5
            r.cq_grad[rows, cols] = jnp.where(low_lane, gq[:span], gq[span:]).astype(bf16)
        return carry

    for i in range(0, pairs, 2):
        lax.fori_loop(i, i + 2, cross_pair, 0)
        red.push()
    swap.send("gcq", half(r.cq_grad, o, width // 2), r.by_cq_grad)
    grad_two = input_grad(r.cq_grad, 3, width // 2)
    red.free(3)
    for q in g.chunks_of(3):
        g.settle(q)
    back, dg, db = norm_back_at(grad_two, r.first[...], gain(1))
    keep_vec(1, dg, db)
    grad_first = r.second[...] + back
    r.first[...] = grad_first
    r.self_branch[...] = grad_first.astype(bf16)
    swap.send("gsb", half(r.self_branch, o, width // 2), r.by_self_branch)
    r.mixed_grad[...] = input_grad(r.self_branch, 2, width // 2).astype(bf16)
    red.free(2)
    for q in g.chunks_of(2):
        g.settle(q)
    swap.wait("gcb")
    swap.wait("cm")
    plain_grad(4, r.cm, r.by_cm, r.branch, r.by_branch, width // 2)
    for s in range(slots):
        j = 0
        for k in range(slots):
            j = jnp.where(lax.rem(r.index[k // 2, k % 2], slots) == s, k, j)
        b, odd = lax.div(j, 2), lax.rem(j, 2)
        r.pool[s] = jnp.where(odd == 0, r.gkv[b, :rows_n], r.gkv[b, rows_n:])
    swap.send("gp", r.pool.at[:, :, pl.ds(pl.multiple_of(o * pool_half, LANES), pool_half)], r.by_pool_grad)

    cosine, signed = r.rope[0, :, :LANES], r.rope[0, :, LANES:]
    place = lax.broadcasted_iota(jnp.int32, (1, quarter), 1) + p.s * quarter
    limit = jnp.maximum(place, r.prefix[0] - 1)
    group, groups = width, 2
    each = pairs // groups

    def self_pair(i, carry):
        cols = pl.ds(pl.multiple_of(i * LANES, LANES), LANES)
        vcols = pl.ds(pl.multiple_of(i * LANES + pool_half, LANES), LANES)
        start = lax.div(i, each) * group + lax.rem(i, each) * LANES
        keys = r.kv[:, :, cols].reshape(-1, LANES)
        values = r.kv[:, :, vcols].reshape(-1, LANES)
        key_grad = value_grad = 0.0
        query_grads = []
        for e, lanes in enumerate((low, high)):
            queries = r.q[:, cols] * (lanes * bf16(HEAD**-0.5))
            grads = r.mixed_grad[:, cols] * lanes
            scores = dot(keys, queries, NT)
            key_place = lax.broadcasted_iota(jnp.int32, scores.shape, 0)
            logsum = r.lse[i, :, e * quarter : (e + 1) * quarter]
            probs = jnp.exp(jnp.where(key_place <= limit, scores, masked) - logsum)
            grad_probs = dot(values, grads, NT)
            score_grad = (probs * (grad_probs - jnp.sum(probs * grad_probs, 0, keepdims=True))).astype(bf16)
            key_grad = key_grad + dot(score_grad, queries)
            value_grad = value_grad + dot(probs.astype(bf16), grads)
            query_grads.append(dot(score_grad, keys, TN))
        for offset, part in ((0, key_grad), (group // 2, value_grad)):
            there = pl.ds(pl.multiple_of(start + offset, LANES), LANES)
            r.gkv[:, :, there] = part.astype(bf16).reshape(4, quarter, LANES)
        query_grad = jnp.where(low_lane, *query_grads) * HEAD**-0.5
        r.q[:, cols] = rotate(query_grad, cosine, -signed).astype(bf16)
        return carry

    for i in range(groups):
        for j in range(each):
            lax.fori_loop(i * each + j, i * each + j + 1, self_pair, 0)
            red.push()
        cols = pl.ds(i * group, group)
        swap.send(f"far{i}", r.gkv.at[p.s_d, :, cols], r.by_act.at[:, cols])
        swap.send(f"near{i}", r.gkv.at[p.s_c, :, cols], r.by_act.at[:, pl.ds((groups + i) * group, group)])
    red.phase = 1
    swap.send("gq", half(r.q, o, width // 2), r.by_q_grad)
    swap.wait("gcq")
    swap.wait("n2")
    plain_grad(3, r.n2, r.by_n2, r.cq_grad, r.by_cq_grad, width // 2)
    for i in range(groups):
        cols = slice(i * group, (i + 1) * group)
        for j, (name, s, other) in enumerate((("near", p.s, groups + i), ("far", p.s_y, i))):
            swap.wait(f"{name}{i}")
            total = r.gkv[s, :, cols].astype(f32) + r.by_act[:, other * group : (other + 1) * group].astype(f32)
            total = jnp.concatenate([turned(total[:, : group // 2], j, -1), total[:, group // 2 :]], 1)
            r.gkv[s, :, cols] = total.astype(bf16)
    half_kv = pl.ds(pl.multiple_of(o * group, LANES), group)
    for j, (name, s) in enumerate((("gkv", p.s), ("gkvy", p.s_y))):
        swap.send(name, r.gkv.at[s, :, half_kv], r.by_hidden_grad.at[:, pl.ds(j * group, group)])
    red.push()
    part = width // 2

    def kv_grads(cols):
        return jnp.concatenate([r.gkv[s, :, cols] for s in (p.s, p.s_y)], 0)

    grad_one = sum(dot(kv_grads(slice(h * group, (h + 1) * group)), half_of(w[0], h, part, group), NT) for h in range(2))
    r.mixed_grad[...] = grad_one[quarter:].astype(bf16)
    to_y = remote(r.mixed_grad, r.one_y, kv_sem.at[0], kv_sem.at[1], p.to_y)
    to_y.start()
    r.second[...] = grad_one[:quarter] + sum(
        dot(r.q[:, h * part : (h + 1) * part], half_of(w[0], h, 0, part), NT) for h in range(2)
    )
    red.free(0)
    for q in g.chunks_of(0):
        g.settle(q)
    for name in ("gq", "n1", "gkv", "gkvy"):
        swap.wait(name)
    first_chunk, *kv_chunks, vec_chunk = red.chunks_of(0)
    plain_grad(0, r.n1.at[:quarter], r.by_n1.at[:quarter], r.q, r.by_q_grad, part, chunks=[first_chunk])
    weight_grad(
        0,
        lambda cols: r.n1[:, cols],
        lambda cols: r.by_n1[:, cols],
        lambda start, n: kv_grads(pl.ds(pl.multiple_of(c * group + start - part, LANES), n)),
        lambda start, n: jnp.concatenate(
            [r.by_hidden_grad[:, j * group + start - part : j * group + start - part + n] for j in range(2)], 0
        ),
        3 * part,
        chunks=kv_chunks,
    )
    swap.wait("gsb")
    swap.wait("att")
    plain_grad(2, r.att, r.by_att, r.self_branch, r.by_self_branch, width // 2)

    out = [None, None]
    for s in range(slots):
        rows = r.pool[s]
        slot_grad = sum(
            dot(rows[:, h * pool_half : (h + 1) * pool_half], half_of(w[1], h), NT) for h in range(2)
        )
        if out[s % 2] is not None:
            out[s % 2].wait()
        stage = r.tokens_grad.at[(s % 2) * rows_n : (s % 2 + 1) * rows_n]
        stage[...] = slot_grad
        out[s % 2] = pltpu.make_async_copy(stage, r.neighbours_grad.at[s], r.out_sem.at[s % 2])
        out[s % 2].start()
        if s == slots // 2:
            red.push()
    red.phase = 2
    red.free(1)
    for q in g.chunks_of(1):
        g.settle(q)
    swap.wait("gp")
    swap.wait("nb")
    size = slots * rows_n
    weight_grad(
        1,
        lambda cols: r.neighbours[:, :, cols].reshape(size, -1),
        lambda cols: r.by_neighbours[:, :, cols].reshape(size, -1),
        lambda start, n: r.pool[:, :, pl.ds(pl.multiple_of(c * pool_half + start, LANES), n)].reshape(size, -1),
        lambda start, n: r.by_pool_grad[:, :, start : start + n].reshape(size, -1),
        pool_half,
    )
    to_y.wait_recv()
    grad_one = r.second[...] + r.one_y[...].astype(f32)
    back, dg, db = norm_back_at(grad_one, r.tokens[...].astype(f32), gain(0))
    keep_vec(0, dg, db)
    for cp in out:
        cp.wait()
    r.tokens_grad[...] = r.first[...] + back
    swap.send("vec", r.vec_sum, r.by_vec)
    swap.wait("vec")
    vec = jnp.concatenate([r.vec_sum[...] + r.by_vec[...], jnp.zeros((LANES - 8, width), f32)], 0)
    w[0][c, :, :, :, 3 * part :] = jnp.transpose(vec).astype(bf16).reshape(p.nz, 4, -1, LANES)
    red.push(vec_chunk)
    red.drain()
    for cp in (*red.sent, *swap.sent, to_y):
        cp.wait_send()


def rope_table(length):
    half = HEAD // 2
    freq = (10000.0 ** (-np.arange(half, dtype=np.float32) / half)).astype(np.float32)
    angles = np.arange(length, dtype=np.float32)[:, None] * freq[None, :]
    cosine, sine = np.cos(angles), np.sin(angles)
    table = np.concatenate([cosine] * 4 + [-sine, sine] * 2, 1)
    return table.astype(np.float32).reshape(4, -1, 2 * LANES)


def deliver_kernel(*refs):
    n = 10
    sources, outs, held = refs[:n], refs[n : 2 * n + 1], refs[2 * n + 1 : 3 * n + 1]
    arrive, leave = refs[3 * n + 1 :]
    taken = [pltpu.make_async_copy(sources[i], held[i], arrive.at[i]) for i in range(n)]
    for cp in taken:
        cp.start()
    left = []

    def put(src, dst):
        left.append(pltpu.make_async_copy(src, dst, leave.at[len(left)]))
        left[-1].start()

    for i in range(n):
        taken[i].wait()
        if i < 3:
            put(held[i], outs[i])
            continue
        parts = 3 if i == 3 else 1
        part = outs[i].shape[1] // (2 * parts)
        for h in range(2):
            for j in range(parts):
                put(held[i].at[h, :, j * part : (j + 1) * part], outs[i].at[:, (2 * j + h) * part : (2 * j + h + 1) * part])
        if i == 3:
            rows = held[i].shape[1]
            vectors = jnp.concatenate([held[i][0, :, parts * part :], jnp.zeros((LANES - rows, LANES), f32)], 0)
            outs[n][...] = jnp.transpose(vectors)[:8, :rows]
    for cp in left:
        cp.wait()


def deliver(out, tokens_grad, neighbours_grad, summed):
    rows = summed[0].shape[1]
    widths = [2 * v.shape[2] for v in summed]
    widths[0] -= 2 * LANES
    shapes = [out, tokens_grad, neighbours_grad] + [
        jax.ShapeDtypeStruct((v.shape[1], n), f32) for v, n in zip(summed, widths)
    ]
    vmem, hbm = pl.BlockSpec(memory_space=pltpu.VMEM), pl.BlockSpec(memory_space=pltpu.HBM)
    sources = (out, tokens_grad, neighbours_grad, *summed)
    out, tokens_grad, neighbours_grad, *grads, vectors = pl.pallas_call(
        deliver_kernel,
        out_shape=[jax.ShapeDtypeStruct(v.shape, v.dtype) for v in shapes] + [jax.ShapeDtypeStruct((8, rows), f32)],
        in_specs=[hbm] * 10,
        out_specs=[hbm] * 10 + [vmem],
        scratch_shapes=[pltpu.VMEM(v.shape, v.dtype) for v in sources]
        + [pltpu.SemaphoreType.DMA((10,)), pltpu.SemaphoreType.DMA((21,))],
        compiler_params=pltpu.CompilerParams(vmem_limit_bytes=64 * 2**20 - 2**17),
        name="deliver",
    )(*sources)
    return (
        out[None],
        tokens_grad[None],
        neighbours_grad[None],
        grads[0],
        grads[2],
        grads[3],
        grads[1],
        grads[4],
        grads[5],
        grads[6],
        *(vectors[i] for i in (0, 3, 1, 4, 2, 5)),
    )


class Refs:
    def take(self, names, refs):
        for name, ref in zip(names, refs, strict=True):
            setattr(self, name, ref)


NAMES_IN = (
    "w_qkv",
    "w_cross_kv",
    "w_out",
    "w_cross_q",
    "w_cross_out",
    "w_up",
    "w_down",
    "vectors",
    "tokens",
    "cotangent",
    "prefix",
    "neighbours",
    "index",
    "rope_table",
)
NAMES_OUT = ("out", "tokens_grad", "neighbours_grad")
GATHER = (
    (0, 768, 512, 2),
    (0, 384, 384, 2),
    (0, 0, 384, 2),
    (1, 0, 384, 2),
    (1, 384, 384, 2),
    (2, 0, 384, 2),
    (3, 0, 384, 2),
    (4, 0, 384, 2),
    (5, 0, 384, 2),
    (5, 384, 384, 2),
    (5, 768, 384, 2),
    (5, 1152, 384, 2),
    (6, 0, 128, 2),
    (6, 128, 128, 2),
    (6, 256, 128, 2),
)
REDUCE = (
    (6, 0, 128, 2),
    (6, 128, 128, 2),
    (6, 256, 128, 2),
    (5, 0, 384, 2),
    (5, 384, 384, 2),
    (5, 768, 384, 2),
    (5, 1152, 384, 2),
    (4, 0, 384, 2),
    (3, 0, 384, 2),
    (2, 0, 384, 2),
    (1, 0, 384, 2),
    (1, 384, 384, 2),
    (0, 0, 384, 2),
    (0, 384, 384, 2),
    (0, 768, 384, 2),
    (0, 1152, 128, 2),
)


def memory(nz, quarter, width, hidden, slots, rows_n, rows):
    halves = (3 * width // 2 + LANES, width, width // 2, width // 2, width // 2, hidden // 2)
    weights = [((2, nz, 4, 2 * rows, h), bf16) for h in halves]
    weights.append(((2, nz, 4, hidden // (4 * nz), width // 2), bf16))
    sums = [((2, rows, h), f32) for h in halves]
    sums.append(((2, hidden // (8 * nz), width // 2), f32))
    tok, half_tok = ((quarter, width), bf16), ((quarter, width // 2), bf16)
    half_hidden = ((quarter, hidden // 2), bf16)
    pool_half = ((slots, rows_n, width), bf16)
    kv = ((quarter, 2 * width), bf16)
    arrays = dict(
        pack=((2, rows, sum(halves)), f32),
        beside=((rows, sum(halves)), f32),
        down_sum=weights[6],
        down_beside=((hidden // (8 * nz), width // 2), f32),
        rope=((2, quarter, 2 * LANES), f32),
        n1=((2 * quarter, width), bf16),
        q=tok,
        kv=((4, *kv[0]), bf16),
        att=tok,
        lse=((width // LANES, 1, 2 * quarter), f32),
        first=((quarter, width), f32),
        n2=tok,
        cq=tok,
        pool=((slots, rows_n, 2 * width), bf16),
        lse_cross=((width // LANES, 8, LANES), f32),
        cm=tok,
        second=((quarter, width), f32),
        n3=tok,
        act=((quarter, hidden), bf16),
        slope=((quarter, hidden), bf16),
        vec=((8, width), f32),
        branch=tok,
        mixed_grad=tok,
        cq_grad=tok,
        self_branch=tok,
        one_y=tok,
        gkv=((4, *kv[0]), bf16),
        vec_sum=((8, width), f32),
        by_act=((quarter, hidden), bf16),
        by_cot=half_tok,
        by_n3=tok,
        by_hidden_grad=half_hidden,
        by_cm=tok,
        by_branch=half_tok,
        by_neighbours=pool_half,
        by_pool_grad=pool_half,
        by_n2=tok,
        by_cq_grad=half_tok,
        by_att=tok,
        by_self_branch=half_tok,
        by_n1=((2 * quarter, width), bf16),
        by_q_grad=half_tok,
        by_vec=((8, width), f32),
    )
    return weights, arrays, sums


def layer_kernel(nz, names, *refs):
    refs = list(refs)
    r = Refs()

    def some(n):
        taken = refs[:n]
        del refs[:n]
        return taken

    r.take(NAMES_IN, some(len(NAMES_IN)))
    r.take(NAMES_OUT, some(len(NAMES_OUT)))
    r.sums, r.w = some(7), some(7)
    r.take(names, some(len(names)))
    r.pair_sem, r.rope_sem, r.out_sem, fkv_sem, kv_sem, swap_sem, g_send, g_recv, r_send, r_recv, r.credit = refs
    p = Place(nz)
    g = Gather(p, r.w, GATHER, g_send, g_recv)
    swap = Swap(p, swap_sem)
    pairs = r.tokens.shape[1] // LANES
    down_part, turned, sent = forward(p, r, g, swap, fkv_sem, pairs)
    red = Reduce(p, r, REDUCE, r_send, r_recv)
    backward(p, r, g, swap, red, kv_sem, pairs, down_part, turned)
    for cp in sent:
        cp.wait_send()


def local_fast(
    tokens,
    prefix_len,
    neighbours,
    neighbour_index,
    w_qkv,
    w_out,
    w_cross_q,
    w_cross_kv,
    w_cross_out,
    w_up,
    w_down,
    gain_one,
    shift_one,
    gain_two,
    shift_two,
    gain_three,
    shift_three,
    cotangent,
):
    nz = lax.axis_size("dp") // 2
    quarter, width = tokens.shape[1:]
    rows, hidden = w_up.shape
    slots, rows_n = neighbours.shape[1:3]
    vectors = jnp.stack([gain_one, gain_two, gain_three, shift_one, shift_two, shift_three])
    weights, arrays, sums = memory(nz, quarter, width, hidden, slots, rows_n, rows)
    vmem, smem, anywhere = (pl.BlockSpec(memory_space=m) for m in (pltpu.VMEM, pltpu.SMEM, pl.ANY))
    made = [((quarter, width), bf16), ((quarter, width), f32), ((slots, rows_n, width), f32), *sums]
    dma = pltpu.SemaphoreType.DMA
    out, tokens_grad, neighbours_grad, *summed = pl.pallas_call(
        functools.partial(layer_kernel, nz, tuple(arrays)),
        out_shape=[jax.ShapeDtypeStruct(*v) for v in made],
        in_specs=[vmem] * 10 + [smem, vmem, smem, anywhere],
        out_specs=[vmem, vmem, anywhere] + [vmem] * len(sums),
        scratch_shapes=[pltpu.VMEM(*v) for v in (*weights, *arrays.values())]
        + [
            dma((6,)),
            dma((2,)),
            dma((2,)),
            dma((2, 2)),
            dma((2,)),
            dma((2, 28)),
            dma((len(GATHER), 14)),
            dma((len(GATHER), 14)),
            dma((len(REDUCE), 8)),
            dma((len(REDUCE), 8)),
            pltpu.SemaphoreType.REGULAR((7,)),
        ],
        compiler_params=pltpu.CompilerParams(
            collective_id=0, has_side_effects=True, vmem_limit_bytes=64 * 2**20 - 2**17
        ),
    )(
        w_qkv, w_cross_kv, w_out, w_cross_q, w_cross_out, w_up, w_down, vectors,
        tokens[0], cotangent[0], prefix_len, neighbours[0],
        neighbour_index[0], jnp.asarray(rope_table(4 * quarter)),
    )
    return deliver(out, tokens_grad, neighbours_grad, summed)


def pick_slots(pool, index):
    return jnp.stack(
        [
            jnp.concatenate([lax.dynamic_slice_in_dim(pool[s], index[s, j], 1, 0) for j in range(index.shape[1])], 0)
            for s in range(index.shape[0])
        ]
    )


def slot_places(index):
    slots = index.shape[1]
    same = index[:, :, None] == jnp.arange(slots)[None, None, :]
    return jnp.sum(jnp.where(same, jnp.arange(slots)[None, :, None], 0), 1)


def dense_dot(left_side, weight):
    return jnp.dot(left_side, weight, preferred_element_type=jnp.float32)


def input_grad(grad_out, weight):
    return lax.dot_general(
        grad_out,
        weight,
        (((grad_out.ndim - 1,), (1,)), ((), ())),
        preferred_element_type=jnp.float32,
    )


def weight_grad(left_side, grad_out):
    flat_left = left_side.reshape(-1, left_side.shape[-1])
    flat_grad = grad_out.reshape(-1, grad_out.shape[-1])
    return lax.dot_general(
        flat_left, flat_grad, (((0,), (0,)), ((), ())), preferred_element_type=jnp.float32
    )


def plain_norm_parts(array_in):
    avg_value = jnp.mean(array_in, -1, keepdims=True)
    centred = array_in - avg_value
    inv_std = lax.rsqrt(jnp.mean(centred * centred, -1, keepdims=True) + eps)
    return (centred * inv_std, inv_std)


def norm_back(grad_out, unit_part, inv_std, gain_f):
    scaled = grad_out * gain_f
    grad_in = inv_std * (
        scaled
        - jnp.mean(scaled, -1, keepdims=True)
        - unit_part * jnp.mean(scaled * unit_part, -1, keepdims=True)
    )
    return (grad_in, jnp.sum(grad_out * unit_part, (0, 1)), jnp.sum(grad_out, (0, 1)))


def rotary_tables(positions):
    half_size = HEAD // 2
    frequency = 10000.0 ** (-jnp.arange(half_size).astype(jnp.float32) / half_size)
    angles = positions.astype(jnp.float32)[:, None] * frequency[None, :]
    return (jnp.cos(angles)[:, None, :], jnp.sin(angles)[:, None, :])


def plain_rotate(array_in, cosine, sine_part):
    half_size = HEAD // 2
    first_half = array_in[..., :half_size]
    second = array_in[..., half_size:]
    return jnp.concatenate(
        [first_half * cosine - second * sine_part, second * cosine + first_half * sine_part], -1
    )


def unrotate(grad_in, cosine, sine_part):
    half_size = HEAD // 2
    first_half = grad_in[..., :half_size]
    second = grad_in[..., half_size:]
    return jnp.concatenate(
        [first_half * cosine + second * sine_part, second * cosine - first_half * sine_part], -1
    )


def grouped(array_in):
    split_heads = array_in.reshape(
        array_in.shape[0], array_in.shape[1], array_in.shape[2] // 4, 4, array_in.shape[3]
    )
    return jnp.moveaxis(split_heads, 2, 0)


def ungrouped(array_in):
    shifted_axes = jnp.moveaxis(array_in, 0, 2)
    return shifted_axes.reshape(
        shifted_axes.shape[0], shifted_axes.shape[1], -1, shifted_axes.shape[-1]
    )


def masked_scores(visible, queries, key_rows):
    scores = jnp.einsum(
        "sqhd,skhd->shqk", queries, key_rows, preferred_element_type=jnp.float32
    ) * HEAD ** (-0.5)
    return jnp.where(visible[:, None], scores, masked)


def attend_group(visible, packed):
    queries, key_rows, values = packed
    scores = masked_scores(visible, queries, key_rows)
    row_max = jnp.max(scores, -1, keepdims=True)
    exp_scores = jnp.exp(scores - row_max)
    row_total = jnp.sum(exp_scores, -1, keepdims=True)
    probabilities = (exp_scores / row_total).astype(jnp.bfloat16)
    mixed_out = jnp.einsum(
        "shqk,skhd->sqhd", probabilities, values, preferred_element_type=jnp.float32
    )
    return (mixed_out, (row_max + jnp.log(row_total))[..., 0])


def attend_back(visible, packed):
    queries, key_rows, values, grad_out, logsum = packed
    scores = masked_scores(visible, queries, key_rows)
    probabilities = jnp.exp(scores - logsum[..., None])
    grad_probs = jnp.einsum("sqhd,skhd->shqk", grad_out, values, preferred_element_type=jnp.float32)
    grad_scores = (
        probabilities * (grad_probs - jnp.sum(probabilities * grad_probs, -1, keepdims=True))
    ).astype(jnp.bfloat16)
    grad_query = jnp.einsum(
        "shqk,skhd->sqhd", grad_scores, key_rows, preferred_element_type=jnp.float32
    ) * HEAD ** (-0.5)
    grad_key = jnp.einsum(
        "shqk,sqhd->skhd", grad_scores, queries, preferred_element_type=jnp.float32
    ) * HEAD ** (-0.5)
    grad_value = jnp.einsum(
        "shqk,sqhd->skhd",
        probabilities.astype(jnp.bfloat16),
        grad_out,
        preferred_element_type=jnp.float32,
    )
    return (grad_query, grad_key, grad_value)


def local_plain(
    tokens,
    prefix_len,
    neighbours,
    neighbour_index,
    w_qkv,
    w_out,
    w_cross_q,
    w_cross_kv,
    w_cross_out,
    w_up,
    w_down,
    gain_one,
    shift_one,
    gain_two,
    shift_two,
    gain_three,
    shift_three,
    cotangent,
):
    forward_set = (
        lax.all_gather(w_qkv, ("dp", "seq"), axis=0, tiled=True),
        lax.all_gather(w_out, ("dp", "seq"), axis=0, tiled=True),
        lax.all_gather(w_cross_q, ("dp", "seq"), axis=0, tiled=True),
        lax.all_gather(w_cross_kv, ("dp", "seq"), axis=0, tiled=True),
        lax.all_gather(w_cross_out, ("dp", "seq"), axis=0, tiled=True),
        lax.all_gather(w_up, ("dp", "seq"), axis=0, tiled=True),
        lax.all_gather(w_down, ("dp", "seq"), axis=0, tiled=True),
        lax.all_gather(gain_one, ("dp", "seq"), axis=0, tiled=True),
        lax.all_gather(shift_one, ("dp", "seq"), axis=0, tiled=True),
        lax.all_gather(gain_two, ("dp", "seq"), axis=0, tiled=True),
        lax.all_gather(shift_two, ("dp", "seq"), axis=0, tiled=True),
        lax.all_gather(gain_three, ("dp", "seq"), axis=0, tiled=True),
        lax.all_gather(shift_three, ("dp", "seq"), axis=0, tiled=True),
    )
    (
        full_qkv,
        full_out,
        full_cross_q,
        full_cross_kv,
        full_cross_out,
        full_up,
        full_down,
        full_gain_one,
        full_shift_one,
        full_gain_two,
        full_shift_two,
        full_gain_three,
        full_shift_three,
    ) = forward_set
    seq_here, quarter, width = tokens.shape
    heads = width // HEAD
    hidden_width = full_up.shape[1]
    length = quarter * lax.axis_size("seq")
    seq_index = lax.axis_index("seq")
    query_pos = seq_index * quarter + jnp.arange(quarter)
    key_pos = jnp.arange(length)
    visible = (key_pos[None, None, :] <= query_pos[None, :, None]) | (
        key_pos[None, None, :] < prefix_len[:, None, None]
    )
    cosine, sine_part = rotary_tables(query_pos)
    gain_f1 = full_gain_one.astype(jnp.float32)
    gain_f2 = full_gain_two.astype(jnp.float32)
    gain_f3 = full_gain_three.astype(jnp.float32)
    resid_in = tokens.astype(jnp.float32)
    unit_one, inv_one = plain_norm_parts(resid_in)
    normed_one = (unit_one * gain_f1 + full_shift_one.astype(jnp.float32)).astype(jnp.bfloat16)
    joined = dense_dot(normed_one, full_qkv)
    query_rot = plain_rotate(
        joined[..., :width].reshape(seq_here, quarter, heads, HEAD), cosine, sine_part
    ).astype(jnp.bfloat16)
    key_local = (
        plain_rotate(
            joined[..., width : 2 * width].reshape(seq_here, quarter, heads, HEAD),
            cosine,
            sine_part,
        )
        .astype(jnp.bfloat16)
        .reshape(seq_here, quarter, width)
    )
    value_local = joined[..., 2 * width :].astype(jnp.bfloat16)
    key_all, value_all = (
        lax.all_gather(key_local, "seq", axis=1, tiled=True),
        lax.all_gather(value_local, "seq", axis=1, tiled=True),
    )
    key_heads = key_all.reshape(seq_here, length, heads, HEAD)
    value_heads = value_all.reshape(seq_here, length, heads, HEAD)
    attended, logsum = lax.map(
        functools.partial(attend_group, visible),
        (grouped(query_rot), grouped(key_heads), grouped(value_heads)),
    )
    attended = ungrouped(attended).reshape(seq_here, quarter, width).astype(jnp.bfloat16)
    first_sum = resid_in + dense_dot(attended, full_out)
    unit_two, inv_two = plain_norm_parts(first_sum)
    normed_two = (unit_two * gain_f2 + full_shift_two.astype(jnp.float32)).astype(jnp.bfloat16)
    cross_query = dense_dot(normed_two, full_cross_q).astype(jnp.bfloat16)
    pool_kv = dense_dot(neighbours, full_cross_kv).astype(jnp.bfloat16)
    slots = neighbours.shape[1]
    spans = slots // 2
    span_len = quarter // spans
    neighbour_rows = 2 * neighbours.shape[2]
    local_index = neighbour_index.reshape(seq_here, slots) - seq_index * slots
    picked = pick_slots(pool_kv, local_index)
    picked = picked.reshape(seq_here, spans, neighbour_rows, 2 * width)
    cross_keys = picked[..., :width].reshape(seq_here, spans, neighbour_rows, heads, HEAD)
    cross_values = picked[..., width:].reshape(seq_here, spans, neighbour_rows, heads, HEAD)
    cross_queries = cross_query.reshape(seq_here, spans, span_len, heads, HEAD)
    cross_scores = jnp.einsum(
        "scqhd,sckhd->schqk", cross_queries, cross_keys, preferred_element_type=jnp.float32
    ) * HEAD ** (-0.5)
    cross_probs = jax.nn.softmax(cross_scores, -1)
    cross_weights = cross_probs.astype(jnp.bfloat16)
    cross_mixed = jnp.einsum(
        "schqk,sckhd->scqhd", cross_weights, cross_values, preferred_element_type=jnp.float32
    )
    cross_mixed = cross_mixed.reshape(seq_here, quarter, width).astype(jnp.bfloat16)
    second_sum = first_sum + dense_dot(cross_mixed, full_cross_out)
    unit_three, inv_three = plain_norm_parts(second_sum)
    normed_three = (unit_three * gain_f3 + full_shift_three.astype(jnp.float32)).astype(
        jnp.bfloat16
    )
    hidden_pre = dense_dot(normed_three, full_up)
    activated = jax.nn.gelu(hidden_pre, approximate=False).astype(jnp.bfloat16)
    output = (second_sum + dense_dot(activated, full_down)).astype(jnp.bfloat16)
    grad_act = input_grad(cotangent, full_down)
    _, gelu_back = jax.vjp(functools.partial(jax.nn.gelu, approximate=False), hidden_pre)
    grad_hidden = gelu_back(grad_act)[0].astype(jnp.bfloat16)
    grad_normed_three = input_grad(grad_hidden, full_up)
    back_three, grad_gain_three, grad_shift_three = norm_back(
        grad_normed_three, unit_three, inv_three, full_gain_three.astype(jnp.float32)
    )
    grad_second = cotangent.astype(jnp.float32) + back_three
    grad_cross_branch = grad_second.astype(jnp.bfloat16)
    grad_mixed = (
        input_grad(grad_cross_branch, full_cross_out)
        .astype(jnp.bfloat16)
        .reshape(seq_here, spans, span_len, heads, HEAD)
    )
    grad_cross_probs = jnp.einsum(
        "scqhd,sckhd->schqk", grad_mixed, cross_values, preferred_element_type=jnp.float32
    )
    grad_cross_scores = (
        cross_probs
        * (grad_cross_probs - jnp.sum(cross_probs * grad_cross_probs, -1, keepdims=True))
    ).astype(jnp.bfloat16)
    grad_cross_query = (
        (
            jnp.einsum(
                "schqk,sckhd->scqhd",
                grad_cross_scores,
                cross_keys,
                preferred_element_type=jnp.float32,
            )
            * HEAD ** (-0.5)
        )
        .astype(jnp.bfloat16)
        .reshape(seq_here, quarter, width)
    )
    grad_cross_keys = jnp.einsum(
        "schqk,scqhd->sckhd", grad_cross_scores, cross_queries, preferred_element_type=jnp.float32
    ) * HEAD ** (-0.5)
    grad_cross_values = jnp.einsum(
        "schqk,scqhd->sckhd", cross_weights, grad_mixed, preferred_element_type=jnp.float32
    )
    grad_picked = jnp.concatenate(
        [
            grad_cross_keys.reshape(seq_here, spans, neighbour_rows, width),
            grad_cross_values.reshape(seq_here, spans, neighbour_rows, width),
        ],
        -1,
    )
    grad_picked = grad_picked.reshape(seq_here, slots, neighbours.shape[2], 2 * width)
    grad_pool_kv = pick_slots(grad_picked.astype(jnp.bfloat16), slot_places(local_index))
    grad_neighbours = input_grad(grad_pool_kv, full_cross_kv)
    grad_normed_two = input_grad(grad_cross_query, full_cross_q)
    back_two, grad_gain_two, grad_shift_two = norm_back(
        grad_normed_two, unit_two, inv_two, full_gain_two.astype(jnp.float32)
    )
    grad_first = grad_second + back_two
    grad_self_branch = grad_first.astype(jnp.bfloat16)
    grad_attended = (
        input_grad(grad_self_branch, full_out)
        .astype(jnp.bfloat16)
        .reshape(seq_here, quarter, heads, HEAD)
    )
    grad_query, grad_key_all, grad_value_all = lax.map(
        functools.partial(attend_back, visible),
        (
            grouped(query_rot),
            grouped(key_heads),
            grouped(value_heads),
            grouped(grad_attended),
            logsum,
        ),
    )
    grad_query = ungrouped(grad_query)
    grad_key_all = ungrouped(grad_key_all).reshape(seq_here, length, width)
    grad_value_all = ungrouped(grad_value_all).reshape(seq_here, length, width)
    grad_key, grad_value = (
        lax.psum_scatter(
            grad_key_all.astype(jnp.bfloat16), "seq", scatter_dimension=1, tiled=True
        ).astype(jnp.float32),
        lax.psum_scatter(
            grad_value_all.astype(jnp.bfloat16), "seq", scatter_dimension=1, tiled=True
        ).astype(jnp.float32),
    )
    grad_joined = jnp.concatenate(
        [
            unrotate(grad_query, cosine, sine_part).reshape(seq_here, quarter, width),
            unrotate(grad_key.reshape(seq_here, quarter, heads, HEAD), cosine, sine_part).reshape(
                seq_here, quarter, width
            ),
            grad_value,
        ],
        -1,
    ).astype(jnp.bfloat16)
    grad_normed_one = input_grad(grad_joined, full_qkv)
    back_one, grad_gain_one, grad_shift_one = norm_back(
        grad_normed_one, unit_one, inv_one, full_gain_one.astype(jnp.float32)
    )
    grad_tokens = grad_first + back_one
    norm_grads = jnp.stack(
        [
            grad_gain_one,
            grad_shift_one,
            grad_gain_two,
            grad_shift_two,
            grad_gain_three,
            grad_shift_three,
        ],
        1,
    )
    width_owned = lax.psum_scatter(
        jnp.concatenate(
            [
                weight_grad(normed_one, grad_joined),
                weight_grad(attended, grad_self_branch),
                weight_grad(normed_two, grad_cross_query),
                weight_grad(neighbours, grad_pool_kv),
                weight_grad(cross_mixed, grad_cross_branch),
                weight_grad(normed_three, grad_hidden),
                norm_grads,
            ],
            1,
        ),
        ("dp", "seq"),
        scatter_dimension=0,
        tiled=True,
    )
    down_owned = lax.psum_scatter(
        weight_grad(activated, cotangent), ("dp", "seq"), scatter_dimension=0, tiled=True
    )
    column = 8 * width + hidden_width
    return (
        output,
        grad_tokens,
        grad_neighbours,
        width_owned[:, : 3 * width],
        width_owned[:, 3 * width : 4 * width],
        width_owned[:, 4 * width : 5 * width],
        width_owned[:, 5 * width : 7 * width],
        width_owned[:, 7 * width : 8 * width],
        width_owned[:, 8 * width : column],
        down_owned,
        width_owned[:, column],
        width_owned[:, column + 1],
        width_owned[:, column + 2],
        width_owned[:, column + 3],
        width_owned[:, column + 4],
        width_owned[:, column + 5],
    )


def solution(mesh):
    sizes = dict(mesh.shape)
    fits = sizes == {"dp": 8, "seq": 4}
    return jax.shard_map(
        local_fast if fits else local_plain,
        mesh=mesh,
        in_specs=(
            P("dp", "seq", None),
            P("dp"),
            P("dp", "seq", None, None),
            P("dp", "seq", None),
            P(("dp", "seq"), None),
            P(("dp", "seq"), None),
            P(("dp", "seq"), None),
            P(("dp", "seq"), None),
            P(("dp", "seq"), None),
            P(("dp", "seq"), None),
            P(("dp", "seq"), None),
            P(("dp", "seq")),
            P(("dp", "seq")),
            P(("dp", "seq")),
            P(("dp", "seq")),
            P(("dp", "seq")),
            P(("dp", "seq")),
            P("dp", "seq", None),
        ),
        out_specs=(
            P("dp", "seq", None),
            P("dp", "seq", None),
            P("dp", "seq", None, None),
            P(("dp", "seq"), None),
            P(("dp", "seq"), None),
            P(("dp", "seq"), None),
            P(("dp", "seq"), None),
            P(("dp", "seq"), None),
            P(("dp", "seq"), None),
            P(("dp", "seq"), None),
            P(("dp", "seq")),
            P(("dp", "seq")),
            P(("dp", "seq")),
            P(("dp", "seq")),
            P(("dp", "seq")),
            P(("dp", "seq")),
        ),
        check_vma=False,
    )
```
